512 devices in a mesh: seq: 64 (over z, y_lo, core), head: 8 (over y_hi, x).
Axes of the slice: x: 4, y: 4 (y_hi: 2, y_lo: 2; y = y_hi * 2 + y_lo), z: 16, core: 2. Of those that a mesh axis runs over, the one named last changes fastest.
Arguments:
- query_states: bfloat16 [8192, 3072], P(('seq', 'head')), may hold values from -48 to 48
- key_states: bfloat16 [8192, 3072], P(('seq', 'head')), may hold values from -9 to 9
- value_states: bfloat16 [8192, 3072], P(('seq', 'head')), may hold values from -6 to 6
- base_patch: bfloat16 [8192, 64], P(('seq', 'head')), may hold values from -4 to 4
- head_proj: bfloat16 [3072, 64], P('head'), may hold values from -0.4375 to 0.4375
- latent_std: float32 [16], replicated, may hold values from 0.5 to 2
- latent_mean: float32 [16], replicated, may hold values from -1 to 1
- w_in: bfloat16 [3, 3, 3, 16, 384], replicated, may hold values from -0.3125 to 0.3125
- b_in: float32 [384], replicated, may hold values from -0.5 to 0.5
- gain_mid: float32 [384], replicated, may hold values from 0.25 to 1.75
- w_up: bfloat16 [3, 3, 384, 192], replicated, may hold values from -0.109375 to 0.109375
- b_up: float32 [192], replicated, may hold values from -0.5 to 0.5
Outputs:
- video_features: bfloat16 [16, 256, 32, 192], P('head', 'seq')
The draws below stay inside these ranges and needn't reach their ends.
All inputs are finite; a program needn't handle non-finite values.
Results may differ from the reference program's by a relative error of at most 0.017.
Values may be sent and summed in bfloat16 or wider, within the bound.
A program may use at most 64 MiB of HBM per device.

```python
import math
import jax
import jax.numpy as jnp
from jax import lax

HEADS = 24
HD = 128
LATENT_CH = 16
CH = 384
OUTCH = 192
WP = 8
PATCH = 64
HP = 64
FRAMES = 16
TOKENS = 8192
LH = 128
LW = 16


def common_draws(key):
    normal_part = jax.random.normal(jax.random.fold_in(key, 7), (TOKENS, HEADS * HD), jnp.float32)
    return normal_part


def draw_key_states(key, part):
    normal_part = common_draws(key)
    return (1.4 * jnp.clip(normal_part, -6.0, 6.0)).astype(jnp.bfloat16)


def draw_query_states(key, part):
    key = jax.random.fold_in(key, 4)
    own_normal = jax.random.normal(key, (TOKENS, HEADS * HD), jnp.float32)
    return (1.4 * jnp.clip(own_normal, -6.0, 6.0)).astype(jnp.bfloat16)


def block_levels(own_key, extent, pieces, least, high):
    level, own = 1.0, jax.random.fold_in(own_key, 6)
    for axis_at, parts in pieces:
        heights = jnp.exp(jax.random.uniform(jax.random.fold_in(own, axis_at), (parts,), jnp.float32, least / len(pieces), high / len(pieces)))
        level = level * jnp.repeat(heights, extent[axis_at] // parts).reshape([-1 if axis == axis_at else 1 for axis in range(len(extent))])
    return level


def gaussian(own_key, extent, width, bound, shards=(), dtype=jnp.bfloat16):
    result = jax.random.normal(own_key, extent, jnp.float32) * width
    if len(shards) > 0:
        result = block_levels(own_key, extent, shards, -0.22, 0.18) * result
    return jnp.clip(result, min=-bound, max=bound).astype(dtype)


def setup_inputs(seed: int = 0) -> dict:
    splits = jax.random.split(jax.random.key(seed), 13)
    query_states = draw_query_states(jax.random.fold_in(splits[12], 71), 0)
    key_states = draw_key_states(jax.random.fold_in(splits[12], 71), 0)
    value_states = gaussian(splits[2], (TOKENS, HEADS * HD), 1.0, 6.0, ((0, 512),))
    base_patch = gaussian(splits[3], (TOKENS, PATCH), 0.5, 4.0, ((0, 512),))
    head_proj = gaussian(splits[4], (HEADS * HD, PATCH), (HEADS * HD // 16) ** -0.5, 0.4375, ((0, 8),))
    latent_std = jnp.clip(jnp.exp(jax.random.uniform(splits[5], (LATENT_CH,), jnp.float32, math.log(0.5), math.log(2.0))), 0.5, 2.0)
    latent_mean = jnp.clip(jax.random.uniform(splits[6], (LATENT_CH,), jnp.float32, -1.0, 1.0), -1.0, 1.0)
    w_in = gaussian(splits[7], (3, 3, 3, LATENT_CH, CH), (27 * LATENT_CH) ** -0.5, 0.3125)
    b_in = jnp.clip(jax.random.uniform(splits[8], (CH,), jnp.float32, -0.5, 0.5), -0.5, 0.5)
    gain_mid = jnp.clip(1.0 + 0.15 * jax.random.normal(splits[9], (CH,), jnp.float32), 0.25, 1.75)
    w_up = gaussian(splits[10], (3, 3, CH, OUTCH), (9 * CH) ** -0.5, 0.109375)
    b_up = jnp.clip(jax.random.uniform(splits[11], (OUTCH,), jnp.float32, -0.5, 0.5), -0.5, 0.5)
    return dict(query_states=query_states, key_states=key_states, value_states=value_states, base_patch=base_patch, head_proj=head_proj, latent_std=latent_std, latent_mean=latent_mean, w_in=w_in, b_in=b_in, gain_mid=gain_mid, w_up=w_up, b_up=b_up)


def attend_head(query_head, key_head, value_head):
    block_len = math.gcd(TOKENS, 1024)
    scaling = 1.0 / math.sqrt(HD)
    blocked = query_head.reshape(TOKENS // block_len, block_len, HD)

    def one_block(rows_in):
        scores = jnp.dot(rows_in, key_head.T, preferred_element_type=jnp.float32) * scaling
        row_max = lax.optimization_barrier(jnp.max(scores, axis=1, keepdims=True))
        weights = jnp.exp(scores - row_max)
        totals = lax.optimization_barrier(jnp.sum(weights, axis=1, keepdims=True))
        summed = jnp.dot(weights.astype(jnp.bfloat16), value_head, preferred_element_type=jnp.float32)
        return (summed / totals).astype(jnp.bfloat16)
    return lax.map(one_block, blocked).reshape(TOKENS, HD)

def by_heads(table):
    return table.reshape(TOKENS, HEADS, HD).transpose(1, 0, 2)

def conv_volume(padded, kernel):
    return lax.conv_general_dilated(padded[None], kernel, (1, 1, 1), 'VALID', dimension_numbers=('NDHWC', 'DHWIO', 'NDHWC'), preferred_element_type=jnp.float32)[0]

def conv_plane(padded, kernel):
    return lax.conv_general_dilated(padded, kernel, (1, 1), 'VALID', dimension_numbers=('NHWC', 'HWIO', 'NHWC'), preferred_element_type=jnp.float32)

def rms_silu(conv_out, gain_mid):
    mean_sq = lax.optimization_barrier(jnp.mean(conv_out * conv_out, axis=-1, keepdims=True))
    normed = conv_out * lax.rsqrt(mean_sq + 1e-06) * gain_mid
    return jax.nn.silu(normed).astype(jnp.bfloat16)

def enlarge(field):
    return jnp.repeat(jnp.repeat(field, 2, axis=1), 2, axis=2)

def reference(query_states, key_states, value_states, base_patch, head_proj, latent_std, latent_mean, w_in, b_in, gain_mid, w_up, b_up):
    per_head = lax.map(lambda triple: attend_head(triple[0], triple[1], triple[2]), (by_heads(query_states), by_heads(key_states), by_heads(value_states)))
    attended = per_head.transpose(1, 0, 2).reshape(TOKENS, HEADS * HD)
    patch = base_patch.astype(jnp.float32) + jnp.dot(attended, head_proj, preferred_element_type=jnp.float32)
    latent_grid = patch.reshape(HP, FRAMES, WP, 2, 2, LATENT_CH).transpose(1, 0, 3, 2, 4, 5).reshape(FRAMES, LH, LW, LATENT_CH)
    latent = (latent_grid * latent_std + latent_mean).astype(jnp.bfloat16)
    conv_out = conv_volume(jnp.pad(latent, ((2, 0), (1, 1), (1, 1), (0, 0))), w_in) + b_in
    activated = rms_silu(conv_out, gain_mid)
    enlarged = enlarge(activated)
    planes = conv_plane(jnp.pad(enlarged, ((0, 0), (1, 1), (1, 1), (0, 0))), w_up) + b_up
    return planes.astype(jnp.bfloat16)
```

```python
import math

import jax
import jax.numpy as jnp
from jax import lax
from jax.experimental import pallas as pl
from jax.experimental.pallas import tpu as pltpu
from jax.sharding import PartitionSpec as P

MESH = pl.DeviceIdType.MESH
F32, BF16 = jnp.float32, jnp.bfloat16

SEQ, GROUPS = 64, 8
ROWS = 4
PLACES = ROWS * GROUPS
OWN = 16
ROW = OWN * GROUPS
PLANE = ROW * ROWS
HD, LOCAL = 128, 3
WIDE = HD * LOCAL
PATCH = 64
NUM = PATCH * LOCAL
MSG = 256
CH, OUTCH = 384, 192
EDGE = 8
LINE = 48
TO_LOG2 = math.log2(math.e) / math.sqrt(HD)


def dot(a, b, dims):
    return lax.dot_general(a, b, (dims, ((), ())), preferred_element_type=F32)


def kernel(
    q_in, k_in, v_in, base_ref, proj_ref, std_ref, mean_ref, w_in_any, b_in_ref, gain_ref, w_up_any, b_up_ref,
    out_ref,
    kv, queries, top, total, summed, turned, sending, parts, lat_own, lat_near, w_in, w_two, w_up, enlarged, columns,
    plane_send, plane_recv, ring_send, ring_recv, part_send, part_recv, near_send, near_recv, weight_sem,
):
    s, g = lax.axis_index("seq"), lax.axis_index("head")
    z, row = s // ROWS, s % ROWS
    place = row * GROUPS + g
    up, down = ((s + ROWS) % SEQ, g), ((s + SEQ - ROWS) % SEQ, g)
    after, before = (s + 1) % SEQ, (s + SEQ - 1) % SEQ
    next_g, last_g = (g + 1) % GROUPS, (g + GROUPS - 1) % GROUPS

    def peer(i):
        other = (place + i) % PLACES
        return other, (z * ROWS + other // GROUPS, other % GROUPS)

    def columns_of(group):
        return pl.ds(pl.multiple_of(group * WIDE, WIDE), WIDE)

    def tokens_of(index):
        return pl.ds(pl.multiple_of(index * OWN, OWN), OWN)

    barrier = pltpu.get_barrier_semaphore()

    def greet(i, carry):
        pl.semaphore_signal(barrier, inc=1, device_id=peer(i)[1], device_id_type=MESH)
        return carry

    lax.fori_loop(1, PLACES, greet, 0)
    for other in (up, down, (after, g), (before, g), (after, last_g), (before, last_g)):
        pl.semaphore_signal(barrier, inc=1, device_id=other, device_id_type=MESH)

    weights_in = pltpu.make_async_copy(w_in_any, w_in, weight_sem.at[0])
    weights_up = pltpu.make_async_copy(w_up_any, w_up, weight_sem.at[1])
    weights_in.start()
    weights_up.start()
    for kind, source in ((0, k_in), (1, v_in)):
        pltpu.make_async_copy(
            source.at[:, columns_of(g)], kv.at[kind, 0, tokens_of(g)], plane_recv.at[kind]
        ).start()
    pltpu.make_async_copy(q_in.at[:, columns_of(g)], queries.at[tokens_of(place)], plane_recv.at[2]).start()
    pl.semaphore_wait(barrier, PLACES - 1 + 6)

    for kind, source in ((0, k_in), (1, v_in)):

        def send_row(i, carry):
            other = (g + i) % GROUPS
            pltpu.make_async_remote_copy(
                src_ref=source.at[:, columns_of(other)],
                dst_ref=kv.at[kind, 0, tokens_of(g)],
                send_sem=plane_send.at[kind],
                recv_sem=plane_recv.at[kind],
                device_id=(s, other),
                device_id_type=MESH,
            ).start()
            return carry

        lax.fori_loop(1, GROUPS, send_row, 0)

    def send_query(i, carry):
        device = peer(i)[1]
        pltpu.make_async_remote_copy(
            src_ref=q_in.at[:, columns_of(device[1])],
            dst_ref=queries.at[tokens_of(place)],
            send_sem=plane_send.at[2],
            recv_sem=plane_recv.at[2],
            device_id=device,
            device_id_type=MESH,
        ).start()
        return carry

    lax.fori_loop(1, PLACES, send_query, 0)

    def hop(kind, source, target, way):
        return pltpu.make_async_remote_copy(
            src_ref=kv.at[kind, source],
            dst_ref=kv.at[kind, target],
            send_sem=ring_send.at[way],
            recv_sem=ring_recv.at[kind, target],
            device_id=(up, down)[way],
            device_id_type=MESH,
        )

    def arrived(kind, slot):
        pltpu.make_async_copy(kv.at[kind, slot], kv.at[kind, slot], ring_recv.at[kind, slot]).wait()

    for kind in (0, 1):
        pltpu.make_async_copy(kv.at[kind, 0], kv.at[kind, 0], plane_recv.at[kind]).wait()
        hop(kind, 0, 1, 0).start()
        hop(kind, 0, 9, 1).start()

    weights_in.wait()
    w_two[...] = jnp.zeros_like(w_two)
    for t in range(3):
        for u in range(3):
            piece = w_in[(t * 3 + u) * 48 : (t * 3 + u) * 48 + 48, :]
            for half in range(2):
                at = t * 256 + (u + half) * 64
                w_two[at : at + 48, half * CH : half * CH + CH] = piece
    enlarged[...] = jnp.zeros_like(enlarged)
    turned[...] = jnp.zeros_like(turned)
    pltpu.make_async_copy(queries, queries, plane_recv.at[2]).wait()

    def attend(slots, first=False):
        for h in range(LOCAL):
            lanes = slice(h * HD, h * HD + HD)
            keys = [kv[0, slot, :, lanes] for slot in slots]
            values = [kv[1, slot, :, lanes] for slot in slots]
            keys = keys[0] if len(keys) == 1 else jnp.concatenate(keys, axis=0)
            values = values[0] if len(values) == 1 else jnp.concatenate(values, axis=0)
            for c in range(2):
                some = slice(c * 256, c * 256 + 256)
                scores = dot(keys, queries[some, lanes], ((1,), (1,)))
                new = jnp.max(scores, axis=0, keepdims=True)
                if not first:
                    old = top[h : h + 1, some]
                    new = jnp.maximum(old, new)
                    fading = jnp.exp2((old - new) * TO_LOG2)
                weights = jnp.exp2((scores - new) * TO_LOG2)
                sums = jnp.sum(weights, axis=0, keepdims=True)
                product = dot(values, weights.astype(BF16), ((0,), (0,)))
                if first:
                    total[h : h + 1, some] = sums
                    summed[lanes, some] = product
                else:
                    total[h : h + 1, some] = total[h : h + 1, some] * fading + sums
                    summed[lanes, some] = summed[lanes, some] * fading + product
                top[h : h + 1, some] = new

    attend([0], first=True)

    def step(t, carry):
        for kind in (0, 1):
            arrived(kind, t)
            hop(kind, t, t + 1, 0).start()
            arrived(kind, t + 8)
            hop(kind, t + 8, t + 9, 1).start()
        attend([t, t + 8])
        return carry

    lax.fori_loop(1, 7, step, 0)
    arrived(0, 7)
    hop(0, 7, 8, 0).start()
    arrived(0, 15)
    arrived(1, 15)
    hop(1, 15, 8, 1).start()
    arrived(1, 7)
    attend([7, 15])
    arrived(0, 8)
    arrived(1, 8)
    attend([8])

    for h in range(LOCAL):
        lanes = slice(h * HD, h * HD + HD)
        sums = total[h : h + 1, :]
        attended = (summed[lanes, :] / sums).astype(BF16)
        turned[h * PATCH : h * PATCH + PATCH, :] = dot(proj_ref[lanes, :], attended, ((0,), (0,)))
        level = top[h : h + 1, :] * TO_LOG2 + jnp.log(sums) * math.log2(math.e)
        for term in range(3):
            rounded = level.astype(BF16).astype(F32)
            turned[NUM + term * LOCAL + h : NUM + term * LOCAL + h + 1, :] = rounded
            level = level - rounded
    sending[...] = turned[...].T.astype(BF16)

    own_part = pltpu.make_async_copy(sending.at[tokens_of(place)], parts.at[tokens_of(place)], part_recv)
    own_part.start()

    def send_part(i, carry):
        other, device = peer(i)
        pltpu.make_async_remote_copy(
            src_ref=sending.at[tokens_of(other)],
            dst_ref=parts.at[tokens_of(place)],
            send_sem=part_send,
            recv_sem=part_recv,
            device_id=device,
            device_id_type=MESH,
        ).start()
        return carry

    lax.fori_loop(1, PLACES, send_part, 0)

    def ones_where(shape, made):
        r = lax.broadcasted_iota(jnp.int32, shape, 0)
        c = lax.broadcasted_iota(jnp.int32, shape, 1)
        return made(r, c).astype(F32).astype(BF16)

    spread = ones_where(
        (MSG, NUM),
        lambda r, c: (r >= NUM) & (r < NUM + 3 * LOCAL) & ((r - NUM) % LOCAL == c // PATCH),
    )
    pltpu.make_async_copy(parts, parts, part_recv).wait()

    levels = dot(parts[...], spread, ((1,), (0,)))
    values = parts[:, :NUM].astype(F32)
    by_row = [slice(r * ROW, r * ROW + ROW) for r in range(ROWS)]
    highest = levels[by_row[0]]
    for r in range(1, ROWS):
        highest = jnp.maximum(highest, levels[by_row[r]])
    above, below = 0.0, 0.0
    for r in range(ROWS):
        share = jnp.exp2(levels[by_row[r]] - highest)
        above = above + share * values[by_row[r]]
        below = below + share
    merged = above / below
    tokens = merged[:OWN]
    for other in range(1, GROUPS):
        tokens = tokens + merged[other * OWN : other * OWN + OWN]
    patch = base_ref[...].astype(F32)
    for h in range(LOCAL):
        patch = patch + tokens[:, h * PATCH : h * PATCH + PATCH]
    std = jnp.concatenate([std_ref[...]] * 4, axis=1)
    mean = jnp.concatenate([mean_ref[...]] * 4, axis=1)
    latent = patch * std + mean
    lat_own[...] = jnp.concatenate([latent, latent], axis=1).astype(BF16)

    for slot, device in enumerate(((after, next_g), (after, g), (s, next_g), (before, next_g), (before, g))):
        pltpu.make_async_remote_copy(
            src_ref=lat_own,
            dst_ref=lat_near.at[slot],
            send_sem=near_send,
            recv_sem=near_recv,
            device_id=device,
            device_id_type=MESH,
        ).start()

    def picks(b):
        def made(r, c):
            a, v, low = c // 64, (c // 16) % 4, c % 16
            spot = v + 1 - b
            wanted = (spot // 2) * 64 + a * 32 + (spot % 2) * 16 + low
            return (v < 3) & (r == wanted)

        return ones_where((128, 128), made)

    pick = [picks(0), picks(1)]
    pltpu.make_async_copy(lat_near, lat_near, near_recv).wait()

    has_before = (s > 0).astype(F32)
    has_after = (s < SEQ - 1).astype(F32)
    has_frames = (g > 0).astype(F32)
    tiles = [
        [lat_near[0].astype(F32) * (has_before * has_frames), lat_near[1].astype(F32) * has_before],
        [lat_near[2].astype(F32) * has_frames, lat_own[...].astype(F32)],
        [lat_near[3].astype(F32) * (has_after * has_frames), lat_near[4].astype(F32) * has_after],
    ]
    lane = lax.broadcasted_iota(jnp.int32, (8, 128), 1)
    line = lax.broadcasted_iota(jnp.int32, (8, 128), 0)
    sides = ([], [])
    for f in range(4):
        for r in range(3):
            here = tiles[r][f // 2][(f % 2) * 8 : (f % 2) * 8 + 8]
            left = jnp.where(line == 0, 0.0, pltpu.roll(here, 1, 0))
            right = jnp.where(line == 7, 0.0, pltpu.roll(here, 7, 0))
            sides[0].append(jnp.where(lane < 64, left, here))
            sides[1].append(jnp.where(lane < 64, here, right))
    windows = [
        dot(jnp.concatenate(side, axis=0).astype(BF16), chosen, ((1,), (0,))) for side, chosen in zip(sides, pick)
    ]

    def window(f, r, b):
        at = (f * 3 + r) * 8
        return windows[b][at : at + 8]

    lines = []
    for f in range(2):
        for pair in range(2):
            for b in range(2):
                pieces = [window(f + t, pair + r, b) for t in range(3) for r in range(2)]
                lines.append(jnp.concatenate(pieces, axis=1))
    conv = dot(jnp.concatenate(lines, axis=0).astype(BF16), w_two[...], ((1,), (0,)))
    for half in range(2):
        out = conv[:, half * CH : half * CH + CH] + b_in_ref[...]
        mean_sq = jnp.mean(out * out, axis=1, keepdims=True)
        normed = out * lax.rsqrt(mean_sq + 1e-6) * gain_ref[...]
        active = normed / (1.0 + jnp.exp(-normed))
        for f in range(2):
            for pair in range(2):
                y = 2 * pair + half
                for b in range(2):
                    at = ((f * 2 + pair) * 2 + b) * 8
                    part = active[at : at + 8]
                    if y == 0:
                        part = part * has_before
                    if y == 3:
                        part = part * has_after
                    for twice in range(2):
                        for tile in range(3):
                            enlarged[tile, f * 4 + y, pl.ds(EDGE + 2 * b + twice, 8, stride=4), :] = part[
                                :, tile * 128 : tile * 128 + 128
                            ]

    for v in range(3):
        for f in range(2):
            for y in range(4):
                piece = [enlarged[tile, f * 4 + y, EDGE - 1 + v : EDGE + 31 + v, :] for tile in range(3)]
                piece = jnp.concatenate(piece, axis=1).astype(BF16)
                for line_out in range(4):
                    for u in range(3):
                        if (line_out + u + 1) // 2 == y:
                            at = (f * 4 + line_out) * 32
                            to = (u * 3 + v) * CH
                            columns[at : at + 32, to : to + CH] = piece
    weights_up.wait()
    planes = dot(columns[...], w_up[...], ((1,), (0,))) + b_up_ref[...]
    out_ref[...] = planes.astype(BF16)

    for kind in (0, 1):
        sent = kv.at[kind, 0, : ROW - OWN]
        pltpu.make_async_copy(sent, sent, plane_send.at[kind]).wait()
    sent = queries.at[: PLANE - OWN]
    pltpu.make_async_copy(sent, sent, plane_send.at[2]).wait()
    for way in (0, 1):
        sent = kv.at[0, :15]
        pltpu.make_async_copy(sent, sent, ring_send.at[way]).wait()
    sent = parts.at[: PLANE - OWN]
    pltpu.make_async_copy(sent, sent, part_send).wait()
    pltpu.make_async_copy(lat_near, lat_near, near_send).wait()


def on_device(
    query_states,
    key_states,
    value_states,
    base_patch,
    head_proj,
    latent_std,
    latent_mean,
    w_in,
    b_in,
    gain_mid,
    w_up,
    b_up,
):
    here = pl.BlockSpec(memory_space=pltpu.VMEM)
    far = pl.BlockSpec(memory_space=pl.ANY)
    DMA = pltpu.SemaphoreType.DMA
    planes = pl.pallas_call(
        kernel,
        out_shape=jax.ShapeDtypeStruct((256, OUTCH), BF16),
        in_specs=[far, far, far, here, here, here, here, far, here, here, far, here],
        out_specs=here,
        scratch_shapes=[
            pltpu.VMEM((2, 16, ROW, WIDE), BF16),
            pltpu.VMEM((PLANE, WIDE), BF16),
            pltpu.VMEM((8, PLANE), F32),
            pltpu.VMEM((8, PLANE), F32),
            pltpu.VMEM((WIDE, PLANE), F32),
            pltpu.VMEM((MSG, PLANE), F32),
            pltpu.VMEM((PLANE, MSG), BF16),
            pltpu.VMEM((PLANE, MSG), BF16),
            pltpu.VMEM((OWN, 128), BF16),
            pltpu.VMEM((5, OWN, 128), BF16),
            pltpu.VMEM((27 * 16, CH), BF16),
            pltpu.VMEM((768, 2 * CH), BF16),
            pltpu.VMEM((9 * CH, OUTCH), BF16),
            pltpu.VMEM((3, 8, LINE, 128), F32),
            pltpu.VMEM((256, 9 * CH), BF16),
            DMA((3,)),
            DMA((3,)),
            DMA((2,)),
            DMA((2, 16)),
            DMA,
            DMA,
            DMA,
            DMA,
            DMA((2,)),
        ],
        compiler_params=pltpu.CompilerParams(
            collective_id=0, has_side_effects=True, vmem_limit_bytes=48 * 1024 * 1024
        ),
        name="attend_and_decode",
    )(
        query_states,
        key_states,
        value_states,
        base_patch,
        head_proj,
        latent_std.reshape(1, 16),
        latent_mean.reshape(1, 16),
        w_in.reshape(27 * 16, CH),
        b_in.reshape(1, CH),
        gain_mid.reshape(1, CH),
        w_up.reshape(9 * CH, OUTCH),
        b_up.reshape(1, OUTCH),
    )
    return planes.reshape(2, 4, 32, OUTCH)


def solution(mesh):
    in_specs = (
        P(("seq", "head"), None),
        P(("seq", "head"), None),
        P(("seq", "head"), None),
        P(("seq", "head"), None),
        P("head", None),
        P(),
        P(),
        P(),
        P(),
        P(),
        P(),
        P(),
    )
    out_specs = P("head", "seq", None, None)
    return jax.shard_map(
        on_device, mesh=mesh, in_specs=in_specs, out_specs=out_specs, check_vma=False
    )
```

```python
import math

import jax
import jax.numpy as jnp
from jax import lax
from jax.experimental import pallas as pl
from jax.experimental.pallas import tpu as pltpu
from jax.sharding import PartitionSpec as P

MESH = pl.DeviceIdType.MESH
F32, BF16 = jnp.float32, jnp.bfloat16

SEQ, GROUPS = 64, 8
ROWS = 4
PLACES = ROWS * GROUPS
OWN = 16
ROW = OWN * GROUPS
PLANE = ROW * ROWS
HD, LOCAL = 128, 3
WIDE = HD * LOCAL
PATCH = 64
NUM = PATCH * LOCAL
MSG = 256
CH, OUTCH = 384, 192
EDGE = 8
LINE = 48
TO_LOG2 = math.log2(math.e) / math.sqrt(HD)


def dot(a, b, dims):
    return lax.dot_general(a, b, (dims, ((), ())), preferred_element_type=F32)


def kernel(
    q_in, k_in, v_in, base_ref, proj_ref, std_ref, mean_ref, w_in_any, b_in_ref, gain_ref, w_up_any, b_up_ref,
    out_ref,
    kv, queries, top, total, fade, weighted, summed, turned, sending, parts, lat_own, lat_near, w_in, w_two, w_up, enlarged, columns,
    plane_send, plane_recv, ring_send, ring_recv, part_send, part_recv, near_send, near_recv, weight_sem,
):
    s, g = lax.axis_index("seq"), lax.axis_index("head")
    z, row = s // ROWS, s % ROWS
    place = row * GROUPS + g
    up, down = ((s + ROWS) % SEQ, g), ((s + SEQ - ROWS) % SEQ, g)
    after, before = (s + 1) % SEQ, (s + SEQ - 1) % SEQ
    next_g, last_g = (g + 1) % GROUPS, (g + GROUPS - 1) % GROUPS

    def peer(i):
        other = (place + i) % PLACES
        return other, (z * ROWS + other // GROUPS, other % GROUPS)

    def columns_of(group):
        return pl.ds(pl.multiple_of(group * WIDE, WIDE), WIDE)

    def tokens_of(index):
        return pl.ds(pl.multiple_of(index * OWN, OWN), OWN)

    barrier = pltpu.get_barrier_semaphore()

    def greet(i, carry):
        pl.semaphore_signal(barrier, inc=1, device_id=peer(i)[1], device_id_type=MESH)
        return carry

    lax.fori_loop(1, PLACES, greet, 0)
    for other in (up, down, (after, g), (before, g), (after, last_g), (before, last_g)):
        pl.semaphore_signal(barrier, inc=1, device_id=other, device_id_type=MESH)

    weights_in = pltpu.make_async_copy(w_in_any, w_in, weight_sem.at[0])
    weights_up = pltpu.make_async_copy(w_up_any, w_up, weight_sem.at[1])
    weights_in.start()
    weights_up.start()
    for kind, source in ((0, k_in), (1, v_in)):
        pltpu.make_async_copy(
            source.at[:, columns_of(g)], kv.at[kind, 0, tokens_of(g)], plane_recv.at[kind]
        ).start()
    pltpu.make_async_copy(q_in.at[:, columns_of(g)], queries.at[tokens_of(place)], plane_recv.at[2]).start()
    pl.semaphore_wait(barrier, PLACES - 1 + 6)

    for kind, source in ((0, k_in), (1, v_in)):

        def send_row(i, carry):
            other = (g + i) % GROUPS
            pltpu.make_async_remote_copy(
                src_ref=source.at[:, columns_of(other)],
                dst_ref=kv.at[kind, 0, tokens_of(g)],
                send_sem=plane_send.at[kind],
                recv_sem=plane_recv.at[kind],
                device_id=(s, other),
                device_id_type=MESH,
            ).start()
            return carry

        lax.fori_loop(1, GROUPS, send_row, 0)

    def send_query(i, carry):
        device = peer(i)[1]
        pltpu.make_async_remote_copy(
            src_ref=q_in.at[:, columns_of(device[1])],
            dst_ref=queries.at[tokens_of(place)],
            send_sem=plane_send.at[2],
            recv_sem=plane_recv.at[2],
            device_id=device,
            device_id_type=MESH,
        ).start()
        return carry

    lax.fori_loop(1, PLACES, send_query, 0)

    def hop(kind, source, target, way):
        return pltpu.make_async_remote_copy(
            src_ref=kv.at[kind, source],
            dst_ref=kv.at[kind, target],
            send_sem=ring_send.at[way],
            recv_sem=ring_recv.at[kind, target],
            device_id=(up, down)[way],
            device_id_type=MESH,
        )

    def arrived(kind, slot):
        pltpu.make_async_copy(kv.at[kind, slot], kv.at[kind, slot], ring_recv.at[kind, slot]).wait()

    for kind in (0, 1):
        pltpu.make_async_copy(kv.at[kind, 0], kv.at[kind, 0], plane_recv.at[kind]).wait()
        hop(kind, 0, 1, 0).start()
        hop(kind, 0, 9, 1).start()

    weights_in.wait()
    w_two[...] = jnp.zeros_like(w_two)
    for t in range(3):
        for u in range(3):
            piece = w_in[(t * 3 + u) * 48 : (t * 3 + u) * 48 + 48, :]
            for half in range(2):
                at = t * 256 + (u + half) * 64
                w_two[at : at + 48, half * CH : half * CH + CH] = piece
    enlarged[...] = jnp.zeros_like(enlarged)
    turned[...] = jnp.zeros_like(turned)
    pltpu.make_async_copy(queries, queries, plane_recv.at[2]).wait()

    def joined(kind, slots, lanes):
        pieces = [kv[kind, slot, :, lanes] for slot in slots]
        return pieces[0] if len(pieces) == 1 else jnp.concatenate(pieces, axis=0)

    units = [
        (h, slice(h * HD, h * HD + HD), slice(c * 256, c * 256 + 256)) for h in range(LOCAL) for c in range(2)
    ]

    def weigh(slots, first=False):
        for h, lanes, some in units:
            scores = dot(joined(0, slots, lanes), queries[some, lanes], ((1,), (1,)))
            new = jnp.max(scores, axis=0, keepdims=True)
            if not first:
                old = top[h : h + 1, some]
                new = jnp.maximum(old, new)
                fading = jnp.exp2((old - new) * TO_LOG2)
                fade[h : h + 1, some] = fading
            weights = jnp.exp2((scores - new) * TO_LOG2)
            sums = jnp.sum(weights, axis=0, keepdims=True)
            total[h : h + 1, some] = sums if first else total[h : h + 1, some] * fading + sums
            top[h : h + 1, some] = new
            weighted[h, : len(slots) * ROW, some] = weights.astype(BF16)

    def add_up(slots, first=False):
        for h, lanes, some in units:
            product = dot(joined(1, slots, lanes), weighted[h, : len(slots) * ROW, some], ((0,), (0,)))
            summed[lanes, some] = product if first else summed[lanes, some] * fade[h : h + 1, some] + product

    weigh([0], first=True)
    add_up([0], first=True)

    def step(t, carry):
        arrived(0, t)
        hop(0, t, t + 1, 0).start()
        arrived(0, t + 8)
        hop(0, t + 8, t + 9, 1).start()
        weigh([t, t + 8])
        arrived(1, t)
        hop(1, t, t + 1, 0).start()
        arrived(1, t + 8)
        hop(1, t + 8, t + 9, 1).start()
        add_up([t, t + 8])
        return carry

    lax.fori_loop(1, 7, step, 0)
    arrived(0, 7)
    hop(0, 7, 8, 0).start()
    arrived(0, 15)
    weigh([7, 15])
    arrived(1, 15)
    hop(1, 15, 8, 1).start()
    arrived(1, 7)
    add_up([7, 15])
    arrived(0, 8)
    weigh([8])
    arrived(1, 8)
    add_up([8])

    for h in range(LOCAL):
        lanes = slice(h * HD, h * HD + HD)
        sums = total[h : h + 1, :]
        attended = (summed[lanes, :] / sums).astype(BF16)
        turned[h * PATCH : h * PATCH + PATCH, :] = dot(proj_ref[:, lanes], attended, ((1,), (0,)))
        level = top[h : h + 1, :] * TO_LOG2 + jnp.log(sums) * math.log2(math.e)
        for term in range(3):
            rounded = level.astype(BF16).astype(F32)
            turned[NUM + term * LOCAL + h : NUM + term * LOCAL + h + 1, :] = rounded
            level = level - rounded
    sending[...] = turned[...].T.astype(BF16)

    own_part = pltpu.make_async_copy(sending.at[tokens_of(place)], parts.at[tokens_of(place)], part_recv)
    own_part.start()

    def send_part(i, carry):
        other, device = peer(i)
        pltpu.make_async_remote_copy(
            src_ref=sending.at[tokens_of(other)],
            dst_ref=parts.at[tokens_of(place)],
            send_sem=part_send,
            recv_sem=part_recv,
            device_id=device,
            device_id_type=MESH,
        ).start()
        return carry

    lax.fori_loop(1, PLACES, send_part, 0)

    def ones_where(shape, made):
        r = lax.broadcasted_iota(jnp.int32, shape, 0)
        c = lax.broadcasted_iota(jnp.int32, shape, 1)
        return made(r, c).astype(F32).astype(BF16)

    spread = ones_where(
        (MSG, NUM),
        lambda r, c: (r >= NUM) & (r < NUM + 3 * LOCAL) & ((r - NUM) % LOCAL == c // PATCH),
    )
    pltpu.make_async_copy(parts, parts, part_recv).wait()

    levels = dot(parts[...], spread, ((1,), (0,)))
    values = parts[:, :NUM].astype(F32)
    by_row = [slice(r * ROW, r * ROW + ROW) for r in range(ROWS)]
    highest = levels[by_row[0]]
    for r in range(1, ROWS):
        highest = jnp.maximum(highest, levels[by_row[r]])
    above, below = 0.0, 0.0
    for r in range(ROWS):
        share = jnp.exp2(levels[by_row[r]] - highest)
        above = above + share * values[by_row[r]]
        below = below + share
    merged = above / below
    tokens = merged[:OWN]
    for other in range(1, GROUPS):
        tokens = tokens + merged[other * OWN : other * OWN + OWN]
    patch = base_ref[...].astype(F32)
    for h in range(LOCAL):
        patch = patch + tokens[:, h * PATCH : h * PATCH + PATCH]
    std = jnp.concatenate([std_ref[...]] * 4, axis=1)
    mean = jnp.concatenate([mean_ref[...]] * 4, axis=1)
    latent = patch * std + mean
    lat_own[...] = jnp.concatenate([latent, latent], axis=1).astype(BF16)

    for slot, device in enumerate(((after, next_g), (after, g), (s, next_g), (before, next_g), (before, g))):
        pltpu.make_async_remote_copy(
            src_ref=lat_own,
            dst_ref=lat_near.at[slot],
            send_sem=near_send,
            recv_sem=near_recv,
            device_id=device,
            device_id_type=MESH,
        ).start()

    def picks(b):
        def made(r, c):
            a, v, low = c // 64, (c // 16) % 4, c % 16
            spot = v + 1 - b
            wanted = (spot // 2) * 64 + a * 32 + (spot % 2) * 16 + low
            return (v < 3) & (r == wanted)

        return ones_where((128, 128), made)

    pick = [picks(0), picks(1)]
    pltpu.make_async_copy(lat_near, lat_near, near_recv).wait()

    has_before = (s > 0).astype(F32)
    has_after = (s < SEQ - 1).astype(F32)
    has_frames = (g > 0).astype(F32)
    tiles = [
        [lat_near[0].astype(F32) * (has_before * has_frames), lat_near[1].astype(F32) * has_before],
        [lat_near[2].astype(F32) * has_frames, lat_own[...].astype(F32)],
        [lat_near[3].astype(F32) * (has_after * has_frames), lat_near[4].astype(F32) * has_after],
    ]
    lane = lax.broadcasted_iota(jnp.int32, (8, 128), 1)
    line = lax.broadcasted_iota(jnp.int32, (8, 128), 0)
    sides = ([], [])
    for f in range(4):
        for r in range(3):
            here = tiles[r][f // 2][(f % 2) * 8 : (f % 2) * 8 + 8]
            left = jnp.where(line == 0, 0.0, pltpu.roll(here, 1, 0))
            right = jnp.where(line == 7, 0.0, pltpu.roll(here, 7, 0))
            sides[0].append(jnp.where(lane < 64, left, here))
            sides[1].append(jnp.where(lane < 64, here, right))
    windows = [
        dot(jnp.concatenate(side, axis=0).astype(BF16), chosen, ((1,), (0,))) for side, chosen in zip(sides, pick)
    ]

    def window(f, r, b):
        at = (f * 3 + r) * 8
        return windows[b][at : at + 8]

    lines = []
    for f in range(2):
        for pair in range(2):
            for b in range(2):
                pieces = [window(f + t, pair + r, b) for t in range(3) for r in range(2)]
                lines.append(jnp.concatenate(pieces, axis=1))
    conv = dot(jnp.concatenate(lines, axis=0).astype(BF16), w_two[...], ((1,), (0,)))
    for half in range(2):
        out = conv[:, half * CH : half * CH + CH] + b_in_ref[...].reshape(1, CH)
        mean_sq = jnp.mean(out * out, axis=1, keepdims=True)
        normed = out * lax.rsqrt(mean_sq + 1e-6) * gain_ref[...].reshape(1, CH)
        active = normed / (1.0 + jnp.exp(-normed))
        for f in range(2):
            for pair in range(2):
                y = 2 * pair + half
                for b in range(2):
                    at = ((f * 2 + pair) * 2 + b) * 8
                    part = active[at : at + 8]
                    if y == 0:
                        part = part * has_before
                    if y == 3:
                        part = part * has_after
                    for twice in range(2):
                        for tile in range(3):
                            enlarged[tile, f * 4 + y, pl.ds(EDGE + 2 * b + twice, 8, stride=4), :] = part[
                                :, tile * 128 : tile * 128 + 128
                            ]

    for v in range(3):
        for f in range(2):
            for y in range(4):
                piece = [enlarged[tile, f * 4 + y, EDGE - 1 + v : EDGE + 31 + v, :] for tile in range(3)]
                piece = jnp.concatenate(piece, axis=1).astype(BF16)
                for line_out in range(4):
                    for u in range(3):
                        if (line_out + u + 1) // 2 == y:
                            at = (f * 4 + line_out) * 32
                            to = (u * 3 + v) * CH
                            columns[at : at + 32, to : to + CH] = piece
    weights_up.wait()
    planes = b_up_ref[...]
    for tap in range(9):
        planes = planes + dot(
            columns[:, tap * CH : tap * CH + CH], w_up[tap * OUTCH : tap * OUTCH + OUTCH, :], ((1,), (1,))
        )
    out_ref[...] = planes.astype(BF16)

    for kind in (0, 1):
        sent = kv.at[kind, 0, : ROW - OWN]
        pltpu.make_async_copy(sent, sent, plane_send.at[kind]).wait()
    sent = queries.at[: PLANE - OWN]
    pltpu.make_async_copy(sent, sent, plane_send.at[2]).wait()
    for way in (0, 1):
        sent = kv.at[0, :15]
        pltpu.make_async_copy(sent, sent, ring_send.at[way]).wait()
    sent = parts.at[: PLANE - OWN]
    pltpu.make_async_copy(sent, sent, part_send).wait()
    pltpu.make_async_copy(lat_near, lat_near, near_send).wait()


def on_device(
    query_states,
    key_states,
    value_states,
    base_patch,
    head_proj,
    latent_std,
    latent_mean,
    w_in,
    b_in,
    gain_mid,
    w_up,
    b_up,
):
    here = pl.BlockSpec(memory_space=pltpu.VMEM)
    far = pl.BlockSpec(memory_space=pl.ANY)
    DMA = pltpu.SemaphoreType.DMA
    planes = pl.pallas_call(
        kernel,
        out_shape=jax.ShapeDtypeStruct((256, OUTCH), BF16),
        in_specs=[far, far, far, here, here, here, here, far, here, here, far, here],
        out_specs=here,
        scratch_shapes=[
            pltpu.VMEM((2, 16, ROW, WIDE), BF16),
            pltpu.VMEM((PLANE, WIDE), BF16),
            pltpu.VMEM((8, PLANE), F32),
            pltpu.VMEM((8, PLANE), F32),
            pltpu.VMEM((8, PLANE), F32),
            pltpu.VMEM((LOCAL, 2 * ROW, PLANE), BF16),
            pltpu.VMEM((WIDE, PLANE), F32),
            pltpu.VMEM((MSG, PLANE), F32),
            pltpu.VMEM((PLANE, MSG), BF16),
            pltpu.VMEM((PLANE, MSG), BF16),
            pltpu.VMEM((OWN, 128), BF16),
            pltpu.VMEM((5, OWN, 128), BF16),
            pltpu.VMEM((27 * 16, CH), BF16),
            pltpu.VMEM((768, 2 * CH), BF16),
            pltpu.VMEM((9 * OUTCH, CH), BF16),
            pltpu.VMEM((3, 8, LINE, 128), F32),
            pltpu.VMEM((256, 9 * CH), BF16),
            DMA((3,)),
            DMA((3,)),
            DMA((2,)),
            DMA((2, 16)),
            DMA,
            DMA,
            DMA,
            DMA,
            DMA((2,)),
        ],
        compiler_params=pltpu.CompilerParams(
            collective_id=0, has_side_effects=True, vmem_limit_bytes=48 * 1024 * 1024
        ),
        name="attend_and_decode",
    )(
        query_states,
        key_states,
        value_states,
        base_patch,
        head_proj.T,
        latent_std.reshape(1, 16),
        latent_mean.reshape(1, 16),
        w_in.reshape(27 * 16, CH),
        b_in,
        gain_mid,
        w_up.transpose(0, 1, 3, 2).reshape(9 * OUTCH, CH),
        b_up.reshape(1, OUTCH),
    )
    return planes.reshape(2, 4, 32, OUTCH)


def solution(mesh):
    in_specs = (
        P(("seq", "head"), None),
        P(("seq", "head"), None),
        P(("seq", "head"), None),
        P(("seq", "head"), None),
        P("head", None),
        P(),
        P(),
        P(),
        P(),
        P(),
        P(),
        P(),
    )
    out_specs = P("head", "seq", None, None)
    return jax.shard_map(
        on_device, mesh=mesh, in_specs=in_specs, out_specs=out_specs, check_vma=False
    )
```

```python
import math

import jax
import jax.numpy as jnp
from jax import lax
from jax.experimental import pallas as pl
from jax.experimental.pallas import tpu as pltpu
from jax.sharding import PartitionSpec as P

MESH = pl.DeviceIdType.MESH
F32, BF16 = jnp.float32, jnp.bfloat16

SEQ, GROUPS = 64, 8
ROWS = 4
PLACES = ROWS * GROUPS
OWN = 16
ROW = OWN * GROUPS
PLANE = ROW * ROWS
HD, LOCAL = 128, 3
WIDE = HD * LOCAL
PATCH = 64
NUM = PATCH * LOCAL
MSG = 256
CH, OUTCH = 384, 192
EDGE = 8
LINE = 48
TO_LOG2 = math.log2(math.e) / math.sqrt(HD)


def dot(a, b, dims):
    return lax.dot_general(a, b, (dims, ((), ())), preferred_element_type=F32)


def kernel(
    q_in, k_in, v_in, base_far, proj_far, std_far, mean_far, w_in_far, b_in_far, gain_far, w_up_far, b_up_far,
    out_ref,
    keys, values, v_row, queries, top, total, fade, weighted, summed, turned, sending, parts, lat_own, lat_near,
    base_ref, proj_ref, std_ref, mean_ref, w_in, b_in_ref, gain_ref, w_up, b_up_ref, w_two, enlarged, columns,
    plane_send, plane_recv, ring_send, ring_recv, part_send, part_recv, near_send, near_recv, weight_sem,
):
    s, g = lax.axis_index("seq"), lax.axis_index("head")
    z, row = s // ROWS, s % ROWS
    place = row * GROUPS + g
    up, down = ((s + ROWS) % SEQ, g), ((s + SEQ - ROWS) % SEQ, g)
    after, before = (s + 1) % SEQ, (s + SEQ - 1) % SEQ
    next_g, last_g = (g + 1) % GROUPS, (g + GROUPS - 1) % GROUPS

    def peer(i):
        other = (place + i) % PLACES
        return other, (z * ROWS + other // GROUPS, other % GROUPS)

    def columns_of(group):
        return pl.ds(pl.multiple_of(group * WIDE, WIDE), WIDE)

    def tokens_of(index):
        return pl.ds(pl.multiple_of(index * OWN, OWN), OWN)

    barrier = pltpu.get_barrier_semaphore()

    def greet(i, carry):
        pl.semaphore_signal(barrier, inc=1, device_id=peer(i)[1], device_id_type=MESH)
        return carry

    lax.fori_loop(1, PLACES, greet, 0)
    for other in (up, down, (after, g), (before, g), (after, last_g), (before, last_g)):
        pl.semaphore_signal(barrier, inc=1, device_id=other, device_id_type=MESH)

    rows_of = ((k_in, keys.at[0]), (v_in, v_row))
    for kind, (source, target) in enumerate(rows_of):
        pltpu.make_async_copy(source.at[:, columns_of(g)], target.at[tokens_of(g)], plane_recv.at[kind]).start()
    pltpu.make_async_copy(q_in.at[:, columns_of(g)], queries.at[tokens_of(place)], plane_recv.at[2]).start()
    parameters = [
        pltpu.make_async_copy(source, target, weight_sem.at[i])
        for i, (source, target) in enumerate(
            (
                (w_in_far, w_in),
                (w_up_far, w_up),
                (base_far, base_ref),
                (proj_far, proj_ref),
                (std_far, std_ref),
                (mean_far, mean_ref),
                (b_in_far, b_in_ref),
                (gain_far, gain_ref),
                (b_up_far, b_up_ref),
            )
        )
    ]
    for copy in parameters:
        copy.start()
    pl.semaphore_wait(barrier, PLACES - 1 + 6)

    for kind, (source, target) in enumerate(rows_of):

        def send_row(i, carry):
            other = (g + i) % GROUPS
            pltpu.make_async_remote_copy(
                src_ref=source.at[:, columns_of(other)],
                dst_ref=target.at[tokens_of(g)],
                send_sem=plane_send.at[kind],
                recv_sem=plane_recv.at[kind],
                device_id=(s, other),
                device_id_type=MESH,
            ).start()
            return carry

        lax.fori_loop(1, GROUPS, send_row, 0)

    def send_query(i, carry):
        device = peer(i)[1]
        pltpu.make_async_remote_copy(
            src_ref=q_in.at[:, columns_of(device[1])],
            dst_ref=queries.at[tokens_of(place)],
            send_sem=plane_send.at[2],
            recv_sem=plane_recv.at[2],
            device_id=device,
            device_id_type=MESH,
        ).start()
        return carry

    lax.fori_loop(1, PLACES, send_query, 0)

    rings = (keys, values)

    def hop(kind, source, target, way):
        return pltpu.make_async_remote_copy(
            src_ref=rings[kind].at[source],
            dst_ref=rings[kind].at[target],
            send_sem=ring_send.at[way],
            recv_sem=ring_recv.at[kind, target],
            device_id=(up, down)[way],
            device_id_type=MESH,
        )

    def arrived(kind, slot):
        pltpu.make_async_copy(rings[kind].at[slot], rings[kind].at[slot], ring_recv.at[kind, slot]).wait()

    for kind, (source, target) in enumerate(rows_of):
        pltpu.make_async_copy(target, target, plane_recv.at[kind]).wait()
        if kind == 1:
            values[0] = v_row[...].T
        hop(kind, 0, 1, 0).start()
        hop(kind, 0, 9, 1).start()

    for copy in parameters:
        copy.wait()
    w_two[...] = jnp.zeros_like(w_two)
    for t in range(3):
        for u in range(3):
            piece = w_in[(t * 3 + u) * 48 : (t * 3 + u) * 48 + 48, :]
            for half in range(2):
                at = t * 256 + (u + half) * 64
                w_two[at : at + 48, half * CH : half * CH + CH] = piece
    enlarged[...] = jnp.zeros_like(enlarged)
    turned[...] = jnp.zeros_like(turned)
    pltpu.make_async_copy(queries, queries, plane_recv.at[2]).wait()

    def joined(pieces, axis):
        return pieces[0] if len(pieces) == 1 else jnp.concatenate(pieces, axis=axis)

    units = [
        (h, slice(h * HD, h * HD + HD), slice(c * 256, c * 256 + 256)) for h in range(LOCAL) for c in range(2)
    ]

    def weigh(slots, first=False):
        for h, lanes, some in units:
            some_keys = joined([keys[slot, :, lanes] for slot in slots], 0)
            scores = dot(some_keys, queries[some, lanes], ((1,), (1,)))
            new = jnp.max(scores, axis=0, keepdims=True)
            if not first:
                old = top[h : h + 1, some]
                new = jnp.maximum(old, new)
                fading = jnp.exp2((old - new) * TO_LOG2)
                fade[h : h + 1, some] = fading
            weights = jnp.exp2((scores - new) * TO_LOG2)
            sums = jnp.sum(weights, axis=0, keepdims=True)
            total[h : h + 1, some] = sums if first else total[h : h + 1, some] * fading + sums
            top[h : h + 1, some] = new
            weighted[h, : len(slots) * ROW, some] = weights.astype(BF16)

    def add_up(slots, first=False):
        for h, lanes, some in units:
            some_values = joined([values[slot, lanes, :] for slot in slots], 1)
            product = dot(some_values, weighted[h, : len(slots) * ROW, some], ((1,), (0,)))
            summed[lanes, some] = product if first else summed[lanes, some] * fade[h : h + 1, some] + product

    weigh([0], first=True)
    add_up([0], first=True)

    def step(t, carry):
        arrived(0, t)
        hop(0, t, t + 1, 0).start()
        arrived(0, t + 8)
        hop(0, t + 8, t + 9, 1).start()
        weigh([t, t + 8])
        arrived(1, t)
        hop(1, t, t + 1, 0).start()
        arrived(1, t + 8)
        hop(1, t + 8, t + 9, 1).start()
        add_up([t, t + 8])
        return carry

    lax.fori_loop(1, 7, step, 0)
    arrived(0, 7)
    hop(0, 7, 8, 0).start()
    arrived(0, 15)
    weigh([7, 15])
    arrived(1, 15)
    hop(1, 15, 8, 1).start()
    arrived(1, 7)
    add_up([7, 15])
    arrived(0, 8)
    weigh([8])
    arrived(1, 8)
    add_up([8])

    for h in range(LOCAL):
        lanes = slice(h * HD, h * HD + HD)
        sums = total[h : h + 1, :]
        attended = (summed[lanes, :] / sums).astype(BF16)
        turned[h * PATCH : h * PATCH + PATCH, :] = dot(proj_ref[:, lanes], attended, ((1,), (0,)))
        level = top[h : h + 1, :] * TO_LOG2 + jnp.log(sums) * math.log2(math.e)
        for term in range(3):
            rounded = level.astype(BF16).astype(F32)
            turned[NUM + term * LOCAL + h : NUM + term * LOCAL + h + 1, :] = rounded
            level = level - rounded
    sending[...] = turned[...].T.astype(BF16)

    own_part = pltpu.make_async_copy(sending.at[tokens_of(place)], parts.at[tokens_of(place)], part_recv)
    own_part.start()

    def send_part(i, carry):
        other, device = peer(i)
        pltpu.make_async_remote_copy(
            src_ref=sending.at[tokens_of(other)],
            dst_ref=parts.at[tokens_of(place)],
            send_sem=part_send,
            recv_sem=part_recv,
            device_id=device,
            device_id_type=MESH,
        ).start()
        return carry

    lax.fori_loop(1, PLACES, send_part, 0)

    def ones_where(shape, made):
        r = lax.broadcasted_iota(jnp.int32, shape, 0)
        c = lax.broadcasted_iota(jnp.int32, shape, 1)
        return made(r, c).astype(F32).astype(BF16)

    spread = ones_where(
        (MSG, NUM),
        lambda r, c: (r >= NUM) & (r < NUM + 3 * LOCAL) & ((r - NUM) % LOCAL == c // PATCH),
    )
    pltpu.make_async_copy(parts, parts, part_recv).wait()

    levels = dot(parts[...], spread, ((1,), (0,)))
    numbers = parts[:, :NUM].astype(F32)
    by_row = [slice(r * ROW, r * ROW + ROW) for r in range(ROWS)]
    highest = levels[by_row[0]]
    for r in range(1, ROWS):
        highest = jnp.maximum(highest, levels[by_row[r]])
    above, below = 0.0, 0.0
    for r in range(ROWS):
        share = jnp.exp2(levels[by_row[r]] - highest)
        above = above + share * numbers[by_row[r]]
        below = below + share
    merged = above / below
    tokens = merged[:OWN]
    for other in range(1, GROUPS):
        tokens = tokens + merged[other * OWN : other * OWN + OWN]
    patch = base_ref[...].astype(F32)
    for h in range(LOCAL):
        patch = patch + tokens[:, h * PATCH : h * PATCH + PATCH]
    std = jnp.concatenate([std_ref[...]] * 4, axis=1)
    mean = jnp.concatenate([mean_ref[...]] * 4, axis=1)
    latent = patch * std + mean
    lat_own[...] = jnp.concatenate([latent, latent], axis=1).astype(BF16)

    for slot, device in enumerate(((after, next_g), (after, g), (s, next_g), (before, next_g), (before, g))):
        pltpu.make_async_remote_copy(
            src_ref=lat_own,
            dst_ref=lat_near.at[slot],
            send_sem=near_send,
            recv_sem=near_recv,
            device_id=device,
            device_id_type=MESH,
        ).start()

    def picks(b):
        def made(r, c):
            a, v, low = c // 64, (c // 16) % 4, c % 16
            spot = v + 1 - b
            wanted = (spot // 2) * 64 + a * 32 + (spot % 2) * 16 + low
            return (v < 3) & (r == wanted)

        return ones_where((128, 128), made)

    pick = [picks(0), picks(1)]
    pltpu.make_async_copy(lat_near, lat_near, near_recv).wait()

    has_before = (s > 0).astype(F32)
    has_after = (s < SEQ - 1).astype(F32)
    has_frames = (g > 0).astype(F32)
    tiles = [
        [lat_near[0].astype(F32) * (has_before * has_frames), lat_near[1].astype(F32) * has_before],
        [lat_near[2].astype(F32) * has_frames, lat_own[...].astype(F32)],
        [lat_near[3].astype(F32) * (has_after * has_frames), lat_near[4].astype(F32) * has_after],
    ]
    lane = lax.broadcasted_iota(jnp.int32, (8, 128), 1)
    line = lax.broadcasted_iota(jnp.int32, (8, 128), 0)
    sides = ([], [])
    for f in range(4):
        for r in range(3):
            here = tiles[r][f // 2][(f % 2) * 8 : (f % 2) * 8 + 8]
            left = jnp.where(line == 0, 0.0, pltpu.roll(here, 1, 0))
            right = jnp.where(line == 7, 0.0, pltpu.roll(here, 7, 0))
            sides[0].append(jnp.where(lane < 64, left, here))
            sides[1].append(jnp.where(lane < 64, here, right))
    windows = [
        dot(jnp.concatenate(side, axis=0).astype(BF16), chosen, ((1,), (0,))) for side, chosen in zip(sides, pick)
    ]

    def window(f, r, b):
        at = (f * 3 + r) * 8
        return windows[b][at : at + 8]

    lines = []
    for f in range(2):
        for pair in range(2):
            for b in range(2):
                pieces = [window(f + t, pair + r, b) for t in range(3) for r in range(2)]
                lines.append(jnp.concatenate(pieces, axis=1))
    conv = dot(jnp.concatenate(lines, axis=0).astype(BF16), w_two[...], ((1,), (0,)))
    for half in range(2):
        out = conv[:, half * CH : half * CH + CH] + b_in_ref[...].reshape(1, CH)
        mean_sq = jnp.mean(out * out, axis=1, keepdims=True)
        normed = out * lax.rsqrt(mean_sq + 1e-6) * gain_ref[...].reshape(1, CH)
        active = normed / (1.0 + jnp.exp(-normed))
        for f in range(2):
            for pair in range(2):
                y = 2 * pair + half
                for b in range(2):
                    at = ((f * 2 + pair) * 2 + b) * 8
                    part = active[at : at + 8]
                    if y == 0:
                        part = part * has_before
                    if y == 3:
                        part = part * has_after
                    for twice in range(2):
                        for tile in range(3):
                            enlarged[tile, f * 4 + y, pl.ds(EDGE + 2 * b + twice, 8, stride=4), :] = part[
                                :, tile * 128 : tile * 128 + 128
                            ]

    for v in range(3):
        for f in range(2):
            for y in range(4):
                piece = [enlarged[tile, f * 4 + y, EDGE - 1 + v : EDGE + 31 + v, :] for tile in range(3)]
                piece = jnp.concatenate(piece, axis=1).astype(BF16)
                for line_out in range(4):
                    for u in range(3):
                        if (line_out + u + 1) // 2 == y:
                            at = (f * 4 + line_out) * 32
                            to = (u * 3 + v) * CH
                            columns[at : at + 32, to : to + CH] = piece
    planes = b_up_ref[...]
    for tap in range(9):
        planes = planes + dot(
            columns[:, tap * CH : tap * CH + CH], w_up[tap * OUTCH : tap * OUTCH + OUTCH, :], ((1,), (1,))
        )
    out_ref[...] = planes.astype(BF16)

    for kind in (0, 1):
        sent = v_row.at[: ROW - OWN]
        pltpu.make_async_copy(sent, sent, plane_send.at[kind]).wait()
    sent = queries.at[: PLANE - OWN]
    pltpu.make_async_copy(sent, sent, plane_send.at[2]).wait()
    for way in (0, 1):
        sent = keys.at[:15]
        pltpu.make_async_copy(sent, sent, ring_send.at[way]).wait()
    sent = parts.at[: PLANE - OWN]
    pltpu.make_async_copy(sent, sent, part_send).wait()
    pltpu.make_async_copy(lat_near, lat_near, near_send).wait()


def on_device(
    query_states,
    key_states,
    value_states,
    base_patch,
    head_proj,
    latent_std,
    latent_mean,
    w_in,
    b_in,
    gain_mid,
    w_up,
    b_up,
):
    here = pl.BlockSpec(memory_space=pltpu.VMEM)
    far = pl.BlockSpec(memory_space=pltpu.HBM)
    DMA = pltpu.SemaphoreType.DMA
    planes = pl.pallas_call(
        kernel,
        out_shape=jax.ShapeDtypeStruct((256, OUTCH), BF16),
        in_specs=[far] * 12,
        out_specs=here,
        scratch_shapes=[
            pltpu.VMEM((16, ROW, WIDE), BF16),
            pltpu.VMEM((16, WIDE, ROW), BF16),
            pltpu.VMEM((ROW, WIDE), BF16),
            pltpu.VMEM((PLANE, WIDE), BF16),
            pltpu.VMEM((8, PLANE), F32),
            pltpu.VMEM((8, PLANE), F32),
            pltpu.VMEM((8, PLANE), F32),
            pltpu.VMEM((LOCAL, 2 * ROW, PLANE), BF16),
            pltpu.VMEM((WIDE, PLANE), F32),
            pltpu.VMEM((MSG, PLANE), F32),
            pltpu.VMEM((PLANE, MSG), BF16),
            pltpu.VMEM((PLANE, MSG), BF16),
            pltpu.VMEM((OWN, 128), BF16),
            pltpu.VMEM((5, OWN, 128), BF16),
            pltpu.VMEM((OWN, PATCH), BF16),
            pltpu.VMEM((PATCH, WIDE), BF16),
            pltpu.VMEM((1, 16), F32),
            pltpu.VMEM((1, 16), F32),
            pltpu.VMEM((27 * 16, CH), BF16),
            pltpu.VMEM((CH,), F32),
            pltpu.VMEM((CH,), F32),
            pltpu.VMEM((9 * OUTCH, CH), BF16),
            pltpu.VMEM((1, OUTCH), F32),
            pltpu.VMEM((768, 2 * CH), BF16),
            pltpu.VMEM((3, 8, LINE, 128), F32),
            pltpu.VMEM((256, 9 * CH), BF16),
            DMA((3,)),
            DMA((3,)),
            DMA((2,)),
            DMA((2, 16)),
            DMA,
            DMA,
            DMA,
            DMA,
            DMA((9,)),
        ],
        compiler_params=pltpu.CompilerParams(
            collective_id=0, has_side_effects=True, vmem_limit_bytes=60 * 1024 * 1024
        ),
        name="attend_and_decode",
    )(
        query_states,
        key_states,
        value_states,
        base_patch,
        head_proj.T,
        latent_std.reshape(1, 16),
        latent_mean.reshape(1, 16),
        w_in.reshape(27 * 16, CH),
        b_in,
        gain_mid,
        w_up.transpose(0, 1, 3, 2).reshape(9 * OUTCH, CH),
        b_up.reshape(1, OUTCH),
    )
    return planes.reshape(2, 4, 32, OUTCH)


def solution(mesh):
    in_specs = (
        P(("seq", "head"), None),
        P(("seq", "head"), None),
        P(("seq", "head"), None),
        P(("seq", "head"), None),
        P("head", None),
        P(),
        P(),
        P(),
        P(),
        P(),
        P(),
        P(),
    )
    out_specs = P("head", "seq", None, None)
    return jax.shard_map(
        on_device, mesh=mesh, in_specs=in_specs, out_specs=out_specs, check_vma=False
    )
```

```python
import math

import jax
import jax.numpy as jnp
from jax import lax
from jax.experimental import pallas as pl
from jax.experimental.pallas import tpu as pltpu
from jax.sharding import PartitionSpec as P

MESH = pl.DeviceIdType.MESH
F32, BF16 = jnp.float32, jnp.bfloat16

SEQ, GROUPS = 64, 8
ROWS = 4
PLACES = ROWS * GROUPS
OWN = 16
ROW = OWN * GROUPS
PLANE = ROW * ROWS
HD, LOCAL = 128, 3
WIDE = HD * LOCAL
PATCH = 64
NUM = PATCH * LOCAL
MSG = 256
CH, OUTCH = 384, 192
EDGE = 8
LINE = 48
TO_LOG2 = math.log2(math.e) / math.sqrt(HD)


def dot(a, b, dims):
    return lax.dot_general(a, b, (dims, ((), ())), preferred_element_type=F32)


def kernel(
    q_in, k_in, v_in, base_far, proj_far, std_far, mean_far, w_in_far, b_in_far, gain_far, w_up_far,
    out_ref,
    keys, values, v_row, queries, top, total, fade, weighted, summed, turned, sending, parts, lat_own, lat_near,
    base_ref, proj_ref, std_ref, mean_ref, w_in, b_in_ref, gain_ref, w_up, w_two, enlarged, columns,
    plane_send, plane_recv, ring_send, ring_recv, part_send, part_recv, near_send, near_recv, weight_sem,
):
    s, g = lax.axis_index("seq"), lax.axis_index("head")
    z, row = s // ROWS, s % ROWS
    place = row * GROUPS + g
    up, down = ((s + ROWS) % SEQ, g), ((s + SEQ - ROWS) % SEQ, g)
    after, before = (s + 1) % SEQ, (s + SEQ - 1) % SEQ
    next_g, last_g = (g + 1) % GROUPS, (g + GROUPS - 1) % GROUPS

    def peer(i):
        other = (place + i) % PLACES
        return other, (z * ROWS + other // GROUPS, other % GROUPS)

    def columns_of(group):
        return pl.ds(pl.multiple_of(group * WIDE, WIDE), WIDE)

    def tokens_of(index):
        return pl.ds(pl.multiple_of(index * OWN, OWN), OWN)

    barrier = pltpu.get_barrier_semaphore()

    for i in range(1, PLACES):
        pl.semaphore_signal(barrier, inc=1, device_id=peer(i)[1], device_id_type=MESH)
    for other in (up, down, (after, g), (before, g), (after, last_g), (before, last_g)):
        pl.semaphore_signal(barrier, inc=1, device_id=other, device_id_type=MESH)

    rows_of = ((k_in, keys.at[0]), (v_in, v_row))
    for kind, (source, target) in enumerate(rows_of):
        pltpu.make_async_copy(source.at[:, columns_of(g)], target.at[tokens_of(g)], plane_recv.at[kind]).start()
    pltpu.make_async_copy(q_in.at[:, columns_of(g)], queries.at[tokens_of(place)], plane_recv.at[2]).start()
    pl.semaphore_wait(barrier, PLACES - 1 + 6)

    for kind, (source, target) in enumerate(rows_of):
        for i in range(1, GROUPS):
            other = (g + i) % GROUPS
            pltpu.make_async_remote_copy(
                src_ref=source.at[:, columns_of(other)],
                dst_ref=target.at[tokens_of(g)],
                send_sem=plane_send.at[kind],
                recv_sem=plane_recv.at[kind],
                device_id=(s, other),
                device_id_type=MESH,
            ).start()

    rings = (keys, values)

    def portion(kind, slot, part):
        half = rings[kind].shape[1] // 2
        return rings[kind].at[slot, pl.ds(part * half, half)]

    def hop(kind, source, target, way, part):
        pltpu.make_async_remote_copy(
            src_ref=portion(kind, source, part),
            dst_ref=portion(kind, target, part),
            send_sem=ring_send.at[way],
            recv_sem=ring_recv.at[kind, target, part],
            device_id=(up, down)[way],
            device_id_type=MESH,
        ).start()

    def arrived(kind, slot, part):
        pltpu.make_async_copy(
            portion(kind, slot, part), portion(kind, slot, part), ring_recv.at[kind, slot, part]
        ).wait()

    for kind, (source, target) in enumerate(rows_of):
        pltpu.make_async_copy(target, target, plane_recv.at[kind]).wait()
        if kind == 1:
            values[0] = v_row[...].T
        for part in range(2):
            hop(kind, 0, 1, 0, part)
            hop(kind, 0, 9, 1, part)

    for i in range(1, PLACES):
        device = peer(i)[1]
        pltpu.make_async_remote_copy(
            src_ref=q_in.at[:, columns_of(device[1])],
            dst_ref=queries.at[tokens_of(place)],
            send_sem=plane_send.at[2],
            recv_sem=plane_recv.at[2],
            device_id=device,
            device_id_type=MESH,
        ).start()

    parameters = [
        pltpu.make_async_copy(source, target, weight_sem.at[i])
        for i, (source, target) in enumerate(
            (
                (w_in_far, w_in),
                (w_up_far, w_up),
                (base_far, base_ref),
                (proj_far, proj_ref),
                (std_far, std_ref),
                (mean_far, mean_ref),
                (b_in_far, b_in_ref),
                (gain_far, gain_ref),
            )
        )
    ]
    for copy in parameters:
        copy.start()

    for copy in parameters:
        copy.wait()
    w_two[...] = jnp.zeros_like(w_two)
    for t in range(3):
        for u in range(3):
            piece = w_in[(t * 3 + u) * 48 : (t * 3 + u) * 48 + 48, :]
            for half in range(2):
                at = t * 256 + (u + half) * 64
                w_two[at : at + 48, half * CH : half * CH + CH] = piece
    enlarged[...] = jnp.zeros_like(enlarged)
    turned[...] = jnp.zeros_like(turned)

    def joined(pieces, axis):
        return pieces[0] if len(pieces) == 1 else jnp.concatenate(pieces, axis=axis)

    units = [
        (h, slice(h * HD, h * HD + HD), slice(c * 256, c * 256 + 256)) for h in range(LOCAL) for c in range(2)
    ]

    def weigh(slots, chosen, first=False):
        for h, lanes, some in chosen:
            some_keys = joined([keys[slot, :, lanes] for slot in slots], 0)
            scores = dot(some_keys, queries[some, lanes], ((1,), (1,)))
            new = jnp.max(scores, axis=0, keepdims=True)
            if not first:
                old = top[h : h + 1, some]
                new = jnp.maximum(old, new)
                fading = jnp.exp2((old - new) * TO_LOG2)
                fade[h : h + 1, some] = fading
            weights = jnp.exp2((scores - new) * TO_LOG2)
            sums = jnp.sum(weights, axis=0, keepdims=True)
            total[h : h + 1, some] = sums if first else total[h : h + 1, some] * fading + sums
            top[h : h + 1, some] = new
            weighted[h, : len(slots) * ROW, some] = weights.astype(BF16)

    def add_up(slots, chosen, first=False):
        for h, lanes, some in chosen:
            some_values = joined([values[slot, lanes, :] for slot in slots], 1)
            product = dot(some_values, weighted[h, : len(slots) * ROW, some], ((1,), (0,)))
            summed[lanes, some] = product if first else summed[lanes, some] * fade[h : h + 1, some] + product

    some, rest = units[:3], units[3:]

    def pass_on(kind, t, part):
        arrived(kind, t, part)
        hop(kind, t, t + 1, 0, part)
        arrived(kind, t + 8, part)
        hop(kind, t + 8, t + 9, 1, part)

    pass_on(0, 1, 0)
    pass_on(0, 1, 1)
    pltpu.make_async_copy(queries, queries, plane_recv.at[2]).wait()
    weigh([0], units, first=True)
    pass_on(1, 1, 0)
    add_up([0], units, first=True)
    pass_on(1, 1, 1)
    weigh([1, 9], units)

    def step(t, carry):
        pass_on(0, t, 0)
        add_up([t - 1, t + 7], some)
        pass_on(0, t, 1)
        add_up([t - 1, t + 7], rest)
        pass_on(1, t, 0)
        weigh([t, t + 8], some)
        pass_on(1, t, 1)
        weigh([t, t + 8], rest)
        return carry

    lax.fori_loop(2, 7, step, 0)
    for part, chosen in ((0, some), (1, rest)):
        arrived(0, 7, part)
        hop(0, 7, 8, 0, part)
        arrived(0, 15, part)
        add_up([6, 14], chosen)
    for part, chosen in ((0, some), (1, rest)):
        arrived(1, 15, part)
        hop(1, 15, 8, 1, part)
        arrived(1, 7, part)
        weigh([7, 15], chosen)
    add_up([7, 15], units)
    for part in range(2):
        arrived(0, 8, part)
    weigh([8], units)
    for part in range(2):
        arrived(1, 8, part)
    add_up([8], units)

    for h in range(LOCAL):
        lanes = slice(h * HD, h * HD + HD)
        sums = total[h : h + 1, :]
        attended = (summed[lanes, :] * (1.0 / sums)).astype(BF16)
        turned[h * PATCH : h * PATCH + PATCH, :] = dot(proj_ref[:, lanes], attended, ((1,), (0,)))
        level = top[h : h + 1, :] * TO_LOG2 + jnp.log(sums) * math.log2(math.e)
        for term in range(3):
            rounded = level.astype(BF16).astype(F32)
            turned[NUM + term * LOCAL + h : NUM + term * LOCAL + h + 1, :] = rounded
            level = level - rounded
    for away in (1, 2, 3, 0):
        to_row = (row + away) % ROWS
        lanes = pl.ds(pl.multiple_of(to_row * ROW, ROW), ROW)
        sending[lanes, :] = turned[:, lanes].astype(BF16).T
        if away == 0:
            pltpu.make_async_copy(sending.at[tokens_of(place)], parts.at[tokens_of(place)], part_recv).start()
        for i in range(0 if away else 1, GROUPS):
            to_group = (g + i) % GROUPS
            pltpu.make_async_remote_copy(
                src_ref=sending.at[tokens_of(to_row * GROUPS + to_group)],
                dst_ref=parts.at[tokens_of(place)],
                send_sem=part_send,
                recv_sem=part_recv,
                device_id=(z * ROWS + to_row, to_group),
                device_id_type=MESH,
            ).start()

    def ones_where(shape, made):
        r = lax.broadcasted_iota(jnp.int32, shape, 0)
        c = lax.broadcasted_iota(jnp.int32, shape, 1)
        return made(r, c).astype(F32).astype(BF16)

    spread = ones_where(
        (MSG, NUM),
        lambda r, c: (r >= NUM) & (r < NUM + 3 * LOCAL) & ((r - NUM) % LOCAL == c // PATCH),
    )
    pltpu.make_async_copy(parts, parts, part_recv).wait()

    levels = dot(parts[...], spread, ((1,), (0,)))
    numbers = parts[:, :NUM].astype(F32)
    by_row = [slice(r * ROW, r * ROW + ROW) for r in range(ROWS)]
    highest = levels[by_row[0]]
    for r in range(1, ROWS):
        highest = jnp.maximum(highest, levels[by_row[r]])
    above, below = 0.0, 0.0
    for r in range(ROWS):
        share = jnp.exp2(levels[by_row[r]] - highest)
        above = above + share * numbers[by_row[r]]
        below = below + share
    merged = above / below
    tokens = merged[:OWN]
    for other in range(1, GROUPS):
        tokens = tokens + merged[other * OWN : other * OWN + OWN]
    patch = base_ref[...].astype(F32)
    for h in range(LOCAL):
        patch = patch + tokens[:, h * PATCH : h * PATCH + PATCH]
    std = jnp.concatenate([std_ref[...]] * 4, axis=1)
    mean = jnp.concatenate([mean_ref[...]] * 4, axis=1)
    latent = patch * std + mean
    lat_own[...] = jnp.concatenate([latent, latent], axis=1).astype(BF16)

    for slot, device in enumerate(((after, next_g), (after, g), (s, next_g), (before, next_g), (before, g))):
        pltpu.make_async_remote_copy(
            src_ref=lat_own,
            dst_ref=lat_near.at[slot],
            send_sem=near_send,
            recv_sem=near_recv,
            device_id=device,
            device_id_type=MESH,
        ).start()

    def picks(b):
        def made(r, c):
            a, v, low = c // 64, (c // 16) % 4, c % 16
            spot = v + 1 - b
            wanted = (spot // 2) * 64 + a * 32 + (spot % 2) * 16 + low
            return (v < 3) & (r == wanted)

        return ones_where((128, 128), made)

    pick = [picks(0), picks(1)]
    pltpu.make_async_copy(lat_near, lat_near, near_recv).wait()

    has_before = (s > 0).astype(F32)
    has_after = (s < SEQ - 1).astype(F32)
    has_frames = (g > 0).astype(F32)
    tiles = [
        [lat_near[0].astype(F32) * (has_before * has_frames), lat_near[1].astype(F32) * has_before],
        [lat_near[2].astype(F32) * has_frames, lat_own[...].astype(F32)],
        [lat_near[3].astype(F32) * (has_after * has_frames), lat_near[4].astype(F32) * has_after],
    ]
    lane = lax.broadcasted_iota(jnp.int32, (8, 128), 1)
    line = lax.broadcasted_iota(jnp.int32, (8, 128), 0)
    sides = ([], [])
    for f in range(4):
        for r in range(3):
            here = tiles[r][f // 2][(f % 2) * 8 : (f % 2) * 8 + 8]
            left = jnp.where(line == 0, 0.0, pltpu.roll(here, 1, 0))
            right = jnp.where(line == 7, 0.0, pltpu.roll(here, 7, 0))
            sides[0].append(jnp.where(lane < 64, left, here))
            sides[1].append(jnp.where(lane < 64, here, right))
    windows = [
        dot(jnp.concatenate(side, axis=0).astype(BF16), chosen, ((1,), (0,))) for side, chosen in zip(sides, pick)
    ]

    def window(f, r, b):
        at = (f * 3 + r) * 8
        return windows[b][at : at + 8]

    lines = []
    for f in range(2):
        for pair in range(2):
            for b in range(2):
                pieces = [window(f + t, pair + r, b) for t in range(3) for r in range(2)]
                lines.append(jnp.concatenate(pieces, axis=1))
    conv = dot(jnp.concatenate(lines, axis=0).astype(BF16), w_two[...], ((1,), (0,)))
    for half in range(2):
        out = conv[:, half * CH : half * CH + CH] + b_in_ref[...].reshape(1, CH)
        mean_sq = jnp.mean(out * out, axis=1, keepdims=True)
        normed = out * lax.rsqrt(mean_sq + 1e-6) * gain_ref[...].reshape(1, CH)
        active = normed / (1.0 + jnp.exp(-normed))
        for f in range(2):
            for pair in range(2):
                y = 2 * pair + half
                for b in range(2):
                    at = ((f * 2 + pair) * 2 + b) * 8
                    part = active[at : at + 8]
                    if y == 0:
                        part = part * has_before
                    if y == 3:
                        part = part * has_after
                    for twice in range(2):
                        for tile in range(3):
                            enlarged[tile, f * 4 + y, pl.ds(EDGE + 2 * b + twice, 8, stride=4), :] = part[
                                :, tile * 128 : tile * 128 + 128
                            ]

    for v in range(3):
        for f in range(2):
            for y in range(4):
                piece = [enlarged[tile, f * 4 + y, EDGE - 1 + v : EDGE + 31 + v, :] for tile in range(3)]
                piece = jnp.concatenate(piece, axis=1).astype(BF16)
                for line_out in range(4):
                    for u in range(3):
                        if (line_out + u + 1) // 2 == y:
                            at = (f * 4 + line_out) * 32
                            to = (u * 3 + v) * CH
                            columns[at : at + 32, to : to + CH] = piece
    planes = 0.0
    for tap in range(9):
        planes = planes + dot(
            columns[:, tap * CH : tap * CH + CH], w_up[tap * OUTCH : tap * OUTCH + OUTCH, :], ((1,), (1,))
        )
    out_ref[...] = planes

    for kind in (0, 1):
        sent = v_row.at[: ROW - OWN]
        pltpu.make_async_copy(sent, sent, plane_send.at[kind]).wait()
    sent = queries.at[: PLANE - OWN]
    pltpu.make_async_copy(sent, sent, plane_send.at[2]).wait()
    for way in (0, 1):
        sent = keys.at[:15]
        pltpu.make_async_copy(sent, sent, ring_send.at[way]).wait()
    sent = parts.at[: PLANE - OWN]
    pltpu.make_async_copy(sent, sent, part_send).wait()
    pltpu.make_async_copy(lat_near, lat_near, near_send).wait()


def on_device(
    query_states,
    key_states,
    value_states,
    base_patch,
    head_proj,
    latent_std,
    latent_mean,
    w_in,
    b_in,
    gain_mid,
    w_up,
    b_up,
):
    here = pl.BlockSpec(memory_space=pltpu.VMEM)
    far = pl.BlockSpec(memory_space=pltpu.HBM)
    DMA = pltpu.SemaphoreType.DMA
    planes = pl.pallas_call(
        kernel,
        out_shape=jax.ShapeDtypeStruct((256, OUTCH), F32),
        in_specs=[far] * 11,
        out_specs=here,
        scratch_shapes=[
            pltpu.VMEM((16, ROW, WIDE), BF16),
            pltpu.VMEM((16, WIDE, ROW), BF16),
            pltpu.VMEM((ROW, WIDE), BF16),
            pltpu.VMEM((PLANE, WIDE), BF16),
            pltpu.VMEM((8, PLANE), F32),
            pltpu.VMEM((8, PLANE), F32),
            pltpu.VMEM((8, PLANE), F32),
            pltpu.VMEM((LOCAL, 2 * ROW, PLANE), BF16),
            pltpu.VMEM((WIDE, PLANE), F32),
            pltpu.VMEM((MSG, PLANE), F32),
            pltpu.VMEM((PLANE, MSG), BF16),
            pltpu.VMEM((PLANE, MSG), BF16),
            pltpu.VMEM((OWN, 128), BF16),
            pltpu.VMEM((5, OWN, 128), BF16),
            pltpu.VMEM((OWN, PATCH), BF16),
            pltpu.VMEM((PATCH, WIDE), BF16),
            pltpu.VMEM((1, 16), F32),
            pltpu.VMEM((1, 16), F32),
            pltpu.VMEM((27 * 16, CH), BF16),
            pltpu.VMEM((CH,), F32),
            pltpu.VMEM((CH,), F32),
            pltpu.VMEM((9 * OUTCH, CH), BF16),
            pltpu.VMEM((768, 2 * CH), BF16),
            pltpu.VMEM((3, 8, LINE, 128), F32),
            pltpu.VMEM((256, 9 * CH), BF16),
            DMA((3,)),
            DMA((3,)),
            DMA((2,)),
            DMA((2, 16, 2)),
            DMA,
            DMA,
            DMA,
            DMA,
            DMA((8,)),
        ],
        compiler_params=pltpu.CompilerParams(
            collective_id=0, has_side_effects=True, vmem_limit_bytes=60 * 1024 * 1024
        ),
        name="attend_and_decode",
    )(
        query_states,
        key_states,
        value_states,
        base_patch,
        head_proj.T,
        latent_std.reshape(1, 16),
        latent_mean.reshape(1, 16),
        w_in.reshape(27 * 16, CH),
        b_in,
        gain_mid,
        w_up.transpose(0, 1, 3, 2).reshape(9 * OUTCH, CH),
    )
    return (planes.reshape(2, 4, 32, OUTCH) + b_up).astype(BF16)


def solution(mesh):
    in_specs = (
        P(("seq", "head"), None),
        P(("seq", "head"), None),
        P(("seq", "head"), None),
        P(("seq", "head"), None),
        P("head", None),
        P(),
        P(),
        P(),
        P(),
        P(),
        P(),
        P(),
    )
    out_specs = P("head", "seq", None, None)
    return jax.shard_map(
        on_device, mesh=mesh, in_specs=in_specs, out_specs=out_specs, check_vma=False
    )
```

```python
import math

import jax
import jax.numpy as jnp
from jax import lax
from jax.experimental import pallas as pl
from jax.experimental.pallas import tpu as pltpu
from jax.sharding import PartitionSpec as P

MESH = pl.DeviceIdType.MESH
F32, BF16 = jnp.float32, jnp.bfloat16

SEQ, GROUPS = 64, 8
ROWS = 4
PLACES = ROWS * GROUPS
OWN = 16
ROW = OWN * GROUPS
PLANE = ROW * ROWS
HD, LOCAL = 128, 3
WIDE = HD * LOCAL
PATCH = 64
NUM = PATCH * LOCAL
MSG = 256
CH, OUTCH = 384, 192
EDGE = 8
LINE = 48
TO_LOG2 = math.log2(math.e) / math.sqrt(HD)


def dot(a, b, dims):
    return lax.dot_general(a, b, (dims, ((), ())), preferred_element_type=F32)


def kernel(
    q_in, k_in, v_in, base_far, proj_far, std_far, mean_far, w_in_far, b_in_far, gain_far, w_up_far, b_up_far,
    out_ref,
    keys, values, v_row, queries, top, total, fade, weighted, summed, turned, sending, parts, lat_own, lat_near,
    base_ref, proj_ref, std_ref, mean_ref, w_in, b_in_ref, gain_ref, w_up, b_up_ref, w_two, enlarged, columns,
    plane_send, plane_recv, ring_send, ring_recv, part_send, part_recv, near_send, near_recv, weight_sem,
):
    s, g = lax.axis_index("seq"), lax.axis_index("head")
    z, row = s // ROWS, s % ROWS
    place = row * GROUPS + g
    up, down = ((s + ROWS) % SEQ, g), ((s + SEQ - ROWS) % SEQ, g)
    after, before = (s + 1) % SEQ, (s + SEQ - 1) % SEQ
    next_g, last_g = (g + 1) % GROUPS, (g + GROUPS - 1) % GROUPS

    def peer(i):
        other = (place + i) % PLACES
        return other, (z * ROWS + other // GROUPS, other % GROUPS)

    def columns_of(group):
        return pl.ds(pl.multiple_of(group * WIDE, WIDE), WIDE)

    def tokens_of(index):
        return pl.ds(pl.multiple_of(index * OWN, OWN), OWN)

    barrier = pltpu.get_barrier_semaphore()

    for i in range(1, PLACES):
        pl.semaphore_signal(barrier, inc=1, device_id=peer(i)[1], device_id_type=MESH)
    for other in (up, down, (after, g), (before, g), (after, last_g), (before, last_g)):
        pl.semaphore_signal(barrier, inc=1, device_id=other, device_id_type=MESH)

    rows_of = ((k_in, keys.at[0]), (v_in, v_row))
    for kind, (source, target) in enumerate(rows_of):
        pltpu.make_async_copy(source.at[:, columns_of(g)], target.at[tokens_of(g)], plane_recv.at[kind]).start()
    pltpu.make_async_copy(q_in.at[:, columns_of(g)], queries.at[tokens_of(place)], plane_recv.at[2]).start()
    proj_in = pltpu.make_async_copy(proj_far, proj_ref, weight_sem.at[8])
    proj_in.start()
    pl.semaphore_wait(barrier, PLACES - 1 + 6)

    for kind, (source, target) in enumerate(rows_of):
        for i in range(1, GROUPS):
            other = (g + i) % GROUPS
            pltpu.make_async_remote_copy(
                src_ref=source.at[:, columns_of(other)],
                dst_ref=target.at[tokens_of(g)],
                send_sem=plane_send.at[kind],
                recv_sem=plane_recv.at[kind],
                device_id=(s, other),
                device_id_type=MESH,
            ).start()

    def portion(kind, slot, part):
        return values.at[slot] if kind else keys.at[slot, pl.ds(part * ROW // 2, ROW // 2)]

    def hop(kind, source, target, way, part):
        pltpu.make_async_remote_copy(
            src_ref=portion(kind, source, part),
            dst_ref=portion(kind, target, part),
            send_sem=ring_send.at[way, kind],
            recv_sem=ring_recv.at[kind, target, part],
            device_id=(up, down)[way],
            device_id_type=MESH,
        ).start()

    def arrived(kind, slot, part):
        pltpu.make_async_copy(
            portion(kind, slot, part), portion(kind, slot, part), ring_recv.at[kind, slot, part]
        ).wait()

    for kind, (source, target) in enumerate(rows_of):
        pltpu.make_async_copy(target, target, plane_recv.at[kind]).wait()
        if kind == 1:
            proj_in.wait()
            for h in range(LOCAL):
                lanes = slice(h * HD, h * HD + HD)
                values[0, h * PATCH : h * PATCH + PATCH, :] = dot(
                    proj_ref[:, lanes], v_row[:, lanes], ((1,), (1,))
                ).astype(BF16)
        for part in range(2 - kind):
            hop(kind, 0, 1, 0, part)
            hop(kind, 0, 9, 1, part)

    for i in range(1, PLACES):
        device = peer(i)[1]
        pltpu.make_async_remote_copy(
            src_ref=q_in.at[:, columns_of(device[1])],
            dst_ref=queries.at[tokens_of(place)],
            send_sem=plane_send.at[2],
            recv_sem=plane_recv.at[2],
            device_id=device,
            device_id_type=MESH,
        ).start()

    parameters = [
        pltpu.make_async_copy(source, target, weight_sem.at[i])
        for i, (source, target) in enumerate(
            (
                (w_in_far, w_in),
                (w_up_far, w_up),
                (base_far, base_ref),
                (std_far, std_ref),
                (mean_far, mean_ref),
                (b_in_far, b_in_ref),
                (gain_far, gain_ref),
                (b_up_far, b_up_ref),
            )
        )
    ]
    for copy in parameters:
        copy.start()

    for copy in parameters:
        copy.wait()
    w_two[...] = jnp.zeros_like(w_two)
    for t in range(3):
        for u in range(3):
            piece = w_in[(t * 3 + u) * 48 : (t * 3 + u) * 48 + 48, :]
            for half in range(2):
                at = t * 256 + (u + half) * 64
                w_two[at : at + 48, half * CH : half * CH + CH] = piece
    enlarged[...] = jnp.zeros_like(enlarged)
    turned[...] = jnp.zeros_like(turned)

    def joined(pieces, axis):
        return pieces[0] if len(pieces) == 1 else jnp.concatenate(pieces, axis=axis)

    units = [
        (h, slice(h * HD, h * HD + HD), slice(c * 256, c * 256 + 256)) for h in range(LOCAL) for c in range(2)
    ]

    def weigh(slots, chosen, first=False):
        for h, lanes, some in chosen:
            some_keys = joined([keys[slot, :, lanes] for slot in slots], 0)
            scores = dot(some_keys, queries[some, lanes], ((1,), (1,)))
            new = jnp.max(scores, axis=0, keepdims=True)
            if not first:
                old = top[h : h + 1, some]
                new = jnp.maximum(old, new)
                fading = jnp.exp2((old - new) * TO_LOG2)
                fade[h : h + 1, some] = fading
            weights = jnp.exp2((scores - new) * TO_LOG2)
            sums = jnp.sum(weights, axis=0, keepdims=True)
            total[h : h + 1, some] = sums if first else total[h : h + 1, some] * fading + sums
            top[h : h + 1, some] = new
            weighted[h, : len(slots) * ROW, some] = weights.astype(BF16)

    def add_up(slots, chosen, first=False):
        for h, lanes, some in chosen:
            rows = slice(h * PATCH, h * PATCH + PATCH)
            some_values = joined([values[slot, rows, :] for slot in slots], 1)
            product = dot(some_values, weighted[h, : len(slots) * ROW, some], ((1,), (0,)))
            summed[rows, some] = product if first else summed[rows, some] * fade[h : h + 1, some] + product

    some, rest = units[:3], units[3:]

    def pass_on(kind, t, part):
        arrived(kind, t, part)
        hop(kind, t, t + 1, 0, part)
        arrived(kind, t + 8, part)
        hop(kind, t + 8, t + 9, 1, part)

    pass_on(0, 1, 0)
    pass_on(0, 1, 1)
    pltpu.make_async_copy(queries, queries, plane_recv.at[2]).wait()
    weigh([0], units, first=True)
    pass_on(1, 1, 0)
    add_up([0], units, first=True)
    weigh([1, 9], units)

    def step(t, carry):
        pass_on(0, t, 0)
        add_up([t - 1, t + 7], units)
        pass_on(0, t, 1)
        weigh([t, t + 8], some)
        pass_on(1, t, 0)
        weigh([t, t + 8], rest)
        return carry

    lax.fori_loop(2, 7, step, 0)
    for part in range(2):
        arrived(0, 7, part)
        hop(0, 7, 8, 0, part)
        arrived(0, 15, part)
        if part == 0:
            add_up([6, 14], units)
    weigh([7, 15], some)
    arrived(1, 15, 0)
    hop(1, 15, 8, 1, 0)
    arrived(1, 7, 0)
    weigh([7, 15], rest)
    add_up([7, 15], units)
    for part in range(2):
        arrived(0, 8, part)
    weigh([8], units)
    arrived(1, 8, 0)
    add_up([8], units)

    for h in range(LOCAL):
        sums = total[h : h + 1, :]
        rows = slice(h * PATCH, h * PATCH + PATCH)
        turned[rows, :] = summed[rows, :] * (1.0 / sums)
        level = top[h : h + 1, :] * TO_LOG2 + jnp.log(sums) * math.log2(math.e)
        for term in range(3):
            rounded = level.astype(BF16).astype(F32)
            turned[NUM + term * LOCAL + h : NUM + term * LOCAL + h + 1, :] = rounded
            level = level - rounded
    for away in (1, 2, 3, 0):
        to_row = (row + away) % ROWS
        lanes = pl.ds(pl.multiple_of(to_row * ROW, ROW), ROW)
        sending[lanes, :] = turned[:, lanes].astype(BF16).T
        if away == 0:
            pltpu.make_async_copy(sending.at[tokens_of(place)], parts.at[tokens_of(place)], part_recv).start()
        for i in range(0 if away else 1, GROUPS):
            to_group = (g + i) % GROUPS
            pltpu.make_async_remote_copy(
                src_ref=sending.at[tokens_of(to_row * GROUPS + to_group)],
                dst_ref=parts.at[tokens_of(place)],
                send_sem=part_send,
                recv_sem=part_recv,
                device_id=(z * ROWS + to_row, to_group),
                device_id_type=MESH,
            ).start()

    def ones_where(shape, made):
        r = lax.broadcasted_iota(jnp.int32, shape, 0)
        c = lax.broadcasted_iota(jnp.int32, shape, 1)
        return made(r, c).astype(F32).astype(BF16)

    spread = ones_where(
        (MSG, NUM),
        lambda r, c: (r >= NUM) & (r < NUM + 3 * LOCAL) & ((r - NUM) % LOCAL == c // PATCH),
    )
    pltpu.make_async_copy(parts, parts, part_recv).wait()

    levels = dot(parts[...], spread, ((1,), (0,)))
    numbers = parts[:, :NUM].astype(F32)
    by_row = [slice(r * ROW, r * ROW + ROW) for r in range(ROWS)]
    highest = levels[by_row[0]]
    for r in range(1, ROWS):
        highest = jnp.maximum(highest, levels[by_row[r]])
    above, below = 0.0, 0.0
    for r in range(ROWS):
        share = jnp.exp2(levels[by_row[r]] - highest)
        above = above + share * numbers[by_row[r]]
        below = below + share
    merged = above / below
    tokens = merged[:OWN]
    for other in range(1, GROUPS):
        tokens = tokens + merged[other * OWN : other * OWN + OWN]
    patch = base_ref[...].astype(F32)
    for h in range(LOCAL):
        patch = patch + tokens[:, h * PATCH : h * PATCH + PATCH]
    std = jnp.concatenate([std_ref[...]] * 4, axis=1)
    mean = jnp.concatenate([mean_ref[...]] * 4, axis=1)
    latent = patch * std + mean
    lat_own[...] = jnp.concatenate([latent, latent], axis=1).astype(BF16)

    for slot, device in enumerate(((after, next_g), (after, g), (s, next_g), (before, next_g), (before, g))):
        pltpu.make_async_remote_copy(
            src_ref=lat_own,
            dst_ref=lat_near.at[slot],
            send_sem=near_send,
            recv_sem=near_recv,
            device_id=device,
            device_id_type=MESH,
        ).start()

    def picks(b):
        def made(r, c):
            a, v, low = c // 64, (c // 16) % 4, c % 16
            spot = v + 1 - b
            wanted = (spot // 2) * 64 + a * 32 + (spot % 2) * 16 + low
            return (v < 3) & (r == wanted)

        return ones_where((128, 128), made)

    pick = [picks(0), picks(1)]
    pltpu.make_async_copy(lat_near, lat_near, near_recv).wait()

    has_before = (s > 0).astype(F32)
    has_after = (s < SEQ - 1).astype(F32)
    has_frames = (g > 0).astype(F32)
    tiles = [
        [lat_near[0].astype(F32) * (has_before * has_frames), lat_near[1].astype(F32) * has_before],
        [lat_near[2].astype(F32) * has_frames, lat_own[...].astype(F32)],
        [lat_near[3].astype(F32) * (has_after * has_frames), lat_near[4].astype(F32) * has_after],
    ]
    lane = lax.broadcasted_iota(jnp.int32, (8, 128), 1)
    line = lax.broadcasted_iota(jnp.int32, (8, 128), 0)
    sides = ([], [])
    for f in range(4):
        for r in range(3):
            here = tiles[r][f // 2][(f % 2) * 8 : (f % 2) * 8 + 8]
            left = jnp.where(line == 0, 0.0, pltpu.roll(here, 1, 0))
            right = jnp.where(line == 7, 0.0, pltpu.roll(here, 7, 0))
            sides[0].append(jnp.where(lane < 64, left, here))
            sides[1].append(jnp.where(lane < 64, here, right))
    windows = [
        dot(jnp.concatenate(side, axis=0).astype(BF16), chosen, ((1,), (0,))) for side, chosen in zip(sides, pick)
    ]

    def window(f, r, b):
        at = (f * 3 + r) * 8
        return windows[b][at : at + 8]

    lines = []
    for f in range(2):
        for pair in range(2):
            for b in range(2):
                pieces = [window(f + t, pair + r, b) for t in range(3) for r in range(2)]
                lines.append(jnp.concatenate(pieces, axis=1))
    conv = dot(jnp.concatenate(lines, axis=0).astype(BF16), w_two[...], ((1,), (0,)))
    for half in range(2):
        out = conv[:, half * CH : half * CH + CH] + b_in_ref[...].reshape(1, CH)
        mean_sq = jnp.mean(out * out, axis=1, keepdims=True)
        normed = out * lax.rsqrt(mean_sq + 1e-6) * gain_ref[...].reshape(1, CH)
        active = normed / (1.0 + jnp.exp(-normed))
        for f in range(2):
            for pair in range(2):
                y = 2 * pair + half
                for b in range(2):
                    at = ((f * 2 + pair) * 2 + b) * 8
                    part = active[at : at + 8]
                    if y == 0:
                        part = part * has_before
                    if y == 3:
                        part = part * has_after
                    for twice in range(2):
                        for tile in range(3):
                            enlarged[tile, f * 4 + y, pl.ds(EDGE + 2 * b + twice, 8, stride=4), :] = part[
                                :, tile * 128 : tile * 128 + 128
                            ]

    for v in range(3):
        for f in range(2):
            for y in range(4):
                piece = [enlarged[tile, f * 4 + y, EDGE - 1 + v : EDGE + 31 + v, :] for tile in range(3)]
                piece = jnp.concatenate(piece, axis=1).astype(BF16)
                for line_out in range(4):
                    for u in range(3):
                        if (line_out + u + 1) // 2 == y:
                            at = (f * 4 + line_out) * 32
                            to = (u * 3 + v) * CH
                            columns[at : at + 32, to : to + CH] = piece
    planes = b_up_ref[...]
    for tap in range(9):
        planes = planes + dot(
            columns[:, tap * CH : tap * CH + CH], w_up[tap * OUTCH : tap * OUTCH + OUTCH, :], ((1,), (1,))
        )
    out_ref[...] = planes.astype(BF16)

    for kind in (0, 1):
        sent = v_row.at[: ROW - OWN]
        pltpu.make_async_copy(sent, sent, plane_send.at[kind]).wait()
    sent = queries.at[: PLANE - OWN]
    pltpu.make_async_copy(sent, sent, plane_send.at[2]).wait()
    for way, kind, ring, count in ((0, 0, keys, 8), (0, 1, values, 7), (1, 0, keys, 7), (1, 1, values, 8)):
        sent = ring.at[:count]
        pltpu.make_async_copy(sent, sent, ring_send.at[way, kind]).wait()
    sent = parts.at[: PLANE - OWN]
    pltpu.make_async_copy(sent, sent, part_send).wait()
    pltpu.make_async_copy(lat_near, lat_near, near_send).wait()


def on_device(
    query_states,
    key_states,
    value_states,
    base_patch,
    head_proj,
    latent_std,
    latent_mean,
    w_in,
    b_in,
    gain_mid,
    w_up,
    b_up,
):
    here = pl.BlockSpec(memory_space=pltpu.VMEM)
    far = pl.BlockSpec(memory_space=pltpu.HBM)
    DMA = pltpu.SemaphoreType.DMA
    planes = pl.pallas_call(
        kernel,
        out_shape=jax.ShapeDtypeStruct((256, OUTCH), BF16),
        in_specs=[far] * 12,
        out_specs=here,
        scratch_shapes=[
            pltpu.VMEM((16, ROW, WIDE), BF16),
            pltpu.VMEM((16, NUM, ROW), BF16),
            pltpu.VMEM((ROW, WIDE), BF16),
            pltpu.VMEM((PLANE, WIDE), BF16),
            pltpu.VMEM((8, PLANE), F32),
            pltpu.VMEM((8, PLANE), F32),
            pltpu.VMEM((8, PLANE), F32),
            pltpu.VMEM((LOCAL, 2 * ROW, PLANE), BF16),
            pltpu.VMEM((NUM, PLANE), F32),
            pltpu.VMEM((MSG, PLANE), F32),
            pltpu.VMEM((PLANE, MSG), BF16),
            pltpu.VMEM((PLANE, MSG), BF16),
            pltpu.VMEM((OWN, 128), BF16),
            pltpu.VMEM((5, OWN, 128), BF16),
            pltpu.VMEM((OWN, PATCH), BF16),
            pltpu.VMEM((PATCH, WIDE), BF16),
            pltpu.VMEM((1, 16), F32),
            pltpu.VMEM((1, 16), F32),
            pltpu.VMEM((27 * 16, CH), BF16),
            pltpu.VMEM((CH,), F32),
            pltpu.VMEM((CH,), F32),
            pltpu.VMEM((9 * OUTCH, CH), BF16),
            pltpu.VMEM((1, OUTCH), F32),
            pltpu.VMEM((768, 2 * CH), BF16),
            pltpu.VMEM((3, 8, LINE, 128), F32),
            pltpu.VMEM((256, 9 * CH), BF16),
            DMA((3,)),
            DMA((3,)),
            DMA((2, 2)),
            DMA((2, 16, 2)),
            DMA,
            DMA,
            DMA,
            DMA,
            DMA((9,)),
        ],
        compiler_params=pltpu.CompilerParams(
            collective_id=0, has_side_effects=True, vmem_limit_bytes=60 * 1024 * 1024
        ),
        name="attend_and_decode",
    )(
        query_states,
        key_states,
        value_states,
        base_patch,
        head_proj.T,
        latent_std.reshape(1, 16),
        latent_mean.reshape(1, 16),
        w_in.reshape(27 * 16, CH),
        b_in,
        gain_mid,
        w_up.transpose(0, 1, 3, 2).reshape(9 * OUTCH, CH),
        b_up.reshape(1, OUTCH),
    )
    return planes.reshape(2, 4, 32, OUTCH)


def solution(mesh):
    in_specs = (
        P(("seq", "head"), None),
        P(("seq", "head"), None),
        P(("seq", "head"), None),
        P(("seq", "head"), None),
        P("head", None),
        P(),
        P(),
        P(),
        P(),
        P(),
        P(),
        P(),
    )
    out_specs = P("head", "seq", None, None)
    return jax.shard_map(
        on_device, mesh=mesh, in_specs=in_specs, out_specs=out_specs, check_vma=False
    )
```

```python
import math

import jax
import jax.numpy as jnp
from jax import lax
from jax.experimental import pallas as pl
from jax.experimental.pallas import tpu as pltpu
from jax.sharding import PartitionSpec as P

MESH = pl.DeviceIdType.MESH
F32, BF16 = jnp.float32, jnp.bfloat16

SEQ, GROUPS = 64, 8
ROWS = 4
PLACES = ROWS * GROUPS
OWN = 16
ROW = OWN * GROUPS
PLANE = ROW * ROWS
HD, LOCAL = 128, 3
WIDE = HD * LOCAL
PATCH = 64
NUM = PATCH * LOCAL
MSG = 256
CH, OUTCH = 384, 192
EDGE = 8
LINE = 48
TO_LOG2 = math.log2(math.e) / math.sqrt(HD)


def dot(a, b, dims):
    return lax.dot_general(a, b, (dims, ((), ())), preferred_element_type=F32)


def kernel(
    q_in, k_in, v_in, base_far, proj_far, std_far, mean_far, w_in_far, b_in_far, gain_far, w_up_far, b_up_far,
    out_ref,
    keys, values, v_row, queries, turned_queries, top, total, fade, weighted, summed, turned, sending, parts, lat_own, lat_near,
    base_ref, proj_ref, std_ref, mean_ref, w_in, b_in_ref, gain_ref, w_up, b_up_ref, w_two, enlarged, columns,
    plane_send, plane_recv, ring_send, ring_recv, part_send, part_recv, near_send, near_recv, weight_sem,
):
    s, g = lax.axis_index("seq"), lax.axis_index("head")
    z, row = s // ROWS, s % ROWS
    place = row * GROUPS + g
    up, down = ((s + ROWS) % SEQ, g), ((s + SEQ - ROWS) % SEQ, g)
    after, before = (s + 1) % SEQ, (s + SEQ - 1) % SEQ
    next_g, last_g = (g + 1) % GROUPS, (g + GROUPS - 1) % GROUPS

    def peer(i):
        other = (place + i) % PLACES
        return other, (z * ROWS + other // GROUPS, other % GROUPS)

    def columns_of(group):
        return pl.ds(pl.multiple_of(group * WIDE, WIDE), WIDE)

    def tokens_of(index):
        return pl.ds(pl.multiple_of(index * OWN, OWN), OWN)

    barrier = pltpu.get_barrier_semaphore()

    for i in range(1, PLACES):
        pl.semaphore_signal(barrier, inc=1, device_id=peer(i)[1], device_id_type=MESH)
    for other in (up, down, (after, g), (before, g), (after, last_g), (before, last_g)):
        pl.semaphore_signal(barrier, inc=1, device_id=other, device_id_type=MESH)

    rows_of = ((k_in, keys.at[0]), (v_in, v_row))
    for kind, (source, target) in enumerate(rows_of):
        pltpu.make_async_copy(source.at[:, columns_of(g)], target.at[tokens_of(g)], plane_recv.at[kind]).start()
    pltpu.make_async_copy(q_in.at[:, columns_of(g)], queries.at[tokens_of(place)], plane_recv.at[2]).start()
    proj_in = pltpu.make_async_copy(proj_far, proj_ref, weight_sem.at[8])
    proj_in.start()
    pl.semaphore_wait(barrier, PLACES - 1 + 6)

    for kind, (source, target) in enumerate(rows_of):
        for i in range(1, GROUPS):
            other = (g + i) % GROUPS
            pltpu.make_async_remote_copy(
                src_ref=source.at[:, columns_of(other)],
                dst_ref=target.at[tokens_of(g)],
                send_sem=plane_send.at[kind],
                recv_sem=plane_recv.at[kind],
                device_id=(s, other),
                device_id_type=MESH,
            ).start()

    def portion(kind, slot, part):
        return values.at[slot] if kind else keys.at[slot, pl.ds(part * ROW // 2, ROW // 2)]

    def hop(kind, source, target, way, part):
        pltpu.make_async_remote_copy(
            src_ref=portion(kind, source, part),
            dst_ref=portion(kind, target, part),
            send_sem=ring_send.at[way, kind],
            recv_sem=ring_recv.at[kind, target, part],
            device_id=(up, down)[way],
            device_id_type=MESH,
        ).start()

    def arrived(kind, slot, part):
        pltpu.make_async_copy(
            portion(kind, slot, part), portion(kind, slot, part), ring_recv.at[kind, slot, part]
        ).wait()

    for kind, (source, target) in enumerate(rows_of):
        pltpu.make_async_copy(target, target, plane_recv.at[kind]).wait()
        if kind == 1:
            proj_in.wait()
            for h in range(LOCAL):
                lanes = slice(h * HD, h * HD + HD)
                values[0, h * PATCH : h * PATCH + PATCH, :] = dot(
                    proj_ref[:, lanes], v_row[:, lanes], ((1,), (1,))
                ).astype(BF16)
        for part in range(2 - kind):
            hop(kind, 0, 1, 0, part)
            hop(kind, 0, 9, 1, part)

    for i in range(1, PLACES):
        device = peer(i)[1]
        pltpu.make_async_remote_copy(
            src_ref=q_in.at[:, columns_of(device[1])],
            dst_ref=queries.at[tokens_of(place)],
            send_sem=plane_send.at[2],
            recv_sem=plane_recv.at[2],
            device_id=device,
            device_id_type=MESH,
        ).start()

    parameters = [
        pltpu.make_async_copy(source, target, weight_sem.at[i])
        for i, (source, target) in enumerate(
            (
                (w_in_far, w_in),
                (w_up_far, w_up),
                (base_far, base_ref),
                (std_far, std_ref),
                (mean_far, mean_ref),
                (b_in_far, b_in_ref),
                (gain_far, gain_ref),
                (b_up_far, b_up_ref),
            )
        )
    ]
    for copy in parameters:
        copy.start()

    for copy in parameters:
        copy.wait()
    w_two[...] = jnp.zeros_like(w_two)
    for t in range(3):
        for u in range(3):
            piece = w_in[(t * 3 + u) * 48 : (t * 3 + u) * 48 + 48, :]
            for half in range(2):
                at = t * 256 + (u + half) * 64
                w_two[at : at + 48, half * CH : half * CH + CH] = piece
    enlarged[...] = jnp.zeros_like(enlarged)
    turned[...] = jnp.zeros_like(turned)

    def joined(pieces, axis):
        return pieces[0] if len(pieces) == 1 else jnp.concatenate(pieces, axis=axis)

    units = [
        (h, slice(h * HD, h * HD + HD), slice(c * 256, c * 256 + 256)) for h in range(LOCAL) for c in range(2)
    ]

    def add_up(slots, chosen, first=False):
        for h, lanes, some in chosen:
            rows = slice(h * PATCH, h * PATCH + PATCH)
            some_values = joined([values[slot, rows, :] for slot in slots], 1)
            product = dot(some_values, weighted[h, : len(slots) * ROW, some], ((1,), (0,)))
            summed[rows, some] = product if first else summed[rows, some] * fade[h : h + 1, some] + product

    def attend(earlier, slots, chosen):
        scores = [
            dot(joined([keys[slot, :, lanes] for slot in slots], 0), turned_queries[lanes, some], ((1,), (0,)))
            for h, lanes, some in chosen
        ]
        if earlier:
            add_up(earlier, chosen, first=earlier == [0])
        for (h, lanes, some), score in zip(chosen, scores):
            new = jnp.max(score, axis=0, keepdims=True)
            if earlier:
                old = top[h : h + 1, some]
                new = jnp.maximum(old, new)
                fading = jnp.exp2((old - new) * TO_LOG2)
                fade[h : h + 1, some] = fading
            weights = jnp.exp2((score - new) * TO_LOG2)
            sums = jnp.sum(weights, axis=0, keepdims=True)
            total[h : h + 1, some] = total[h : h + 1, some] * fading + sums if earlier else sums
            top[h : h + 1, some] = new
            weighted[h, : len(slots) * ROW, some] = weights.astype(BF16)

    some, rest = units[:3], units[3:]

    def pass_on(kind, t, part):
        arrived(kind, t, part)
        hop(kind, t, t + 1, 0, part)
        arrived(kind, t + 8, part)
        hop(kind, t + 8, t + 9, 1, part)

    pass_on(0, 1, 0)
    pass_on(0, 1, 1)
    pltpu.make_async_copy(queries, queries, plane_recv.at[2]).wait()
    turned_queries[...] = queries[...].T
    attend([], [0], units)
    pass_on(1, 1, 0)
    attend([0], [1, 9], units)

    def step(t, carry):
        pass_on(0, t, 0)
        pass_on(0, t, 1)
        attend([t - 1, t + 7], [t, t + 8], some)
        pass_on(1, t, 0)
        attend([t - 1, t + 7], [t, t + 8], rest)
        return carry

    lax.fori_loop(2, 7, step, 0)
    for part in range(2):
        arrived(0, 7, part)
        hop(0, 7, 8, 0, part)
        arrived(0, 15, part)
    attend([6, 14], [7, 15], some)
    arrived(1, 15, 0)
    hop(1, 15, 8, 1, 0)
    arrived(1, 7, 0)
    attend([6, 14], [7, 15], rest)
    for part in range(2):
        arrived(0, 8, part)
    attend([7, 15], [8], units)
    arrived(1, 8, 0)
    add_up([8], units)

    for h in range(LOCAL):
        sums = total[h : h + 1, :]
        rows = slice(h * PATCH, h * PATCH + PATCH)
        turned[rows, :] = summed[rows, :] * (1.0 / sums)
        level = top[h : h + 1, :] * TO_LOG2 + jnp.log(sums) * math.log2(math.e)
        for term in range(3):
            rounded = level.astype(BF16).astype(F32)
            turned[NUM + term * LOCAL + h : NUM + term * LOCAL + h + 1, :] = rounded
            level = level - rounded
    for away in (1, 2, 3, 0):
        to_row = (row + away) % ROWS
        lanes = pl.ds(pl.multiple_of(to_row * ROW, ROW), ROW)
        sending[lanes, :] = turned[:, lanes].astype(BF16).T
        if away == 0:
            pltpu.make_async_copy(sending.at[tokens_of(place)], parts.at[tokens_of(place)], part_recv).start()
        for i in range(0 if away else 1, GROUPS):
            to_group = (g + i) % GROUPS
            pltpu.make_async_remote_copy(
                src_ref=sending.at[tokens_of(to_row * GROUPS + to_group)],
                dst_ref=parts.at[tokens_of(place)],
                send_sem=part_send,
                recv_sem=part_recv,
                device_id=(z * ROWS + to_row, to_group),
                device_id_type=MESH,
            ).start()

    def ones_where(shape, made):
        r = lax.broadcasted_iota(jnp.int32, shape, 0)
        c = lax.broadcasted_iota(jnp.int32, shape, 1)
        return made(r, c).astype(F32).astype(BF16)

    spread = ones_where(
        (MSG, NUM),
        lambda r, c: (r >= NUM) & (r < NUM + 3 * LOCAL) & ((r - NUM) % LOCAL == c // PATCH),
    )
    pltpu.make_async_copy(parts, parts, part_recv).wait()

    levels = dot(parts[...], spread, ((1,), (0,)))
    numbers = parts[:, :NUM].astype(F32)
    by_row = [slice(r * ROW, r * ROW + ROW) for r in range(ROWS)]
    highest = levels[by_row[0]]
    for r in range(1, ROWS):
        highest = jnp.maximum(highest, levels[by_row[r]])
    above, below = 0.0, 0.0
    for r in range(ROWS):
        share = jnp.exp2(levels[by_row[r]] - highest)
        above = above + share * numbers[by_row[r]]
        below = below + share
    merged = above / below
    tokens = merged[:OWN]
    for other in range(1, GROUPS):
        tokens = tokens + merged[other * OWN : other * OWN + OWN]
    patch = base_ref[...].astype(F32)
    for h in range(LOCAL):
        patch = patch + tokens[:, h * PATCH : h * PATCH + PATCH]
    std = jnp.concatenate([std_ref[...]] * 4, axis=1)
    mean = jnp.concatenate([mean_ref[...]] * 4, axis=1)
    latent = patch * std + mean
    lat_own[...] = jnp.concatenate([latent, latent], axis=1).astype(BF16)

    for slot, device in enumerate(((after, next_g), (after, g), (s, next_g), (before, next_g), (before, g))):
        pltpu.make_async_remote_copy(
            src_ref=lat_own,
            dst_ref=lat_near.at[slot],
            send_sem=near_send,
            recv_sem=near_recv,
            device_id=device,
            device_id_type=MESH,
        ).start()

    def picks(b):
        def made(r, c):
            a, v, low = c // 64, (c // 16) % 4, c % 16
            spot = v + 1 - b
            wanted = (spot // 2) * 64 + a * 32 + (spot % 2) * 16 + low
            return (v < 3) & (r == wanted)

        return ones_where((128, 128), made)

    pick = [picks(0), picks(1)]
    pltpu.make_async_copy(lat_near, lat_near, near_recv).wait()

    has_before = (s > 0).astype(F32)
    has_after = (s < SEQ - 1).astype(F32)
    has_frames = (g > 0).astype(F32)
    tiles = [
        [lat_near[0].astype(F32) * (has_before * has_frames), lat_near[1].astype(F32) * has_before],
        [lat_near[2].astype(F32) * has_frames, lat_own[...].astype(F32)],
        [lat_near[3].astype(F32) * (has_after * has_frames), lat_near[4].astype(F32) * has_after],
    ]
    lane = lax.broadcasted_iota(jnp.int32, (8, 128), 1)
    line = lax.broadcasted_iota(jnp.int32, (8, 128), 0)
    sides = ([], [])
    for f in range(4):
        for r in range(3):
            here = tiles[r][f // 2][(f % 2) * 8 : (f % 2) * 8 + 8]
            left = jnp.where(line == 0, 0.0, pltpu.roll(here, 1, 0))
            right = jnp.where(line == 7, 0.0, pltpu.roll(here, 7, 0))
            sides[0].append(jnp.where(lane < 64, left, here))
            sides[1].append(jnp.where(lane < 64, here, right))
    windows = [
        dot(jnp.concatenate(side, axis=0).astype(BF16), chosen, ((1,), (0,))) for side, chosen in zip(sides, pick)
    ]

    def window(f, r, b):
        at = (f * 3 + r) * 8
        return windows[b][at : at + 8]

    lines = []
    for f in range(2):
        for pair in range(2):
            for b in range(2):
                pieces = [window(f + t, pair + r, b) for t in range(3) for r in range(2)]
                lines.append(jnp.concatenate(pieces, axis=1))
    conv = dot(jnp.concatenate(lines, axis=0).astype(BF16), w_two[...], ((1,), (0,)))
    for half in range(2):
        out = conv[:, half * CH : half * CH + CH] + b_in_ref[...].reshape(1, CH)
        mean_sq = jnp.mean(out * out, axis=1, keepdims=True)
        normed = out * lax.rsqrt(mean_sq + 1e-6) * gain_ref[...].reshape(1, CH)
        active = normed / (1.0 + jnp.exp(-normed))
        for f in range(2):
            for pair in range(2):
                y = 2 * pair + half
                for b in range(2):
                    at = ((f * 2 + pair) * 2 + b) * 8
                    part = active[at : at + 8]
                    if y == 0:
                        part = part * has_before
                    if y == 3:
                        part = part * has_after
                    for twice in range(2):
                        for tile in range(3):
                            enlarged[tile, f * 4 + y, pl.ds(EDGE + 2 * b + twice, 8, stride=4), :] = part[
                                :, tile * 128 : tile * 128 + 128
                            ]

    for v in range(3):
        for f in range(2):
            for y in range(4):
                piece = [enlarged[tile, f * 4 + y, EDGE - 1 + v : EDGE + 31 + v, :] for tile in range(3)]
                piece = jnp.concatenate(piece, axis=1).astype(BF16)
                for line_out in range(4):
                    for u in range(3):
                        if (line_out + u + 1) // 2 == y:
                            at = (f * 4 + line_out) * 32
                            to = (u * 3 + v) * CH
                            columns[at : at + 32, to : to + CH] = piece
    planes = b_up_ref[...]
    for tap in range(9):
        planes = planes + dot(
            columns[:, tap * CH : tap * CH + CH], w_up[tap * OUTCH : tap * OUTCH + OUTCH, :], ((1,), (1,))
        )
    out_ref[...] = planes.astype(BF16)

    for kind in (0, 1):
        sent = v_row.at[: ROW - OWN]
        pltpu.make_async_copy(sent, sent, plane_send.at[kind]).wait()
    sent = queries.at[: PLANE - OWN]
    pltpu.make_async_copy(sent, sent, plane_send.at[2]).wait()
    for way, kind, ring, count in ((0, 0, keys, 8), (0, 1, values, 7), (1, 0, keys, 7), (1, 1, values, 8)):
        sent = ring.at[:count]
        pltpu.make_async_copy(sent, sent, ring_send.at[way, kind]).wait()
    sent = parts.at[: PLANE - OWN]
    pltpu.make_async_copy(sent, sent, part_send).wait()
    pltpu.make_async_copy(lat_near, lat_near, near_send).wait()


def on_device(
    query_states,
    key_states,
    value_states,
    base_patch,
    head_proj,
    latent_std,
    latent_mean,
    w_in,
    b_in,
    gain_mid,
    w_up,
    b_up,
):
    here = pl.BlockSpec(memory_space=pltpu.VMEM)
    far = pl.BlockSpec(memory_space=pltpu.HBM)
    DMA = pltpu.SemaphoreType.DMA
    planes = pl.pallas_call(
        kernel,
        out_shape=jax.ShapeDtypeStruct((256, OUTCH), BF16),
        in_specs=[far] * 12,
        out_specs=here,
        scratch_shapes=[
            pltpu.VMEM((16, ROW, WIDE), BF16),
            pltpu.VMEM((16, NUM, ROW), BF16),
            pltpu.VMEM((ROW, WIDE), BF16),
            pltpu.VMEM((PLANE, WIDE), BF16),
            pltpu.VMEM((WIDE, PLANE), BF16),
            pltpu.VMEM((8, PLANE), F32),
            pltpu.VMEM((8, PLANE), F32),
            pltpu.VMEM((8, PLANE), F32),
            pltpu.VMEM((LOCAL, 2 * ROW, PLANE), BF16),
            pltpu.VMEM((NUM, PLANE), F32),
            pltpu.VMEM((MSG, PLANE), F32),
            pltpu.VMEM((PLANE, MSG), BF16),
            pltpu.VMEM((PLANE, MSG), BF16),
            pltpu.VMEM((OWN, 128), BF16),
            pltpu.VMEM((5, OWN, 128), BF16),
            pltpu.VMEM((OWN, PATCH), BF16),
            pltpu.VMEM((PATCH, WIDE), BF16),
            pltpu.VMEM((1, 16), F32),
            pltpu.VMEM((1, 16), F32),
            pltpu.VMEM((27 * 16, CH), BF16),
            pltpu.VMEM((CH,), F32),
            pltpu.VMEM((CH,), F32),
            pltpu.VMEM((9 * OUTCH, CH), BF16),
            pltpu.VMEM((1, OUTCH), F32),
            pltpu.VMEM((768, 2 * CH), BF16),
            pltpu.VMEM((3, 8, LINE, 128), F32),
            pltpu.VMEM((256, 9 * CH), BF16),
            DMA((3,)),
            DMA((3,)),
            DMA((2, 2)),
            DMA((2, 16, 2)),
            DMA,
            DMA,
            DMA,
            DMA,
            DMA((9,)),
        ],
        compiler_params=pltpu.CompilerParams(
            collective_id=0, has_side_effects=True, vmem_limit_bytes=60 * 1024 * 1024
        ),
        name="attend_and_decode",
    )(
        query_states,
        key_states,
        value_states,
        base_patch,
        head_proj.T,
        latent_std.reshape(1, 16),
        latent_mean.reshape(1, 16),
        w_in.reshape(27 * 16, CH),
        b_in,
        gain_mid,
        w_up.transpose(0, 1, 3, 2).reshape(9 * OUTCH, CH),
        b_up.reshape(1, OUTCH),
    )
    return planes.reshape(2, 4, 32, OUTCH)


def solution(mesh):
    in_specs = (
        P(("seq", "head"), None),
        P(("seq", "head"), None),
        P(("seq", "head"), None),
        P(("seq", "head"), None),
        P("head", None),
        P(),
        P(),
        P(),
        P(),
        P(),
        P(),
        P(),
    )
    out_specs = P("head", "seq", None, None)
    return jax.shard_map(
        on_device, mesh=mesh, in_specs=in_specs, out_specs=out_specs, check_vma=False
    )
```

```python
import math

import jax
import jax.numpy as jnp
from jax import lax
from jax.experimental import pallas as pl
from jax.experimental.pallas import tpu as pltpu
from jax.sharding import PartitionSpec as P

MESH = pl.DeviceIdType.MESH
F32, BF16 = jnp.float32, jnp.bfloat16

SEQ, GROUPS = 64, 8
ROWS = 4
PLACES = ROWS * GROUPS
OWN = 16
ROW = OWN * GROUPS
PLANE = ROW * ROWS
HD, LOCAL = 128, 3
WIDE = HD * LOCAL
PATCH = 64
NUM = PATCH * LOCAL
MSG = 256
CH, OUTCH = 384, 192
EDGE = 8
LINE = 48
TO_LOG2 = math.log2(math.e) / math.sqrt(HD)


def dot(a, b, dims):
    return lax.dot_general(a, b, (dims, ((), ())), preferred_element_type=F32)


def kernel(
    q_in, k_in, v_in, base_far, proj_far, std_far, mean_far, w_in_far, b_in_far, gain_far, w_up_far, b_up_far,
    out_ref,
    keys, values, v_row, queries, turned_queries, top, total, fade, weighted, summed, turned, sending, parts, lat_own, lat_near,
    base_ref, proj_ref, std_ref, mean_ref, w_in, b_in_ref, gain_ref, w_up, b_up_ref, w_two, enlarged, columns, planes,
    plane_send, plane_recv, ring_send, ring_recv, part_send, part_recv, near_send, near_recv, weight_sem,
):
    s, g = lax.axis_index("seq"), lax.axis_index("head")
    z, row = s // ROWS, s % ROWS
    place = row * GROUPS + g
    up, down = ((s + ROWS) % SEQ, g), ((s + SEQ - ROWS) % SEQ, g)
    after, before = (s + 1) % SEQ, (s + SEQ - 1) % SEQ
    next_g, last_g = (g + 1) % GROUPS, (g + GROUPS - 1) % GROUPS

    def peer(i):
        other = (place + i) % PLACES
        return other, (z * ROWS + other // GROUPS, other % GROUPS)

    def columns_of(group):
        return pl.ds(pl.multiple_of(group * WIDE, WIDE), WIDE)

    def tokens_of(index):
        return pl.ds(pl.multiple_of(index * OWN, OWN), OWN)

    barrier = pltpu.get_barrier_semaphore()

    @pl.loop(1, PLACES)
    def greet(i):
        pl.semaphore_signal(barrier, inc=1, device_id=peer(i)[1], device_id_type=MESH)

    for other in (up, down, (after, g), (before, g), (after, last_g), (before, last_g)):
        pl.semaphore_signal(barrier, inc=1, device_id=other, device_id_type=MESH)

    rows_of = ((k_in, keys.at[0]), (v_in, v_row))
    for kind, (source, target) in enumerate(rows_of):
        pltpu.make_async_copy(source.at[:, columns_of(g)], target.at[tokens_of(g)], plane_recv.at[kind]).start()
    pltpu.make_async_copy(q_in.at[:, columns_of(g)], queries.at[tokens_of(place)], plane_recv.at[2]).start()
    proj_in = pltpu.make_async_copy(proj_far, proj_ref, weight_sem.at[8])
    proj_in.start()
    pl.semaphore_wait(barrier, PLACES - 1 + 6)

    for kind, (source, target) in enumerate(rows_of):

        @pl.loop(1, GROUPS)
        def send_row(i):
            other = (g + i) % GROUPS
            pltpu.make_async_remote_copy(
                src_ref=source.at[:, columns_of(other)],
                dst_ref=target.at[tokens_of(g)],
                send_sem=plane_send.at[kind],
                recv_sem=plane_recv.at[kind],
                device_id=(s, other),
                device_id_type=MESH,
            ).start()

    def portion(kind, slot, part):
        return values.at[slot] if kind else keys.at[slot, pl.ds(part * ROW // 2, ROW // 2)]

    def hop(kind, source, target, way, part):
        pltpu.make_async_remote_copy(
            src_ref=portion(kind, source, part),
            dst_ref=portion(kind, target, part),
            send_sem=ring_send.at[way, kind],
            recv_sem=ring_recv.at[kind, target, part],
            device_id=(up, down)[way],
            device_id_type=MESH,
        ).start()

    def arrived(kind, slot, part):
        pltpu.make_async_copy(
            portion(kind, slot, part), portion(kind, slot, part), ring_recv.at[kind, slot, part]
        ).wait()

    for kind, (source, target) in enumerate(rows_of):
        pltpu.make_async_copy(target, target, plane_recv.at[kind]).wait()
        if kind == 1:
            proj_in.wait()
            for h in range(LOCAL):
                lanes = slice(h * HD, h * HD + HD)
                values[0, h] = dot(
                    proj_ref[:, lanes], v_row[:, lanes], ((1,), (1,))
                ).astype(BF16)
        for part in range(2 - kind):
            hop(kind, 0, 1, 0, part)
            hop(kind, 0, 9, 1, part)

    @pl.loop(1, PLACES)
    def send_query(i):
        device = peer(i)[1]
        pltpu.make_async_remote_copy(
            src_ref=q_in.at[:, columns_of(device[1])],
            dst_ref=queries.at[tokens_of(place)],
            send_sem=plane_send.at[2],
            recv_sem=plane_recv.at[2],
            device_id=device,
            device_id_type=MESH,
        ).start()

    parameters = [
        pltpu.make_async_copy(source, target, weight_sem.at[i])
        for i, (source, target) in enumerate(
            (
                (w_in_far, w_in),
                (w_up_far, w_up),
                (base_far, base_ref),
                (std_far, std_ref),
                (mean_far, mean_ref),
                (b_in_far, b_in_ref),
                (gain_far, gain_ref),
                (b_up_far, b_up_ref),
            )
        )
    ]
    for copy in parameters:
        copy.start()

    for copy in parameters:
        copy.wait()
    w_two[...] = jnp.zeros_like(w_two)
    for t in range(3):
        for u in range(3):
            piece = w_in[(t * 3 + u) * 48 : (t * 3 + u) * 48 + 48, :]
            for half in range(2):
                at = t * 256 + (u + half) * 64
                w_two[at : at + 48, half * CH : half * CH + CH] = piece
    enlarged[...] = jnp.zeros_like(enlarged)
    turned[...] = jnp.zeros_like(turned)
    top[...] = jnp.full_like(top, -1e30)
    total[...] = jnp.zeros_like(total)
    summed[...] = jnp.zeros_like(summed)

    pltpu.make_async_copy(queries, queries, plane_recv.at[2]).wait()
    for h in range(LOCAL):
        turned_queries[h] = queries[:, h * HD : h * HD + HD].T

    halves = (slice(0, PLANE // 2), slice(PLANE // 2, PLANE))

    @pl.loop(1, 9)
    def step(i):
        first = i % 8
        slots = (first, first + 8)

        for part in range(2):

            @pl.when(i < 8)
            def pass_keys():
                arrived(0, i, part)
                hop(0, i, i + 1, 0, part)
                arrived(0, i + 8, part)

                @pl.when(i < 7)
                def further():
                    hop(0, i + 8, i + 9, 1, part)

        @pl.when(i == 8)
        def last_keys():
            arrived(0, 8, 0)
            arrived(0, 8, 1)

        @pl.loop(0, LOCAL)
        def weigh(h):
            lanes = pl.ds(pl.multiple_of(h * HD, HD), HD)
            shard = jnp.concatenate([keys[slot, :, lanes] for slot in slots], axis=0)
            scores = [dot(shard, turned_queries[h, :, some], ((1,), (0,))) for some in halves]
            for some, score in zip(halves, scores):
                old = top[h, :, some]
                new = jnp.maximum(old, jnp.max(score, axis=0, keepdims=True))
                fading = jnp.exp2((old - new) * TO_LOG2)
                weights = jnp.exp2((score - new) * TO_LOG2)
                total[h, :, some] = total[h, :, some] * fading + jnp.sum(weights, axis=0, keepdims=True)
                fade[h, :, some] = fading
                top[h, :, some] = new
                weighted[h, :, some] = weights.astype(BF16)

        @pl.when(i < 8)
        def pass_values():
            arrived(1, i, 0)

            @pl.when(i < 7)
            def further():
                hop(1, i, i + 1, 0, 0)

            arrived(1, i + 8, 0)
            hop(1, i + 8, 8 + (i + 1) % 8, 1, 0)

        @pl.when(i == 8)
        def last_values():
            arrived(1, 8, 0)

        @pl.loop(0, LOCAL)
        def add_up(h):
            shard = jnp.concatenate([values[slot, h] for slot in slots], axis=1)
            for some in halves:
                product = dot(shard, weighted[h, :, some], ((1,), (0,)))
                summed[h, :, some] = summed[h, :, some] * fade[h, :, some] + product

    for h in range(LOCAL):
        sums = total[h]
        turned[h * PATCH : h * PATCH + PATCH, :] = summed[h] * (1.0 / sums)
        level = top[h] * TO_LOG2 + jnp.log(sums) * math.log2(math.e)
        for term in range(3):
            rounded = level.astype(BF16).astype(F32)
            turned[NUM + term * LOCAL + h : NUM + term * LOCAL + h + 1, :] = rounded
            level = level - rounded
    @pl.loop(0, ROWS)
    def send_parts(away):
        to_row = (row + 1 + away) % ROWS
        lanes = pl.ds(pl.multiple_of(to_row * ROW, ROW), ROW)
        sending[lanes, :] = turned[:, lanes].astype(BF16).T

        @pl.loop(jnp.where(away == ROWS - 1, 1, 0), GROUPS)
        def send_part(i):
            to_group = (g + i) % GROUPS
            pltpu.make_async_remote_copy(
                src_ref=sending.at[tokens_of(to_row * GROUPS + to_group)],
                dst_ref=parts.at[tokens_of(place)],
                send_sem=part_send,
                recv_sem=part_recv,
                device_id=(z * ROWS + to_row, to_group),
                device_id_type=MESH,
            ).start()

    own_part = pltpu.make_async_copy(sending.at[tokens_of(place)], parts.at[tokens_of(place)], part_recv)
    own_part.start()

    def ones_where(shape, made):
        r = lax.broadcasted_iota(jnp.int32, shape, 0)
        c = lax.broadcasted_iota(jnp.int32, shape, 1)
        return made(r, c).astype(F32).astype(BF16)

    spread = ones_where(
        (MSG, NUM),
        lambda r, c: (r >= NUM) & (r < NUM + 3 * LOCAL) & ((r - NUM) % LOCAL == c // PATCH),
    )
    pltpu.make_async_copy(parts, parts, part_recv).wait()

    levels = dot(parts[...], spread, ((1,), (0,)))
    numbers = parts[:, :NUM].astype(F32)
    by_row = [slice(r * ROW, r * ROW + ROW) for r in range(ROWS)]
    highest = levels[by_row[0]]
    for r in range(1, ROWS):
        highest = jnp.maximum(highest, levels[by_row[r]])
    above, below = 0.0, 0.0
    for r in range(ROWS):
        share = jnp.exp2(levels[by_row[r]] - highest)
        above = above + share * numbers[by_row[r]]
        below = below + share
    merged = above / below
    tokens = merged[:OWN]
    for other in range(1, GROUPS):
        tokens = tokens + merged[other * OWN : other * OWN + OWN]
    patch = base_ref[...].astype(F32)
    for h in range(LOCAL):
        patch = patch + tokens[:, h * PATCH : h * PATCH + PATCH]
    std = jnp.concatenate([std_ref[...]] * 4, axis=1)
    mean = jnp.concatenate([mean_ref[...]] * 4, axis=1)
    latent = patch * std + mean
    lat_own[...] = jnp.concatenate([latent, latent], axis=1).astype(BF16)

    for slot, device in enumerate(((after, next_g), (after, g), (s, next_g), (before, next_g), (before, g))):
        pltpu.make_async_remote_copy(
            src_ref=lat_own,
            dst_ref=lat_near.at[slot],
            send_sem=near_send,
            recv_sem=near_recv,
            device_id=device,
            device_id_type=MESH,
        ).start()

    def picks(b):
        def made(r, c):
            a, v, low = c // 64, (c // 16) % 4, c % 16
            spot = v + 1 - b
            wanted = (spot // 2) * 64 + a * 32 + (spot % 2) * 16 + low
            return (v < 3) & (r == wanted)

        return ones_where((128, 128), made)

    pick = [picks(0), picks(1)]
    pltpu.make_async_copy(lat_near, lat_near, near_recv).wait()

    has_before = (s > 0).astype(F32)
    has_after = (s < SEQ - 1).astype(F32)
    has_frames = (g > 0).astype(F32)
    tiles = [
        [lat_near[0].astype(F32) * (has_before * has_frames), lat_near[1].astype(F32) * has_before],
        [lat_near[2].astype(F32) * has_frames, lat_own[...].astype(F32)],
        [lat_near[3].astype(F32) * (has_after * has_frames), lat_near[4].astype(F32) * has_after],
    ]
    lane = lax.broadcasted_iota(jnp.int32, (8, 128), 1)
    line = lax.broadcasted_iota(jnp.int32, (8, 128), 0)
    sides = ([], [])
    for f in range(4):
        for r in range(3):
            here = tiles[r][f // 2][(f % 2) * 8 : (f % 2) * 8 + 8]
            left = jnp.where(line == 0, 0.0, pltpu.roll(here, 1, 0))
            right = jnp.where(line == 7, 0.0, pltpu.roll(here, 7, 0))
            sides[0].append(jnp.where(lane < 64, left, here))
            sides[1].append(jnp.where(lane < 64, here, right))
    windows = [
        dot(jnp.concatenate(side, axis=0).astype(BF16), chosen, ((1,), (0,))) for side, chosen in zip(sides, pick)
    ]

    def window(f, r, b):
        at = (f * 3 + r) * 8
        return windows[b][at : at + 8]

    lines = []
    for f in range(2):
        for pair in range(2):
            for b in range(2):
                pieces = [window(f + t, pair + r, b) for t in range(3) for r in range(2)]
                lines.append(jnp.concatenate(pieces, axis=1))
    conv = dot(jnp.concatenate(lines, axis=0).astype(BF16), w_two[...], ((1,), (0,)))
    for half in range(2):
        out = conv[:, half * CH : half * CH + CH] + b_in_ref[...].reshape(1, CH)
        mean_sq = jnp.mean(out * out, axis=1, keepdims=True)
        normed = out * lax.rsqrt(mean_sq + 1e-6) * gain_ref[...].reshape(1, CH)
        active = normed / (1.0 + jnp.exp(-normed))
        for f in range(2):
            for pair in range(2):
                y = 2 * pair + half
                for b in range(2):
                    at = ((f * 2 + pair) * 2 + b) * 8
                    part = active[at : at + 8]
                    if y == 0:
                        part = part * has_before
                    if y == 3:
                        part = part * has_after
                    for twice in range(2):
                        for tile in range(3):
                            enlarged[tile, f * 4 + y, pl.ds(EDGE + 2 * b + twice, 8, stride=4), :] = part[
                                :, tile * 128 : tile * 128 + 128
                            ]

    for v in range(3):
        for f in range(2):
            for y in range(4):
                piece = [enlarged[tile, f * 4 + y, EDGE - 1 + v : EDGE + 31 + v, :] for tile in range(3)]
                piece = jnp.concatenate(piece, axis=1).astype(BF16)
                for line_out in range(4):
                    for u in range(3):
                        if (line_out + u + 1) // 2 == y:
                            at = (f * 4 + line_out) * 32
                            to = (u * 3 + v) * CH
                            columns[at : at + 32, to : to + CH] = piece
    planes[...] = jnp.zeros_like(planes) + b_up_ref[...]

    @pl.loop(0, 9)
    def convolve(tap):
        lanes = pl.ds(pl.multiple_of(tap * CH, CH), CH)
        rows = pl.ds(pl.multiple_of(tap * OUTCH, OUTCH), OUTCH)
        planes[...] += dot(columns[:, lanes], w_up[rows, :], ((1,), (1,)))

    out_ref[...] = planes[...].astype(BF16)

    for kind in (0, 1):
        sent = v_row.at[: ROW - OWN]
        pltpu.make_async_copy(sent, sent, plane_send.at[kind]).wait()
    sent = queries.at[: PLANE - OWN]
    pltpu.make_async_copy(sent, sent, plane_send.at[2]).wait()
    for way, kind, ring, count in ((0, 0, keys, 8), (0, 1, values, 7), (1, 0, keys, 7), (1, 1, values, 8)):
        sent = ring.at[:count]
        pltpu.make_async_copy(sent, sent, ring_send.at[way, kind]).wait()
    sent = parts.at[: PLANE - OWN]
    pltpu.make_async_copy(sent, sent, part_send).wait()
    pltpu.make_async_copy(lat_near, lat_near, near_send).wait()


def on_device(
    query_states,
    key_states,
    value_states,
    base_patch,
    head_proj,
    latent_std,
    latent_mean,
    w_in,
    b_in,
    gain_mid,
    w_up,
    b_up,
):
    here = pl.BlockSpec(memory_space=pltpu.VMEM)
    far = pl.BlockSpec(memory_space=pltpu.HBM)
    DMA = pltpu.SemaphoreType.DMA
    planes = pl.pallas_call(
        kernel,
        out_shape=jax.ShapeDtypeStruct((256, OUTCH), BF16),
        in_specs=[far] * 12,
        out_specs=here,
        scratch_shapes=[
            pltpu.VMEM((16, ROW, WIDE), BF16),
            pltpu.VMEM((16, LOCAL, PATCH, ROW), BF16),
            pltpu.VMEM((ROW, WIDE), BF16),
            pltpu.VMEM((PLANE, WIDE), BF16),
            pltpu.VMEM((LOCAL, HD, PLANE), BF16),
            pltpu.VMEM((LOCAL, 1, PLANE), F32),
            pltpu.VMEM((LOCAL, 1, PLANE), F32),
            pltpu.VMEM((LOCAL, 1, PLANE), F32),
            pltpu.VMEM((LOCAL, 2 * ROW, PLANE), BF16),
            pltpu.VMEM((LOCAL, PATCH, PLANE), F32),
            pltpu.VMEM((MSG, PLANE), F32),
            pltpu.VMEM((PLANE, MSG), BF16),
            pltpu.VMEM((PLANE, MSG), BF16),
            pltpu.VMEM((OWN, 128), BF16),
            pltpu.VMEM((5, OWN, 128), BF16),
            pltpu.VMEM((OWN, PATCH), BF16),
            pltpu.VMEM((PATCH, WIDE), BF16),
            pltpu.VMEM((1, 16), F32),
            pltpu.VMEM((1, 16), F32),
            pltpu.VMEM((27 * 16, CH), BF16),
            pltpu.VMEM((CH,), F32),
            pltpu.VMEM((CH,), F32),
            pltpu.VMEM((9 * OUTCH, CH), BF16),
            pltpu.VMEM((1, OUTCH), F32),
            pltpu.VMEM((768, 2 * CH), BF16),
            pltpu.VMEM((3, 8, LINE, 128), F32),
            pltpu.VMEM((256, 9 * CH), BF16),
            pltpu.VMEM((256, OUTCH), F32),
            DMA((3,)),
            DMA((3,)),
            DMA((2, 2)),
            DMA((2, 16, 2)),
            DMA,
            DMA,
            DMA,
            DMA,
            DMA((9,)),
        ],
        compiler_params=pltpu.CompilerParams(
            collective_id=0, has_side_effects=True, vmem_limit_bytes=60 * 1024 * 1024
        ),
        name="attend_and_decode",
    )(
        query_states,
        key_states,
        value_states,
        base_patch,
        head_proj.T,
        latent_std.reshape(1, 16),
        latent_mean.reshape(1, 16),
        w_in.reshape(27 * 16, CH),
        b_in,
        gain_mid,
        w_up.transpose(0, 1, 3, 2).reshape(9 * OUTCH, CH),
        b_up.reshape(1, OUTCH),
    )
    return planes.reshape(2, 4, 32, OUTCH)


def solution(mesh):
    in_specs = (
        P(("seq", "head"), None),
        P(("seq", "head"), None),
        P(("seq", "head"), None),
        P(("seq", "head"), None),
        P("head", None),
        P(),
        P(),
        P(),
        P(),
        P(),
        P(),
        P(),
    )
    out_specs = P("head", "seq", None, None)
    return jax.shard_map(
        on_device, mesh=mesh, in_specs=in_specs, out_specs=out_specs, check_vma=False
    )
```

```python
import math

import jax
import jax.numpy as jnp
from jax import lax
from jax.experimental import pallas as pl
from jax.experimental.pallas import tpu as pltpu
from jax.sharding import PartitionSpec as P

MESH = pl.DeviceIdType.MESH
F32, BF16 = jnp.float32, jnp.bfloat16

SEQ, GROUPS = 64, 8
ROWS = 4
PLACES = ROWS * GROUPS
OWN = 16
ROW = OWN * GROUPS
PLANE = ROW * ROWS
HD, LOCAL = 128, 3
WIDE = HD * LOCAL
PATCH = 64
NUM = PATCH * LOCAL
MSG = 256
TALL = PATCH + 8
CH, OUTCH = 384, 192
EDGE = 8
LINE = 48
TO_LOG2 = math.log2(math.e) / math.sqrt(HD)


def dot(a, b, dims):
    return lax.dot_general(a, b, (dims, ((), ())), preferred_element_type=F32)


def kernel(
    q_in, k_in, v_in, base_far, proj_far, std_far, mean_far, w_in_far, b_in_far, gain_far, w_up_far, b_up_far,
    out_ref,
    keys, values, v_row, queries, turned_queries, top, fade, weighted, summed, turned, sending, parts, lat_own, lat_near,
    base_ref, proj_ref, std_ref, mean_ref, w_in, b_in_ref, gain_ref, w_up, b_up_ref, w_two, enlarged, columns,
    plane_send, plane_recv, ring_send, ring_recv, part_send, part_recv, near_send, near_recv, weight_sem,
):
    s, g = lax.axis_index("seq"), lax.axis_index("head")
    z, row = s // ROWS, s % ROWS
    place = row * GROUPS + g
    up, down = ((s + ROWS) % SEQ, g), ((s + SEQ - ROWS) % SEQ, g)
    after, before = (s + 1) % SEQ, (s + SEQ - 1) % SEQ
    next_g, last_g = (g + 1) % GROUPS, (g + GROUPS - 1) % GROUPS

    def peer(i):
        other = (place + i) % PLACES
        return other, (z * ROWS + other // GROUPS, other % GROUPS)

    def columns_of(group):
        return pl.ds(pl.multiple_of(group * WIDE, WIDE), WIDE)

    def tokens_of(index):
        return pl.ds(pl.multiple_of(index * OWN, OWN), OWN)

    barrier = pltpu.get_barrier_semaphore()

    for i in range(1, PLACES):
        pl.semaphore_signal(barrier, inc=1, device_id=peer(i)[1], device_id_type=MESH)
    for other in (up, down, (after, g), (before, g), (after, last_g), (before, last_g)):
        pl.semaphore_signal(barrier, inc=1, device_id=other, device_id_type=MESH)

    rows_of = ((k_in, keys.at[0]), (v_in, v_row))
    for kind, (source, target) in enumerate(rows_of):
        pltpu.make_async_copy(source.at[:, columns_of(g)], target.at[tokens_of(g)], plane_recv.at[kind]).start()
    pltpu.make_async_copy(q_in.at[:, columns_of(g)], queries.at[tokens_of(place)], plane_recv.at[2]).start()
    proj_in = pltpu.make_async_copy(proj_far, proj_ref, weight_sem.at[8])
    proj_in.start()
    pl.semaphore_wait(barrier, PLACES - 1 + 6)

    for kind, (source, target) in enumerate(rows_of):
        for i in range(1, GROUPS):
            other = (g + i) % GROUPS
            pltpu.make_async_remote_copy(
                src_ref=source.at[:, columns_of(other)],
                dst_ref=target.at[tokens_of(g)],
                send_sem=plane_send.at[kind],
                recv_sem=plane_recv.at[kind],
                device_id=(s, other),
                device_id_type=MESH,
            ).start()

    def portion(kind, slot, part):
        return values.at[slot] if kind else keys.at[slot, pl.ds(part * ROW // 2, ROW // 2)]

    def hop(kind, source, target, way, part):
        pltpu.make_async_remote_copy(
            src_ref=portion(kind, source, part),
            dst_ref=portion(kind, target, part),
            send_sem=ring_send.at[way, kind],
            recv_sem=ring_recv.at[kind, target, part],
            device_id=(up, down)[way],
            device_id_type=MESH,
        ).start()

    def arrived(kind, slot, part):
        pltpu.make_async_copy(
            portion(kind, slot, part), portion(kind, slot, part), ring_recv.at[kind, slot, part]
        ).wait()

    for kind, (source, target) in enumerate(rows_of):
        pltpu.make_async_copy(target, target, plane_recv.at[kind]).wait()
        if kind == 1:
            proj_in.wait()
            for h in range(LOCAL):
                lanes = slice(h * HD, h * HD + HD)
                values[0, h * PATCH : h * PATCH + PATCH, :] = dot(
                    proj_ref[:, lanes], v_row[:, lanes], ((1,), (1,))
                ).astype(BF16)
        for part in range(2 - kind):
            hop(kind, 0, 1, 0, part)
            hop(kind, 0, 9, 1, part)

    for i in range(1, PLACES):
        device = peer(i)[1]
        pltpu.make_async_remote_copy(
            src_ref=q_in.at[:, columns_of(device[1])],
            dst_ref=queries.at[tokens_of(place)],
            send_sem=plane_send.at[2],
            recv_sem=plane_recv.at[2],
            device_id=device,
            device_id_type=MESH,
        ).start()

    parameters = [
        pltpu.make_async_copy(source, target, weight_sem.at[i])
        for i, (source, target) in enumerate(
            (
                (w_in_far, w_in),
                (w_up_far, w_up),
                (base_far, base_ref),
                (std_far, std_ref),
                (mean_far, mean_ref),
                (b_in_far, b_in_ref),
                (gain_far, gain_ref),
                (b_up_far, b_up_ref),
            )
        )
    ]
    for copy in parameters:
        copy.start()

    for copy in parameters:
        copy.wait()
    w_two[...] = jnp.zeros_like(w_two)
    for t in range(3):
        for u in range(3):
            piece = w_in[(t * 3 + u) * 48 : (t * 3 + u) * 48 + 48, :]
            for half in range(2):
                at = t * 256 + (u + half) * 64
                w_two[at : at + 48, half * CH : half * CH + CH] = piece
    enlarged[...] = jnp.zeros_like(enlarged)
    turned[...] = jnp.zeros_like(turned)

    def joined(pieces, axis):
        return pieces[0] if len(pieces) == 1 else jnp.concatenate(pieces, axis=axis)

    units = [
        (h, slice(h * HD, h * HD + HD), slice(c * 256, c * 256 + 256)) for h in range(LOCAL) for c in range(2)
    ]

    def add_up(slots, chosen, first=False):
        for h, lanes, some in chosen:
            some_values = joined([values[slot, h * PATCH : h * PATCH + PATCH, :] for slot in slots], 1)
            some_values = jnp.concatenate([some_values, jnp.ones((16, len(slots) * ROW), BF16)], axis=0)
            product = dot(some_values, weighted[h, : len(slots) * ROW, some], ((1,), (0,)))[:TALL]
            rows = slice(h * TALL, h * TALL + TALL)
            summed[rows, some] = product if first else summed[rows, some] * fade[h : h + 1, some] + product

    def attend(earlier, slots, chosen):
        scores = [
            dot(joined([keys[slot, :, lanes] for slot in slots], 0), turned_queries[lanes, some], ((1,), (0,)))
            for h, lanes, some in chosen
        ]
        if earlier:
            add_up(earlier, chosen, first=earlier == [0])
        for (h, lanes, some), score in zip(chosen, scores):
            new = jnp.max(score, axis=0, keepdims=True)
            if earlier:
                old = top[h : h + 1, some]
                new = jnp.maximum(old, new)
                fading = jnp.exp2((old - new) * TO_LOG2)
                fade[h : h + 1, some] = fading
            weights = jnp.exp2((score - new) * TO_LOG2)
            top[h : h + 1, some] = new
            weighted[h, : len(slots) * ROW, some] = weights.astype(BF16)

    some, rest = units[:3], units[3:]

    def pass_on(kind, t, part):
        arrived(kind, t, part)
        hop(kind, t, t + 1, 0, part)
        arrived(kind, t + 8, part)
        hop(kind, t + 8, t + 9, 1, part)

    pass_on(0, 1, 0)
    pass_on(0, 1, 1)
    pass_on(1, 1, 0)
    pltpu.make_async_copy(queries, queries, plane_recv.at[2]).wait()
    turned_queries[...] = queries[...].T
    attend([], [0], units)
    pass_on(0, 2, 0)
    pass_on(0, 2, 1)
    attend([0], [1, 9], some)
    pass_on(1, 2, 0)
    attend([0], [1, 9], rest)

    def step(t, carry):
        for event, (kind, part) in enumerate(((0, 0), (0, 1), (1, 0))):
            pass_on(kind, t, part)
            attend([t - 2, t + 6], [t - 1, t + 7], units[event * 2 : event * 2 + 2])
        return carry

    lax.fori_loop(3, 7, step, 0)
    for part in range(2):
        arrived(0, 7, part)
        hop(0, 7, 8, 0, part)
        arrived(0, 15, part)
        attend([5, 13], [6, 14], units[part * 2 : part * 2 + 2])
    arrived(1, 15, 0)
    hop(1, 15, 8, 1, 0)
    arrived(1, 7, 0)
    attend([5, 13], [6, 14], units[4:])
    attend([6, 14], [7, 15], units)
    for part in range(2):
        arrived(0, 8, part)
    attend([7, 15], [8], units)
    arrived(1, 8, 0)
    add_up([8], units)

    for h in range(LOCAL):
        sums = summed[h * TALL + PATCH : h * TALL + PATCH + 1, :]
        turned[h * PATCH : h * PATCH + PATCH, :] = summed[h * TALL : h * TALL + PATCH, :] * (1.0 / sums)
        level = top[h : h + 1, :] * TO_LOG2 + jnp.log(sums) * math.log2(math.e)
        for term in range(3):
            rounded = level.astype(BF16).astype(F32)
            turned[NUM + term * LOCAL + h : NUM + term * LOCAL + h + 1, :] = rounded
            level = level - rounded
    for away in (1, 2, 3, 0):
        to_row = (row + away) % ROWS
        lanes = pl.ds(pl.multiple_of(to_row * ROW, ROW), ROW)
        sending[lanes, :] = turned[:, lanes].astype(BF16).T
        if away == 0:
            pltpu.make_async_copy(sending.at[tokens_of(place)], parts.at[tokens_of(place)], part_recv).start()
        for i in range(0 if away else 1, GROUPS):
            to_group = (g + i) % GROUPS
            pltpu.make_async_remote_copy(
                src_ref=sending.at[tokens_of(to_row * GROUPS + to_group)],
                dst_ref=parts.at[tokens_of(place)],
                send_sem=part_send,
                recv_sem=part_recv,
                device_id=(z * ROWS + to_row, to_group),
                device_id_type=MESH,
            ).start()

    def ones_where(shape, made):
        r = lax.broadcasted_iota(jnp.int32, shape, 0)
        c = lax.broadcasted_iota(jnp.int32, shape, 1)
        return made(r, c).astype(F32).astype(BF16)

    spread = ones_where(
        (MSG, NUM),
        lambda r, c: (r >= NUM) & (r < NUM + 3 * LOCAL) & ((r - NUM) % LOCAL == c // PATCH),
    )
    pltpu.make_async_copy(parts, parts, part_recv).wait()

    levels = dot(parts[...], spread, ((1,), (0,)))
    numbers = parts[:, :NUM].astype(F32)
    by_row = [slice(r * ROW, r * ROW + ROW) for r in range(ROWS)]
    highest = levels[by_row[0]]
    for r in range(1, ROWS):
        highest = jnp.maximum(highest, levels[by_row[r]])
    above, below = 0.0, 0.0
    for r in range(ROWS):
        share = jnp.exp2(levels[by_row[r]] - highest)
        above = above + share * numbers[by_row[r]]
        below = below + share
    merged = above / below
    tokens = merged[:OWN]
    for other in range(1, GROUPS):
        tokens = tokens + merged[other * OWN : other * OWN + OWN]
    patch = base_ref[...].astype(F32)
    for h in range(LOCAL):
        patch = patch + tokens[:, h * PATCH : h * PATCH + PATCH]
    std = jnp.concatenate([std_ref[...]] * 4, axis=1)
    mean = jnp.concatenate([mean_ref[...]] * 4, axis=1)
    latent = patch * std + mean
    lat_own[...] = jnp.concatenate([latent, latent], axis=1).astype(BF16)

    for slot, device in enumerate(((after, next_g), (after, g), (s, next_g), (before, next_g), (before, g))):
        pltpu.make_async_remote_copy(
            src_ref=lat_own,
            dst_ref=lat_near.at[slot],
            send_sem=near_send,
            recv_sem=near_recv,
            device_id=device,
            device_id_type=MESH,
        ).start()

    def picks(b):
        def made(r, c):
            a, v, low = c // 64, (c // 16) % 4, c % 16
            spot = v + 1 - b
            wanted = (spot // 2) * 64 + a * 32 + (spot % 2) * 16 + low
            return (v < 3) & (r == wanted)

        return ones_where((128, 128), made)

    pick = [picks(0), picks(1)]
    pltpu.make_async_copy(lat_near, lat_near, near_recv).wait()

    has_before = (s > 0).astype(F32)
    has_after = (s < SEQ - 1).astype(F32)
    has_frames = (g > 0).astype(F32)
    tiles = [
        [lat_near[0].astype(F32) * (has_before * has_frames), lat_near[1].astype(F32) * has_before],
        [lat_near[2].astype(F32) * has_frames, lat_own[...].astype(F32)],
        [lat_near[3].astype(F32) * (has_after * has_frames), lat_near[4].astype(F32) * has_after],
    ]
    lane = lax.broadcasted_iota(jnp.int32, (8, 128), 1)
    line = lax.broadcasted_iota(jnp.int32, (8, 128), 0)
    sides = ([], [])
    for f in range(4):
        for r in range(3):
            here = tiles[r][f // 2][(f % 2) * 8 : (f % 2) * 8 + 8]
            left = jnp.where(line == 0, 0.0, pltpu.roll(here, 1, 0))
            right = jnp.where(line == 7, 0.0, pltpu.roll(here, 7, 0))
            sides[0].append(jnp.where(lane < 64, left, here))
            sides[1].append(jnp.where(lane < 64, here, right))
    windows = [
        dot(jnp.concatenate(side, axis=0).astype(BF16), chosen, ((1,), (0,))) for side, chosen in zip(sides, pick)
    ]

    def window(f, r, b):
        at = (f * 3 + r) * 8
        return windows[b][at : at + 8]

    lines = []
    for f in range(2):
        for pair in range(2):
            for b in range(2):
                pieces = [window(f + t, pair + r, b) for t in range(3) for r in range(2)]
                lines.append(jnp.concatenate(pieces, axis=1))
    conv = dot(jnp.concatenate(lines, axis=0).astype(BF16), w_two[...], ((1,), (0,)))
    for half in range(2):
        out = conv[:, half * CH : half * CH + CH] + b_in_ref[...].reshape(1, CH)
        mean_sq = jnp.mean(out * out, axis=1, keepdims=True)
        normed = out * lax.rsqrt(mean_sq + 1e-6) * gain_ref[...].reshape(1, CH)
        active = normed / (1.0 + jnp.exp(-normed))
        for f in range(2):
            for pair in range(2):
                y = 2 * pair + half
                for b in range(2):
                    at = ((f * 2 + pair) * 2 + b) * 8
                    part = active[at : at + 8]
                    if y == 0:
                        part = part * has_before
                    if y == 3:
                        part = part * has_after
                    for twice in range(2):
                        for tile in range(3):
                            enlarged[tile, f * 4 + y, pl.ds(EDGE + 2 * b + twice, 8, stride=4), :] = part[
                                :, tile * 128 : tile * 128 + 128
                            ]

    for v in range(3):
        for f in range(2):
            for y in range(4):
                piece = [enlarged[tile, f * 4 + y, EDGE - 1 + v : EDGE + 31 + v, :] for tile in range(3)]
                piece = jnp.concatenate(piece, axis=1).astype(BF16)
                for line_out in range(4):
                    for u in range(3):
                        if (line_out + u + 1) // 2 == y:
                            at = (f * 4 + line_out) * 32
                            to = (u * 3 + v) * CH
                            columns[at : at + 32, to : to + CH] = piece
    planes = b_up_ref[...]
    for tap in range(9):
        planes = planes + dot(
            columns[:, tap * CH : tap * CH + CH], w_up[tap * OUTCH : tap * OUTCH + OUTCH, :], ((1,), (1,))
        )
    out_ref[...] = planes.astype(BF16)

    for kind in (0, 1):
        sent = v_row.at[: ROW - OWN]
        pltpu.make_async_copy(sent, sent, plane_send.at[kind]).wait()
    sent = queries.at[: PLANE - OWN]
    pltpu.make_async_copy(sent, sent, plane_send.at[2]).wait()
    for way, kind, ring, count in ((0, 0, keys, 8), (0, 1, values, 7), (1, 0, keys, 7), (1, 1, values, 8)):
        sent = ring.at[:count]
        pltpu.make_async_copy(sent, sent, ring_send.at[way, kind]).wait()
    sent = parts.at[: PLANE - OWN]
    pltpu.make_async_copy(sent, sent, part_send).wait()
    pltpu.make_async_copy(lat_near, lat_near, near_send).wait()


def on_device(
    query_states,
    key_states,
    value_states,
    base_patch,
    head_proj,
    latent_std,
    latent_mean,
    w_in,
    b_in,
    gain_mid,
    w_up,
    b_up,
):
    here = pl.BlockSpec(memory_space=pltpu.VMEM)
    far = pl.BlockSpec(memory_space=pltpu.HBM)
    DMA = pltpu.SemaphoreType.DMA
    planes = pl.pallas_call(
        kernel,
        out_shape=pltpu.VMEM((256, OUTCH), BF16),
        in_specs=[far] * 12,
        out_specs=here,
        scratch_shapes=[
            pltpu.VMEM((16, ROW, WIDE), BF16),
            pltpu.VMEM((16, NUM, ROW), BF16),
            pltpu.VMEM((ROW, WIDE), BF16),
            pltpu.VMEM((PLANE, WIDE), BF16),
            pltpu.VMEM((WIDE, PLANE), BF16),
            pltpu.VMEM((8, PLANE), F32),
            pltpu.VMEM((8, PLANE), F32),
            pltpu.VMEM((LOCAL, 2 * ROW, PLANE), BF16),
            pltpu.VMEM((LOCAL * TALL, PLANE), F32),
            pltpu.VMEM((MSG, PLANE), F32),
            pltpu.VMEM((PLANE, MSG), BF16),
            pltpu.VMEM((PLANE, MSG), BF16),
            pltpu.VMEM((OWN, 128), BF16),
            pltpu.VMEM((5, OWN, 128), BF16),
            pltpu.VMEM((OWN, PATCH), BF16),
            pltpu.VMEM((PATCH, WIDE), BF16),
            pltpu.VMEM((1, 16), F32),
            pltpu.VMEM((1, 16), F32),
            pltpu.VMEM((27 * 16, CH), BF16),
            pltpu.VMEM((CH,), F32),
            pltpu.VMEM((CH,), F32),
            pltpu.VMEM((9 * OUTCH, CH), BF16),
            pltpu.VMEM((1, OUTCH), F32),
            pltpu.VMEM((768, 2 * CH), BF16),
            pltpu.VMEM((3, 8, LINE, 128), F32),
            pltpu.VMEM((256, 9 * CH), BF16),
            DMA((3,)),
            DMA((3,)),
            DMA((2, 2)),
            DMA((2, 16, 2)),
            DMA,
            DMA,
            DMA,
            DMA,
            DMA((9,)),
        ],
        compiler_params=pltpu.CompilerParams(
            collective_id=0, has_side_effects=True, vmem_limit_bytes=60 * 1024 * 1024
        ),
        name="attend_and_decode",
    )(
        query_states,
        key_states,
        value_states,
        base_patch,
        head_proj.T,
        latent_std.reshape(1, 16),
        latent_mean.reshape(1, 16),
        w_in.reshape(27 * 16, CH),
        b_in,
        gain_mid,
        w_up.transpose(0, 1, 3, 2).reshape(9 * OUTCH, CH),
        b_up.reshape(1, OUTCH),
    )
    return planes.reshape(2, 4, 32, OUTCH)


def solution(mesh):
    in_specs = (
        P(("seq", "head"), None),
        P(("seq", "head"), None),
        P(("seq", "head"), None),
        P(("seq", "head"), None),
        P("head", None),
        P(),
        P(),
        P(),
        P(),
        P(),
        P(),
        P(),
    )
    out_specs = P("head", "seq", None, None)
    return jax.shard_map(
        on_device, mesh=mesh, in_specs=in_specs, out_specs=out_specs, check_vma=False
    )
```

```python
import math

import jax
import jax.numpy as jnp
from jax import lax
from jax.experimental import pallas as pl
from jax.experimental.pallas import tpu as pltpu
from jax.sharding import PartitionSpec as P

MESH = pl.DeviceIdType.MESH
F32, BF16 = jnp.float32, jnp.bfloat16

SEQ, GROUPS = 64, 8
ROWS = 4
PLACES = ROWS * GROUPS
OWN = 16
ROW = OWN * GROUPS
PLANE = ROW * ROWS
HD, LOCAL = 128, 3
WIDE = HD * LOCAL
PATCH = 64
NUM = PATCH * LOCAL
MSG = 256
TALL = PATCH + 8
CH, OUTCH = 384, 192
EDGE = 8
LINE = 48
TO_LOG2 = math.log2(math.e) / math.sqrt(HD)


def dot(a, b, dims):
    return lax.dot_general(a, b, (dims, ((), ())), preferred_element_type=F32)


def kernel(
    q_in, k_in, v_in, base_far, proj_far, std_far, mean_far, w_in_far, b_in_far, gain_far, w_up_far, b_up_far,
    out_ref,
    keys, values, v_row, queries, turned_queries, top, fade, weighted, summed, turned, sending, parts, lat_own, lat_near,
    base_ref, proj_ref, std_ref, mean_ref, w_in, b_in_ref, gain_ref, w_up, b_up_ref, w_two, enlarged, columns,
    plane_send, plane_recv, ring_send, ring_recv, part_send, part_recv, near_send, near_recv, weight_sem,
):
    s, g = lax.axis_index("seq"), lax.axis_index("head")
    z, row = s // ROWS, s % ROWS
    place = row * GROUPS + g
    up, down = ((s + ROWS) % SEQ, g), ((s + SEQ - ROWS) % SEQ, g)
    after, before = (s + 1) % SEQ, (s + SEQ - 1) % SEQ
    next_g, last_g = (g + 1) % GROUPS, (g + GROUPS - 1) % GROUPS

    def peer(i):
        other = (place + i) % PLACES
        return other, (z * ROWS + other // GROUPS, other % GROUPS)

    def columns_of(group):
        return pl.ds(pl.multiple_of(group * WIDE, WIDE), WIDE)

    def tokens_of(index):
        return pl.ds(pl.multiple_of(index * OWN, OWN), OWN)

    barrier = pltpu.get_barrier_semaphore()

    for i in range(1, PLACES):
        pl.semaphore_signal(barrier, inc=1, device_id=peer(i)[1], device_id_type=MESH)
    for other in (up, down, (after, g), (before, g), (after, last_g), (before, last_g)):
        pl.semaphore_signal(barrier, inc=1, device_id=other, device_id_type=MESH)

    q_row = queries.at[pl.ds(pl.multiple_of(row * ROW, ROW), ROW)]
    rows_of = ((k_in, keys.at[0]), (v_in, v_row), (q_in, q_row))
    for kind, (source, target) in enumerate(rows_of):
        pltpu.make_async_copy(source.at[:, columns_of(g)], target.at[tokens_of(g)], plane_recv.at[kind]).start()
    proj_in = pltpu.make_async_copy(proj_far, proj_ref, weight_sem.at[8])
    proj_in.start()
    pl.semaphore_wait(barrier, PLACES - 1 + 6)

    for kind, (source, target) in enumerate(rows_of):
        for i in range(1, GROUPS):
            other = (g + i) % GROUPS
            pltpu.make_async_remote_copy(
                src_ref=source.at[:, columns_of(other)],
                dst_ref=target.at[tokens_of(g)],
                send_sem=plane_send.at[kind],
                recv_sem=plane_recv.at[kind],
                device_id=(s, other),
                device_id_type=MESH,
            ).start()

    def portion(kind, slot, part):
        return values.at[slot] if kind else keys.at[slot, pl.ds(part * ROW // 2, ROW // 2)]

    def hop(kind, source, target, way, part):
        pltpu.make_async_remote_copy(
            src_ref=portion(kind, source, part),
            dst_ref=portion(kind, target, part),
            send_sem=ring_send.at[way, kind],
            recv_sem=ring_recv.at[kind, target, part],
            device_id=(up, down)[way],
            device_id_type=MESH,
        ).start()

    def arrived(kind, slot, part):
        pltpu.make_async_copy(
            portion(kind, slot, part), portion(kind, slot, part), ring_recv.at[kind, slot, part]
        ).wait()

    for kind, (source, target) in enumerate(rows_of[:2]):
        pltpu.make_async_copy(target, target, plane_recv.at[kind]).wait()
        if kind == 1:
            proj_in.wait()
            for h in range(LOCAL):
                lanes = slice(h * HD, h * HD + HD)
                values[0, h * PATCH : h * PATCH + PATCH, :] = dot(
                    proj_ref[:, lanes], v_row[:, lanes], ((1,), (1,))
                ).astype(BF16)
        for part in range(2 - kind):
            hop(kind, 0, 1, 0, part)
            hop(kind, 0, 9, 1, part)

    pltpu.make_async_copy(q_row, q_row, plane_recv.at[2]).wait()
    for i in range(1, ROWS):
        pltpu.make_async_remote_copy(
            src_ref=q_row,
            dst_ref=q_row,
            send_sem=plane_send.at[3],
            recv_sem=plane_recv.at[3],
            device_id=(z * ROWS + (row + i) % ROWS, g),
            device_id_type=MESH,
        ).start()

    parameters = [
        pltpu.make_async_copy(source, target, weight_sem.at[i])
        for i, (source, target) in enumerate(
            (
                (w_in_far, w_in),
                (w_up_far, w_up),
                (base_far, base_ref),
                (std_far, std_ref),
                (mean_far, mean_ref),
                (b_in_far, b_in_ref),
                (gain_far, gain_ref),
                (b_up_far, b_up_ref),
            )
        )
    ]
    for copy in parameters:
        copy.start()

    for copy in parameters:
        copy.wait()
    w_two[...] = jnp.zeros_like(w_two)
    for t in range(3):
        for u in range(3):
            piece = w_in[(t * 3 + u) * 48 : (t * 3 + u) * 48 + 48, :]
            for half in range(2):
                at = t * 256 + (u + half) * 64
                w_two[at : at + 48, half * CH : half * CH + CH] = piece
    enlarged[...] = jnp.zeros_like(enlarged)
    turned[...] = jnp.zeros_like(turned)

    def joined(pieces, axis):
        return pieces[0] if len(pieces) == 1 else jnp.concatenate(pieces, axis=axis)

    units = [
        (h, slice(h * HD, h * HD + HD), slice(c * 256, c * 256 + 256)) for h in range(LOCAL) for c in range(2)
    ]

    def add_up(slots, chosen, first=False):
        for h, lanes, some in chosen:
            some_values = joined([values[slot, h * PATCH : h * PATCH + PATCH, :] for slot in slots], 1)
            some_values = jnp.concatenate([some_values, jnp.ones((16, len(slots) * ROW), BF16)], axis=0)
            product = dot(some_values, weighted[h, : len(slots) * ROW, some], ((1,), (0,)))[:TALL]
            rows = slice(h * TALL, h * TALL + TALL)
            summed[rows, some] = product if first else summed[rows, some] * fade[h : h + 1, some] + product

    def attend(earlier, slots, chosen):
        scores = [
            dot(joined([keys[slot, :, lanes] for slot in slots], 0), turned_queries[lanes, some], ((1,), (0,)))
            for h, lanes, some in chosen
        ]
        first = earlier == []
        if earlier:
            add_up(earlier, chosen, first=earlier == [0])
        for (h, lanes, some), score in zip(chosen, scores):
            new = jnp.max(score, axis=0, keepdims=True)
            if not first:
                old = top[h : h + 1, some]
                new = jnp.maximum(old, new)
                fading = jnp.exp2((old - new) * TO_LOG2)
                fade[h : h + 1, some] = fading
            weights = jnp.exp2((score - new) * TO_LOG2)
            top[h : h + 1, some] = new
            weighted[h, : len(slots) * ROW, some] = weights.astype(BF16)

    some, rest = units[:3], units[3:]

    def pass_on(kind, t, part):
        arrived(kind, t, part)
        hop(kind, t, t + 1, 0, part)
        arrived(kind, t + 8, part)
        hop(kind, t + 8, t + 9, 1, part)

    pass_on(0, 1, 0)
    pass_on(0, 1, 1)
    pass_on(1, 1, 0)
    others = queries.at[: PLANE - ROW]
    pltpu.make_async_copy(others, others, plane_recv.at[3]).wait()
    turned_queries[...] = queries[...].T
    attend([], [0], units)
    pass_on(0, 2, 0)
    pass_on(0, 2, 1)
    attend([0], [1, 9], some)
    pass_on(1, 2, 0)
    attend([0], [1, 9], rest)

    def step(t, carry):
        for event, (kind, part) in enumerate(((0, 0), (0, 1), (1, 0))):
            pass_on(kind, t, part)
            attend([t - 2, t + 6], [t - 1, t + 7], units[event * 2 : event * 2 + 2])
        return carry

    lax.fori_loop(3, 7, step, 0)
    for part in range(2):
        arrived(0, 7, part)
        hop(0, 7, 8, 0, part)
        arrived(0, 15, part)
        attend([5, 13], [6, 14], units[part * 2 : part * 2 + 2])
    arrived(1, 15, 0)
    hop(1, 15, 8, 1, 0)
    arrived(1, 7, 0)
    attend([5, 13], [6, 14], units[4:])
    attend([6, 14], [7, 15], units)
    add_up([7, 15], units)
    for part in range(2):
        arrived(0, 8, part)
    attend(None, [8], units)
    arrived(1, 8, 0)
    add_up([8], units)

    for h in range(LOCAL):
        sums = summed[h * TALL + PATCH : h * TALL + PATCH + 1, :]
        turned[h * PATCH : h * PATCH + PATCH, :] = summed[h * TALL : h * TALL + PATCH, :] * (1.0 / sums)
        level = top[h : h + 1, :] * TO_LOG2 + jnp.log(sums) * math.log2(math.e)
        for term in range(3):
            rounded = level.astype(BF16).astype(F32)
            turned[NUM + term * LOCAL + h : NUM + term * LOCAL + h + 1, :] = rounded
            level = level - rounded
    for away in (1, 2, 3, 0):
        to_row = (row + away) % ROWS
        lanes = pl.ds(pl.multiple_of(to_row * ROW, ROW), ROW)
        sending[lanes, :] = turned[:, lanes].astype(BF16).T
        if away == 0:
            pltpu.make_async_copy(sending.at[tokens_of(place)], parts.at[tokens_of(place)], part_recv).start()
        for i in range(0 if away else 1, GROUPS):
            to_group = (g + i) % GROUPS
            pltpu.make_async_remote_copy(
                src_ref=sending.at[tokens_of(to_row * GROUPS + to_group)],
                dst_ref=parts.at[tokens_of(place)],
                send_sem=part_send,
                recv_sem=part_recv,
                device_id=(z * ROWS + to_row, to_group),
                device_id_type=MESH,
            ).start()

    def ones_where(shape, made):
        r = lax.broadcasted_iota(jnp.int32, shape, 0)
        c = lax.broadcasted_iota(jnp.int32, shape, 1)
        return made(r, c).astype(F32).astype(BF16)

    spread = ones_where(
        (MSG, NUM),
        lambda r, c: (r >= NUM) & (r < NUM + 3 * LOCAL) & ((r - NUM) % LOCAL == c // PATCH),
    )
    pltpu.make_async_copy(parts, parts, part_recv).wait()

    levels = dot(parts[...], spread, ((1,), (0,)))
    numbers = parts[:, :NUM].astype(F32)
    by_row = [slice(r * ROW, r * ROW + ROW) for r in range(ROWS)]
    highest = levels[by_row[0]]
    for r in range(1, ROWS):
        highest = jnp.maximum(highest, levels[by_row[r]])
    above, below = 0.0, 0.0
    for r in range(ROWS):
        share = jnp.exp2(levels[by_row[r]] - highest)
        above = above + share * numbers[by_row[r]]
        below = below + share
    merged = above / below
    tokens = merged[:OWN]
    for other in range(1, GROUPS):
        tokens = tokens + merged[other * OWN : other * OWN + OWN]
    patch = base_ref[...].astype(F32)
    for h in range(LOCAL):
        patch = patch + tokens[:, h * PATCH : h * PATCH + PATCH]
    std = jnp.concatenate([std_ref[...]] * 4, axis=1)
    mean = jnp.concatenate([mean_ref[...]] * 4, axis=1)
    latent = patch * std + mean
    lat_own[...] = jnp.concatenate([latent, latent], axis=1).astype(BF16)

    for slot, device in enumerate(((after, next_g), (after, g), (s, next_g), (before, next_g), (before, g))):
        pltpu.make_async_remote_copy(
            src_ref=lat_own,
            dst_ref=lat_near.at[slot],
            send_sem=near_send,
            recv_sem=near_recv,
            device_id=device,
            device_id_type=MESH,
        ).start()

    def picks(b):
        def made(r, c):
            a, v, low = c // 64, (c // 16) % 4, c % 16
            spot = v + 1 - b
            wanted = (spot // 2) * 64 + a * 32 + (spot % 2) * 16 + low
            return (v < 3) & (r == wanted)

        return ones_where((128, 128), made)

    pick = [picks(0), picks(1)]
    pltpu.make_async_copy(lat_near, lat_near, near_recv).wait()

    has_before = (s > 0).astype(F32)
    has_after = (s < SEQ - 1).astype(F32)
    has_frames = (g > 0).astype(F32)
    tiles = [
        [lat_near[0].astype(F32) * (has_before * has_frames), lat_near[1].astype(F32) * has_before],
        [lat_near[2].astype(F32) * has_frames, lat_own[...].astype(F32)],
        [lat_near[3].astype(F32) * (has_after * has_frames), lat_near[4].astype(F32) * has_after],
    ]
    lane = lax.broadcasted_iota(jnp.int32, (8, 128), 1)
    line = lax.broadcasted_iota(jnp.int32, (8, 128), 0)
    sides = ([], [])
    for f in range(4):
        for r in range(3):
            here = tiles[r][f // 2][(f % 2) * 8 : (f % 2) * 8 + 8]
            left = jnp.where(line == 0, 0.0, pltpu.roll(here, 1, 0))
            right = jnp.where(line == 7, 0.0, pltpu.roll(here, 7, 0))
            sides[0].append(jnp.where(lane < 64, left, here))
            sides[1].append(jnp.where(lane < 64, here, right))
    windows = [
        dot(jnp.concatenate(side, axis=0).astype(BF16), chosen, ((1,), (0,))) for side, chosen in zip(sides, pick)
    ]

    def window(f, r, b):
        at = (f * 3 + r) * 8
        return windows[b][at : at + 8]

    lines = []
    for f in range(2):
        for pair in range(2):
            for b in range(2):
                pieces = [window(f + t, pair + r, b) for t in range(3) for r in range(2)]
                lines.append(jnp.concatenate(pieces, axis=1))
    conv = dot(jnp.concatenate(lines, axis=0).astype(BF16), w_two[...], ((1,), (0,)))
    for half in range(2):
        out = conv[:, half * CH : half * CH + CH] + b_in_ref[...].reshape(1, CH)
        mean_sq = jnp.mean(out * out, axis=1, keepdims=True)
        normed = out * lax.rsqrt(mean_sq + 1e-6) * gain_ref[...].reshape(1, CH)
        active = normed / (1.0 + jnp.exp(-normed))
        for f in range(2):
            for pair in range(2):
                y = 2 * pair + half
                for b in range(2):
                    at = ((f * 2 + pair) * 2 + b) * 8
                    part = active[at : at + 8]
                    if y == 0:
                        part = part * has_before
                    if y == 3:
                        part = part * has_after
                    for twice in range(2):
                        for tile in range(3):
                            enlarged[tile, f * 4 + y, pl.ds(EDGE + 2 * b + twice, 8, stride=4), :] = part[
                                :, tile * 128 : tile * 128 + 128
                            ]

    for v in range(3):
        for f in range(2):
            for y in range(4):
                piece = [enlarged[tile, f * 4 + y, EDGE - 1 + v : EDGE + 31 + v, :] for tile in range(3)]
                piece = jnp.concatenate(piece, axis=1).astype(BF16)
                for line_out in range(4):
                    for u in range(3):
                        if (line_out + u + 1) // 2 == y:
                            at = (f * 4 + line_out) * 32
                            to = (u * 3 + v) * CH
                            columns[at : at + 32, to : to + CH] = piece
    planes = b_up_ref[...]
    for tap in range(9):
        planes = planes + dot(
            columns[:, tap * CH : tap * CH + CH], w_up[tap * OUTCH : tap * OUTCH + OUTCH, :], ((1,), (1,))
        )
    out_ref[...] = planes.astype(BF16)

    for kind in range(3):
        sent = v_row.at[: ROW - OWN]
        pltpu.make_async_copy(sent, sent, plane_send.at[kind]).wait()
    sent = queries.at[: PLANE - ROW]
    pltpu.make_async_copy(sent, sent, plane_send.at[3]).wait()
    for way, kind, ring, count in ((0, 0, keys, 8), (0, 1, values, 7), (1, 0, keys, 7), (1, 1, values, 8)):
        sent = ring.at[:count]
        pltpu.make_async_copy(sent, sent, ring_send.at[way, kind]).wait()
    sent = parts.at[: PLANE - OWN]
    pltpu.make_async_copy(sent, sent, part_send).wait()
    pltpu.make_async_copy(lat_near, lat_near, near_send).wait()


def on_device(
    query_states,
    key_states,
    value_states,
    base_patch,
    head_proj,
    latent_std,
    latent_mean,
    w_in,
    b_in,
    gain_mid,
    w_up,
    b_up,
):
    here = pl.BlockSpec(memory_space=pltpu.VMEM)
    far = pl.BlockSpec(memory_space=pltpu.HBM)
    DMA = pltpu.SemaphoreType.DMA
    planes = pl.pallas_call(
        kernel,
        out_shape=pltpu.VMEM((256, OUTCH), BF16),
        in_specs=[far] * 12,
        out_specs=here,
        scratch_shapes=[
            pltpu.VMEM((16, ROW, WIDE), BF16),
            pltpu.VMEM((16, NUM, ROW), BF16),
            pltpu.VMEM((ROW, WIDE), BF16),
            pltpu.VMEM((PLANE, WIDE), BF16),
            pltpu.VMEM((WIDE, PLANE), BF16),
            pltpu.VMEM((8, PLANE), F32),
            pltpu.VMEM((8, PLANE), F32),
            pltpu.VMEM((LOCAL, 2 * ROW, PLANE), BF16),
            pltpu.VMEM((LOCAL * TALL, PLANE), F32),
            pltpu.VMEM((MSG, PLANE), F32),
            pltpu.VMEM((PLANE, MSG), BF16),
            pltpu.VMEM((PLANE, MSG), BF16),
            pltpu.VMEM((OWN, 128), BF16),
            pltpu.VMEM((5, OWN, 128), BF16),
            pltpu.VMEM((OWN, PATCH), BF16),
            pltpu.VMEM((PATCH, WIDE), BF16),
            pltpu.VMEM((1, 16), F32),
            pltpu.VMEM((1, 16), F32),
            pltpu.VMEM((27 * 16, CH), BF16),
            pltpu.VMEM((CH,), F32),
            pltpu.VMEM((CH,), F32),
            pltpu.VMEM((9 * OUTCH, CH), BF16),
            pltpu.VMEM((1, OUTCH), F32),
            pltpu.VMEM((768, 2 * CH), BF16),
            pltpu.VMEM((3, 8, LINE, 128), F32),
            pltpu.VMEM((256, 9 * CH), BF16),
            DMA((4,)),
            DMA((4,)),
            DMA((2, 2)),
            DMA((2, 16, 2)),
            DMA,
            DMA,
            DMA,
            DMA,
            DMA((9,)),
        ],
        compiler_params=pltpu.CompilerParams(
            collective_id=0, has_side_effects=True, vmem_limit_bytes=60 * 1024 * 1024
        ),
        name="attend_and_decode",
    )(
        query_states,
        key_states,
        value_states,
        base_patch,
        head_proj.T,
        latent_std.reshape(1, 16),
        latent_mean.reshape(1, 16),
        w_in.reshape(27 * 16, CH),
        b_in,
        gain_mid,
        w_up.transpose(0, 1, 3, 2).reshape(9 * OUTCH, CH),
        b_up.reshape(1, OUTCH),
    )
    return planes.reshape(2, 4, 32, OUTCH)


def solution(mesh):
    in_specs = (
        P(("seq", "head"), None),
        P(("seq", "head"), None),
        P(("seq", "head"), None),
        P(("seq", "head"), None),
        P("head", None),
        P(),
        P(),
        P(),
        P(),
        P(),
        P(),
        P(),
    )
    out_specs = P("head", "seq", None, None)
    return jax.shard_map(
        on_device, mesh=mesh, in_specs=in_specs, out_specs=out_specs, check_vma=False
    )
```

```python
import math

import jax
import jax.numpy as jnp
from jax import lax
from jax.experimental import pallas as pl
from jax.experimental.pallas import tpu as pltpu
from jax.sharding import PartitionSpec as P

MESH = pl.DeviceIdType.MESH
F32, BF16 = jnp.float32, jnp.bfloat16

SEQ, GROUPS = 64, 8
ROWS = 4
PLACES = ROWS * GROUPS
OWN = 16
ROW = OWN * GROUPS
PLANE = ROW * ROWS
HD, LOCAL = 128, 3
WIDE = HD * LOCAL
PATCH = 64
NUM = PATCH * LOCAL
MSG = 256
TALL = PATCH + 8
CH, OUTCH = 384, 192
EDGE = 8
LINE = 48
TO_LOG2 = math.log2(math.e) / math.sqrt(HD)


def dot(a, b, dims):
    return lax.dot_general(a, b, (dims, ((), ())), preferred_element_type=F32)


def kernel(
    q_in, k_in, v_in, base_far, proj_far, std_far, mean_far, w_in_far, b_in_far, gain_far, w_up_far, b_up_far,
    out_ref,
    keys, values, v_row, queries, turned_queries, top, fade, weighted, summed, turned, sending, parts, lat_own, lat_near,
    base_ref, proj_ref, std_ref, mean_ref, w_in, b_in_ref, gain_ref, w_up, b_up_ref, w_two, enlarged, columns,
    plane_send, plane_recv, ring_send, ring_recv, part_send, part_recv, near_send, near_recv, weight_sem,
):
    s, g = lax.axis_index("seq"), lax.axis_index("head")
    z, row = s // ROWS, s % ROWS
    place = row * GROUPS + g
    up, down = ((s + ROWS) % SEQ, g), ((s + SEQ - ROWS) % SEQ, g)
    after, before = (s + 1) % SEQ, (s + SEQ - 1) % SEQ
    next_g, last_g = (g + 1) % GROUPS, (g + GROUPS - 1) % GROUPS

    def peer(i):
        other = (place + i) % PLACES
        return other, (z * ROWS + other // GROUPS, other % GROUPS)

    def columns_of(group):
        return pl.ds(pl.multiple_of(group * WIDE, WIDE), WIDE)

    def tokens_of(index):
        return pl.ds(pl.multiple_of(index * OWN, OWN), OWN)

    barrier = pltpu.get_barrier_semaphore()

    for i in range(1, PLACES):
        pl.semaphore_signal(barrier, inc=1, device_id=peer(i)[1], device_id_type=MESH)
    for other in (up, down, (after, g), (before, g), (after, last_g), (before, last_g)):
        pl.semaphore_signal(barrier, inc=1, device_id=other, device_id_type=MESH)

    q_row = queries.at[pl.ds(pl.multiple_of(row * ROW, ROW), ROW)]
    rows_of = ((k_in, keys.at[0]), (v_in, v_row), (q_in, q_row))
    for kind, (source, target) in enumerate(rows_of):
        pltpu.make_async_copy(source.at[:, columns_of(g)], target.at[tokens_of(g)], plane_recv.at[kind]).start()
    proj_in = pltpu.make_async_copy(proj_far, proj_ref, weight_sem.at[8])
    proj_in.start()
    pl.semaphore_wait(barrier, PLACES - 1 + 6)

    for kind, (source, target) in enumerate(rows_of):
        for i in range(1, GROUPS):
            other = (g + i) % GROUPS
            pltpu.make_async_remote_copy(
                src_ref=source.at[:, columns_of(other)],
                dst_ref=target.at[tokens_of(g)],
                send_sem=plane_send.at[kind],
                recv_sem=plane_recv.at[kind],
                device_id=(s, other),
                device_id_type=MESH,
            ).start()

    def portion(kind, slot, part):
        return values.at[slot] if kind else keys.at[slot, pl.ds(part * ROW // 2, ROW // 2)]

    def hop(kind, source, target, way, part):
        pltpu.make_async_remote_copy(
            src_ref=portion(kind, source, part),
            dst_ref=portion(kind, target, part),
            send_sem=ring_send.at[way, kind],
            recv_sem=ring_recv.at[kind, target, part],
            device_id=(up, down)[way],
            device_id_type=MESH,
        ).start()

    def arrived(kind, slot, part):
        pltpu.make_async_copy(
            portion(kind, slot, part), portion(kind, slot, part), ring_recv.at[kind, slot, part]
        ).wait()

    for kind, (source, target) in enumerate(rows_of[:2]):
        pltpu.make_async_copy(target, target, plane_recv.at[kind]).wait()
        if kind == 1:
            proj_in.wait()
            for h in range(LOCAL):
                lanes = slice(h * HD, h * HD + HD)
                values[0, h * PATCH : h * PATCH + PATCH, :] = dot(
                    proj_ref[:, lanes], v_row[:, lanes], ((1,), (1,))
                ).astype(BF16)
        for part in range(2 - kind):
            hop(kind, 0, 1, 0, part)
            hop(kind, 0, 9, 1, part)

    pltpu.make_async_copy(q_row, q_row, plane_recv.at[2]).wait()
    for i in range(1, ROWS):
        pltpu.make_async_remote_copy(
            src_ref=q_row,
            dst_ref=q_row,
            send_sem=plane_send.at[3],
            recv_sem=plane_recv.at[3],
            device_id=(z * ROWS + (row + i) % ROWS, g),
            device_id_type=MESH,
        ).start()

    parameters = [
        pltpu.make_async_copy(source, target, weight_sem.at[i])
        for i, (source, target) in enumerate(
            (
                (w_in_far, w_in),
                (w_up_far, w_up),
                (base_far, base_ref),
                (std_far, std_ref),
                (mean_far, mean_ref),
                (b_in_far, b_in_ref),
                (gain_far, gain_ref),
                (b_up_far, b_up_ref),
            )
        )
    ]
    for copy in parameters:
        copy.start()

    for copy in parameters:
        copy.wait()
    w_two[...] = jnp.zeros_like(w_two)
    for t in range(3):
        for u in range(3):
            piece = w_in[(t * 3 + u) * 48 : (t * 3 + u) * 48 + 48, :]
            for half in range(2):
                at = t * 256 + (u + half) * 64
                w_two[at : at + 48, half * CH : half * CH + CH] = piece
    enlarged[...] = jnp.zeros_like(enlarged)
    turned[...] = jnp.zeros_like(turned)

    def joined(pieces, axis):
        return pieces[0] if len(pieces) == 1 else jnp.concatenate(pieces, axis=axis)

    units = [
        (h, slice(h * HD, h * HD + HD), slice(c * 256, c * 256 + 256)) for h in range(LOCAL) for c in range(2)
    ]

    def add_up(slots, chosen, first=False):
        for h, lanes, some in chosen:
            some_values = joined([values[slot, h * PATCH : h * PATCH + PATCH, :] for slot in slots], 1)
            some_values = jnp.concatenate([some_values, jnp.ones((16, len(slots) * ROW), BF16)], axis=0)
            product = dot(some_values, weighted[h, : len(slots) * ROW, some], ((1,), (0,)))[:TALL]
            rows = slice(h * TALL, h * TALL + TALL)
            summed[rows, some] = product if first else summed[rows, some] * fade[h : h + 1, some] + product

    def attend(earlier, slots, chosen):
        scores = [
            dot(joined([keys[slot, :, lanes] for slot in slots], 0), turned_queries[lanes, some], ((1,), (0,)))
            for h, lanes, some in chosen
        ]
        first = earlier == []
        if earlier:
            add_up(earlier, chosen, first=earlier == [0])
        for (h, lanes, some), score in zip(chosen, scores):
            new = jnp.max(score, axis=0, keepdims=True)
            if not first:
                old = top[h : h + 1, some]
                new = jnp.maximum(old, new)
                fading = jnp.exp2((old - new) * TO_LOG2)
                fade[h : h + 1, some] = fading
            weights = jnp.exp2((score - new) * TO_LOG2)
            top[h : h + 1, some] = new
            weighted[h, : len(slots) * ROW, some] = weights.astype(BF16)

    some, rest = units[:3], units[3:]

    def pass_on(kind, t, part):
        arrived(kind, t, part)
        hop(kind, t, t + 1, 0, part)
        arrived(kind, t + 8, part)
        hop(kind, t + 8, t + 9, 1, part)

    pass_on(0, 1, 0)
    pass_on(0, 1, 1)
    pass_on(1, 1, 0)
    others = queries.at[: PLANE - ROW]
    pltpu.make_async_copy(others, others, plane_recv.at[3]).wait()
    turned_queries[...] = queries[...].T
    attend([], [0], units)
    pass_on(0, 2, 0)
    pass_on(0, 2, 1)
    attend([0], [1, 9], some)
    pass_on(1, 2, 0)
    attend([0], [1, 9], rest)

    def step(t, carry):
        pass_on(0, t, 0)
        pass_on(0, t, 1)
        attend([t - 2, t + 6], [t - 1, t + 7], some)
        pass_on(1, t, 0)
        attend([t - 2, t + 6], [t - 1, t + 7], rest)
        return carry

    lax.fori_loop(3, 7, step, 0)
    for part in range(2):
        arrived(0, 7, part)
        hop(0, 7, 8, 0, part)
        arrived(0, 15, part)
    attend([5, 13], [6, 14], some)
    arrived(1, 15, 0)
    hop(1, 15, 8, 1, 0)
    arrived(1, 7, 0)
    attend([5, 13], [6, 14], rest)
    attend([6, 14], [7, 15], units)
    add_up([7, 15], units)
    for part in range(2):
        arrived(0, 8, part)
    attend(None, [8], units)
    arrived(1, 8, 0)
    add_up([8], units)

    for h in range(LOCAL):
        sums = summed[h * TALL + PATCH : h * TALL + PATCH + 1, :]
        turned[h * PATCH : h * PATCH + PATCH, :] = summed[h * TALL : h * TALL + PATCH, :] * (1.0 / sums)
        level = top[h : h + 1, :] * TO_LOG2 + jnp.log(sums) * math.log2(math.e)
        for term in range(3):
            rounded = level.astype(BF16).astype(F32)
            turned[NUM + term * LOCAL + h : NUM + term * LOCAL + h + 1, :] = rounded
            level = level - rounded
    for away in (1, 2, 3, 0):
        to_row = (row + away) % ROWS
        lanes = pl.ds(pl.multiple_of(to_row * ROW, ROW), ROW)
        sending[lanes, :] = turned[:, lanes].astype(BF16).T
        if away == 0:
            pltpu.make_async_copy(sending.at[tokens_of(place)], parts.at[tokens_of(place)], part_recv).start()
        for i in range(0 if away else 1, GROUPS):
            to_group = (g + i) % GROUPS
            pltpu.make_async_remote_copy(
                src_ref=sending.at[tokens_of(to_row * GROUPS + to_group)],
                dst_ref=parts.at[tokens_of(place)],
                send_sem=part_send,
                recv_sem=part_recv,
                device_id=(z * ROWS + to_row, to_group),
                device_id_type=MESH,
            ).start()

    def ones_where(shape, made):
        r = lax.broadcasted_iota(jnp.int32, shape, 0)
        c = lax.broadcasted_iota(jnp.int32, shape, 1)
        return made(r, c).astype(F32).astype(BF16)

    spread = ones_where(
        (MSG, NUM),
        lambda r, c: (r >= NUM) & (r < NUM + 3 * LOCAL) & ((r - NUM) % LOCAL == c // PATCH),
    )
    pltpu.make_async_copy(parts, parts, part_recv).wait()

    levels = dot(parts[...], spread, ((1,), (0,)))
    numbers = parts[:, :NUM].astype(F32)
    by_row = [slice(r * ROW, r * ROW + ROW) for r in range(ROWS)]
    highest = levels[by_row[0]]
    for r in range(1, ROWS):
        highest = jnp.maximum(highest, levels[by_row[r]])
    above, below = 0.0, 0.0
    for r in range(ROWS):
        share = jnp.exp2(levels[by_row[r]] - highest)
        above = above + share * numbers[by_row[r]]
        below = below + share
    merged = above / below
    tokens = merged[:OWN]
    for other in range(1, GROUPS):
        tokens = tokens + merged[other * OWN : other * OWN + OWN]
    patch = base_ref[...].astype(F32)
    for h in range(LOCAL):
        patch = patch + tokens[:, h * PATCH : h * PATCH + PATCH]
    std = jnp.concatenate([std_ref[...]] * 4, axis=1)
    mean = jnp.concatenate([mean_ref[...]] * 4, axis=1)
    latent = patch * std + mean
    lat_own[...] = jnp.concatenate([latent, latent], axis=1).astype(BF16)

    for slot, device in enumerate(((after, next_g), (after, g), (s, next_g), (before, next_g), (before, g))):
        pltpu.make_async_remote_copy(
            src_ref=lat_own,
            dst_ref=lat_near.at[slot],
            send_sem=near_send,
            recv_sem=near_recv,
            device_id=device,
            device_id_type=MESH,
        ).start()

    def picks(b):
        def made(r, c):
            a, v, low = c // 64, (c // 16) % 4, c % 16
            spot = v + 1 - b
            wanted = (spot // 2) * 64 + a * 32 + (spot % 2) * 16 + low
            return (v < 3) & (r == wanted)

        return ones_where((128, 128), made)

    pick = [picks(0), picks(1)]
    pltpu.make_async_copy(lat_near, lat_near, near_recv).wait()

    has_before = (s > 0).astype(F32)
    has_after = (s < SEQ - 1).astype(F32)
    has_frames = (g > 0).astype(F32)
    tiles = [
        [lat_near[0].astype(F32) * (has_before * has_frames), lat_near[1].astype(F32) * has_before],
        [lat_near[2].astype(F32) * has_frames, lat_own[...].astype(F32)],
        [lat_near[3].astype(F32) * (has_after * has_frames), lat_near[4].astype(F32) * has_after],
    ]
    lane = lax.broadcasted_iota(jnp.int32, (8, 128), 1)
    line = lax.broadcasted_iota(jnp.int32, (8, 128), 0)
    sides = ([], [])
    for f in range(4):
        for r in range(3):
            here = tiles[r][f // 2][(f % 2) * 8 : (f % 2) * 8 + 8]
            left = jnp.where(line == 0, 0.0, pltpu.roll(here, 1, 0))
            right = jnp.where(line == 7, 0.0, pltpu.roll(here, 7, 0))
            sides[0].append(jnp.where(lane < 64, left, here))
            sides[1].append(jnp.where(lane < 64, here, right))
    windows = [
        dot(jnp.concatenate(side, axis=0).astype(BF16), chosen, ((1,), (0,))) for side, chosen in zip(sides, pick)
    ]

    def window(f, r, b):
        at = (f * 3 + r) * 8
        return windows[b][at : at + 8]

    lines = []
    for f in range(2):
        for pair in range(2):
            for b in range(2):
                pieces = [window(f + t, pair + r, b) for t in range(3) for r in range(2)]
                lines.append(jnp.concatenate(pieces, axis=1))
    conv = dot(jnp.concatenate(lines, axis=0).astype(BF16), w_two[...], ((1,), (0,)))
    for half in range(2):
        out = conv[:, half * CH : half * CH + CH] + b_in_ref[...].reshape(1, CH)
        mean_sq = jnp.mean(out * out, axis=1, keepdims=True)
        normed = out * lax.rsqrt(mean_sq + 1e-6) * gain_ref[...].reshape(1, CH)
        active = normed / (1.0 + jnp.exp(-normed))
        for f in range(2):
            for pair in range(2):
                y = 2 * pair + half
                for b in range(2):
                    at = ((f * 2 + pair) * 2 + b) * 8
                    part = active[at : at + 8]
                    if y == 0:
                        part = part * has_before
                    if y == 3:
                        part = part * has_after
                    for twice in range(2):
                        for tile in range(3):
                            enlarged[tile, f * 4 + y, pl.ds(EDGE + 2 * b + twice, 8, stride=4), :] = part[
                                :, tile * 128 : tile * 128 + 128
                            ]

    for v in range(3):
        for f in range(2):
            for y in range(4):
                piece = [enlarged[tile, f * 4 + y, EDGE - 1 + v : EDGE + 31 + v, :] for tile in range(3)]
                piece = jnp.concatenate(piece, axis=1).astype(BF16)
                for line_out in range(4):
                    for u in range(3):
                        if (line_out + u + 1) // 2 == y:
                            at = (f * 4 + line_out) * 32
                            to = (u * 3 + v) * CH
                            columns[at : at + 32, to : to + CH] = piece
    planes = b_up_ref[...]
    for tap in range(9):
        planes = planes + dot(
            columns[:, tap * CH : tap * CH + CH], w_up[tap * OUTCH : tap * OUTCH + OUTCH, :], ((1,), (1,))
        )
    out_ref[...] = planes.astype(BF16)

    for kind in range(3):
        sent = v_row.at[: ROW - OWN]
        pltpu.make_async_copy(sent, sent, plane_send.at[kind]).wait()
    sent = queries.at[: PLANE - ROW]
    pltpu.make_async_copy(sent, sent, plane_send.at[3]).wait()
    for way, kind, ring, count in ((0, 0, keys, 8), (0, 1, values, 7), (1, 0, keys, 7), (1, 1, values, 8)):
        sent = ring.at[:count]
        pltpu.make_async_copy(sent, sent, ring_send.at[way, kind]).wait()
    sent = parts.at[: PLANE - OWN]
    pltpu.make_async_copy(sent, sent, part_send).wait()
    pltpu.make_async_copy(lat_near, lat_near, near_send).wait()


def on_device(
    query_states,
    key_states,
    value_states,
    base_patch,
    head_proj,
    latent_std,
    latent_mean,
    w_in,
    b_in,
    gain_mid,
    w_up,
    b_up,
):
    here = pl.BlockSpec(memory_space=pltpu.VMEM)
    far = pl.BlockSpec(memory_space=pltpu.HBM)
    DMA = pltpu.SemaphoreType.DMA
    planes = pl.pallas_call(
        kernel,
        out_shape=pltpu.VMEM((256, OUTCH), BF16),
        in_specs=[far] * 12,
        out_specs=here,
        scratch_shapes=[
            pltpu.VMEM((16, ROW, WIDE), BF16),
            pltpu.VMEM((16, NUM, ROW), BF16),
            pltpu.VMEM((ROW, WIDE), BF16),
            pltpu.VMEM((PLANE, WIDE), BF16),
            pltpu.VMEM((WIDE, PLANE), BF16),
            pltpu.VMEM((8, PLANE), F32),
            pltpu.VMEM((8, PLANE), F32),
            pltpu.VMEM((LOCAL, 2 * ROW, PLANE), BF16),
            pltpu.VMEM((LOCAL * TALL, PLANE), F32),
            pltpu.VMEM((MSG, PLANE), F32),
            pltpu.VMEM((PLANE, MSG), BF16),
            pltpu.VMEM((PLANE, MSG), BF16),
            pltpu.VMEM((OWN, 128), BF16),
            pltpu.VMEM((5, OWN, 128), BF16),
            pltpu.VMEM((OWN, PATCH), BF16),
            pltpu.VMEM((PATCH, WIDE), BF16),
            pltpu.VMEM((1, 16), F32),
            pltpu.VMEM((1, 16), F32),
            pltpu.VMEM((27 * 16, CH), BF16),
            pltpu.VMEM((CH,), F32),
            pltpu.VMEM((CH,), F32),
            pltpu.VMEM((9 * OUTCH, CH), BF16),
            pltpu.VMEM((1, OUTCH), F32),
            pltpu.VMEM((768, 2 * CH), BF16),
            pltpu.VMEM((3, 8, LINE, 128), F32),
            pltpu.VMEM((256, 9 * CH), BF16),
            DMA((4,)),
            DMA((4,)),
            DMA((2, 2)),
            DMA((2, 16, 2)),
            DMA,
            DMA,
            DMA,
            DMA,
            DMA((9,)),
        ],
        compiler_params=pltpu.CompilerParams(
            collective_id=0, has_side_effects=True, vmem_limit_bytes=60 * 1024 * 1024
        ),
        name="attend_and_decode",
    )(
        query_states,
        key_states,
        value_states,
        base_patch,
        head_proj.T,
        latent_std.reshape(1, 16),
        latent_mean.reshape(1, 16),
        w_in.reshape(27 * 16, CH),
        b_in,
        gain_mid,
        w_up.transpose(0, 1, 3, 2).reshape(9 * OUTCH, CH),
        b_up.reshape(1, OUTCH),
    )
    return planes.reshape(2, 4, 32, OUTCH)


def solution(mesh):
    in_specs = (
        P(("seq", "head"), None),
        P(("seq", "head"), None),
        P(("seq", "head"), None),
        P(("seq", "head"), None),
        P("head", None),
        P(),
        P(),
        P(),
        P(),
        P(),
        P(),
        P(),
    )
    out_specs = P("head", "seq", None, None)
    return jax.shard_map(
        on_device, mesh=mesh, in_specs=in_specs, out_specs=out_specs, check_vma=False
    )
```

```python
import math

import jax
import jax.numpy as jnp
from jax import lax
from jax.experimental import pallas as pl
from jax.experimental.pallas import tpu as pltpu
from jax.sharding import PartitionSpec as P

MESH = pl.DeviceIdType.MESH
F32, BF16 = jnp.float32, jnp.bfloat16

SEQ, GROUPS = 64, 8
ROWS = 4
PLACES = ROWS * GROUPS
OWN = 16
ROW = OWN * GROUPS
PLANE = ROW * ROWS
HD, LOCAL = 128, 3
WIDE = HD * LOCAL
PATCH = 64
NUM = PATCH * LOCAL
MSG = 256
TALL = PATCH + 8
CH, OUTCH = 384, 192
EDGE = 8
LINE = 48
TO_LOG2 = math.log2(math.e) / math.sqrt(HD)


def dot(a, b, dims):
    return lax.dot_general(a, b, (dims, ((), ())), preferred_element_type=F32)


def kernel(
    q_in, k_in, v_in, base_far, proj_far, std_far, mean_far, w_in_far, b_in_far, gain_far, w_up_far, b_up_far,
    out_ref,
    keys, values, v_row, queries, turned_queries, top, fade, weighted, summed, turned, sending, parts, lat_own, lat_near,
    base_ref, proj_ref, std_ref, mean_ref, w_in, b_in_ref, gain_ref, w_up, b_up_ref, w_two, enlarged, columns, spread, pick, affine,
    plane_send, plane_recv, ring_send, ring_recv, part_send, part_recv, near_send, near_recv, weight_sem,
):
    s, g = lax.axis_index("seq"), lax.axis_index("head")
    z, row = s // ROWS, s % ROWS
    place = row * GROUPS + g
    up, down = ((s + ROWS) % SEQ, g), ((s + SEQ - ROWS) % SEQ, g)
    after, before = (s + 1) % SEQ, (s + SEQ - 1) % SEQ
    next_g, last_g = (g + 1) % GROUPS, (g + GROUPS - 1) % GROUPS

    def peer(i):
        other = (place + i) % PLACES
        return other, (z * ROWS + other // GROUPS, other % GROUPS)

    def columns_of(group):
        return pl.ds(pl.multiple_of(group * WIDE, WIDE), WIDE)

    def tokens_of(index):
        return pl.ds(pl.multiple_of(index * OWN, OWN), OWN)

    barrier = pltpu.get_barrier_semaphore()

    for i in range(1, PLACES):
        pl.semaphore_signal(barrier, inc=1, device_id=peer(i)[1], device_id_type=MESH)
    for other in (up, down, (after, g), (before, g), (after, last_g), (before, last_g)):
        pl.semaphore_signal(barrier, inc=1, device_id=other, device_id_type=MESH)

    q_row = queries.at[pl.ds(pl.multiple_of(row * ROW, ROW), ROW)]
    rows_of = ((k_in, keys.at[0]), (v_in, v_row), (q_in, q_row))
    proj_in = pltpu.make_async_copy(proj_far, proj_ref, weight_sem.at[8])
    proj_in.start()
    pl.semaphore_wait(barrier, PLACES - 1 + 6)

    for kind, (source, target) in enumerate(rows_of):
        for i in range(1, GROUPS):
            other = (g + i) % GROUPS
            pltpu.make_async_remote_copy(
                src_ref=source.at[:, columns_of(other)],
                dst_ref=target.at[tokens_of(g)],
                send_sem=plane_send.at[kind],
                recv_sem=plane_recv.at[kind],
                device_id=(s, other),
                device_id_type=MESH,
            ).start()
        pltpu.make_async_copy(source.at[:, columns_of(g)], target.at[tokens_of(g)], plane_recv.at[kind]).start()

    def portion(kind, slot, part):
        return values.at[slot] if kind else keys.at[slot, pl.ds(part * ROW // 2, ROW // 2)]

    def hop(kind, source, target, way, part):
        pltpu.make_async_remote_copy(
            src_ref=portion(kind, source, part),
            dst_ref=portion(kind, target, part),
            send_sem=ring_send.at[way, kind],
            recv_sem=ring_recv.at[kind, target, part],
            device_id=(up, down)[way],
            device_id_type=MESH,
        ).start()

    def arrived(kind, slot, part):
        pltpu.make_async_copy(
            portion(kind, slot, part), portion(kind, slot, part), ring_recv.at[kind, slot, part]
        ).wait()

    for kind, (source, target) in enumerate(rows_of[:2]):
        pltpu.make_async_copy(target, target, plane_recv.at[kind]).wait()
        if kind == 1:
            proj_in.wait()
            for h in range(LOCAL):
                lanes = slice(h * HD, h * HD + HD)
                values[0, h * PATCH : h * PATCH + PATCH, :] = dot(
                    proj_ref[:, lanes], v_row[:, lanes], ((1,), (1,))
                ).astype(BF16)
        for part in range(2 - kind):
            hop(kind, 0, 1, 0, part)
            hop(kind, 0, 9, 1, part)

    pltpu.make_async_copy(q_row, q_row, plane_recv.at[2]).wait()
    for i in range(1, ROWS):
        pltpu.make_async_remote_copy(
            src_ref=q_row,
            dst_ref=q_row,
            send_sem=plane_send.at[3],
            recv_sem=plane_recv.at[3],
            device_id=(z * ROWS + (row + i) % ROWS, g),
            device_id_type=MESH,
        ).start()

    parameters = [
        pltpu.make_async_copy(source, target, weight_sem.at[i])
        for i, (source, target) in enumerate(
            (
                (w_in_far, w_in),
                (w_up_far, w_up),
                (base_far, base_ref),
                (std_far, std_ref),
                (mean_far, mean_ref),
                (b_in_far, b_in_ref),
                (gain_far, gain_ref),
                (b_up_far, b_up_ref),
            )
        )
    ]
    for copy in parameters:
        copy.start()

    for copy in parameters:
        copy.wait()
    w_two[...] = jnp.zeros_like(w_two)
    for t in range(3):
        for u in range(3):
            piece = w_in[(t * 3 + u) * 48 : (t * 3 + u) * 48 + 48, :]
            for half in range(2):
                at = t * 256 + (u + half) * 64
                w_two[at : at + 48, half * CH : half * CH + CH] = piece

    enlarged[...] = jnp.zeros_like(enlarged)
    turned[...] = jnp.zeros_like(turned)

    def joined(pieces, axis):
        return pieces[0] if len(pieces) == 1 else jnp.concatenate(pieces, axis=axis)

    units = [
        (h, slice(h * HD, h * HD + HD), slice(c * 256, c * 256 + 256)) for h in range(LOCAL) for c in range(2)
    ]

    def add_up(slots, chosen, first=False):
        for h, lanes, some in chosen:
            some_values = joined([values[slot, h * PATCH : h * PATCH + PATCH, :] for slot in slots], 1)
            some_values = jnp.concatenate([some_values, jnp.ones((16, len(slots) * ROW), BF16)], axis=0)
            product = dot(some_values, weighted[h, : len(slots) * ROW, some], ((1,), (0,)))[:TALL]
            rows = slice(h * TALL, h * TALL + TALL)
            summed[rows, some] = product if first else summed[rows, some] * fade[h : h + 1, some] + product

    def attend(earlier, slots, chosen):
        scores = [
            dot(joined([keys[slot, :, lanes] for slot in slots], 0), turned_queries[lanes, some], ((1,), (0,)))
            for h, lanes, some in chosen
        ]
        first = earlier == []
        if earlier:
            add_up(earlier, chosen, first=earlier == [0])
        for (h, lanes, some), score in zip(chosen, scores):
            new = jnp.max(score, axis=0, keepdims=True)
            if not first:
                old = top[h : h + 1, some]
                new = jnp.maximum(old, new)
                fading = jnp.exp2((old - new) * TO_LOG2)
                fade[h : h + 1, some] = fading
            weights = jnp.exp2((score - new) * TO_LOG2)
            top[h : h + 1, some] = new
            weighted[h, : len(slots) * ROW, some] = weights.astype(BF16)

    some, rest = units[:3], units[3:]

    def pass_on(kind, t, part):
        arrived(kind, t, part)
        hop(kind, t, t + 1, 0, part)
        arrived(kind, t + 8, part)
        hop(kind, t + 8, t + 9, 1, part)

    pass_on(0, 1, 0)
    pass_on(0, 1, 1)
    pass_on(1, 1, 0)

    def ones_where(shape, made):
        r = lax.broadcasted_iota(jnp.int32, shape, 0)
        c = lax.broadcasted_iota(jnp.int32, shape, 1)
        return made(r, c).astype(F32).astype(BF16)

    spread[...] = ones_where(
        (MSG, NUM),
        lambda r, c: (r >= NUM) & (r < NUM + 3 * LOCAL) & ((r - NUM) % LOCAL == c // PATCH),
    )
    def picks(b):
        def made(r, c):
            a, v, low = c // 64, (c // 16) % 4, c % 16
            spot = v + 1 - b
            wanted = (spot // 2) * 64 + a * 32 + (spot % 2) * 16 + low
            return (v < 3) & (r == wanted)

        return ones_where((128, 128), made)

    pick[0] = picks(0)
    pick[1] = picks(1)
    for i, ref in enumerate((std_ref, mean_ref)):
        affine[i : i + 1, :PATCH] = jnp.concatenate([ref[...]] * 4, axis=1)

    others = queries.at[: PLANE - ROW]
    pltpu.make_async_copy(others, others, plane_recv.at[3]).wait()
    turned_queries[...] = queries[...].T
    attend([], [0], units)
    pass_on(0, 2, 0)
    pass_on(0, 2, 1)
    attend([0], [1, 9], some)
    pass_on(1, 2, 0)
    attend([0], [1, 9], rest)

    def step(t, carry):
        for event, (kind, part) in enumerate(((0, 0), (0, 1), (1, 0))):
            pass_on(kind, t, part)
            attend([t - 2, t + 6], [t - 1, t + 7], units[event * 2 : event * 2 + 2])
        return carry

    lax.fori_loop(3, 7, step, 0)
    for part in range(2):
        arrived(0, 7, part)
        hop(0, 7, 8, 0, part)
        arrived(0, 15, part)
        attend([5, 13], [6, 14], units[part * 2 : part * 2 + 2])
    arrived(1, 15, 0)
    hop(1, 15, 8, 1, 0)
    arrived(1, 7, 0)
    attend([5, 13], [6, 14], units[4:])
    attend([6, 14], [7, 15], units)
    add_up([7, 15], units)
    for part in range(2):
        arrived(0, 8, part)
    attend(None, [8], units)
    arrived(1, 8, 0)
    add_up([8], units)

    for h in range(LOCAL):
        sums = summed[h * TALL + PATCH : h * TALL + PATCH + 1, :]
        turned[h * PATCH : h * PATCH + PATCH, :] = summed[h * TALL : h * TALL + PATCH, :] * (1.0 / sums)
        level = top[h : h + 1, :] * TO_LOG2 + jnp.log(sums) * math.log2(math.e)
        for term in range(3):
            rounded = level.astype(BF16).astype(F32)
            turned[NUM + term * LOCAL + h : NUM + term * LOCAL + h + 1, :] = rounded
            level = level - rounded
    for away in (1, 2, 3, 0):
        to_row = (row + away) % ROWS
        lanes = pl.ds(pl.multiple_of(to_row * ROW, ROW), ROW)
        sending[lanes, :] = turned[:, lanes].astype(BF16).T
        if away == 0:
            pltpu.make_async_copy(sending.at[tokens_of(place)], parts.at[tokens_of(place)], part_recv).start()
        for i in range(0 if away else 1, GROUPS):
            to_group = (g + i) % GROUPS
            pltpu.make_async_remote_copy(
                src_ref=sending.at[tokens_of(to_row * GROUPS + to_group)],
                dst_ref=parts.at[tokens_of(place)],
                send_sem=part_send,
                recv_sem=part_recv,
                device_id=(z * ROWS + to_row, to_group),
                device_id_type=MESH,
            ).start()

    pltpu.make_async_copy(parts, parts, part_recv).wait()

    levels = dot(parts[...], spread[...], ((1,), (0,)))
    numbers = parts[:, :NUM].astype(F32)
    by_row = [slice(r * ROW, r * ROW + ROW) for r in range(ROWS)]
    highest = levels[by_row[0]]
    for r in range(1, ROWS):
        highest = jnp.maximum(highest, levels[by_row[r]])
    above, below = 0.0, 0.0
    for r in range(ROWS):
        share = jnp.exp2(levels[by_row[r]] - highest)
        above = above + share * numbers[by_row[r]]
        below = below + share
    merged = above / below
    tokens = merged[:OWN]
    for other in range(1, GROUPS):
        tokens = tokens + merged[other * OWN : other * OWN + OWN]
    patch = base_ref[...].astype(F32)
    for h in range(LOCAL):
        patch = patch + tokens[:, h * PATCH : h * PATCH + PATCH]
    latent = patch * affine[0:1, :PATCH] + affine[1:2, :PATCH]
    lat_own[...] = jnp.concatenate([latent, latent], axis=1).astype(BF16)

    for slot, device in enumerate(((after, next_g), (after, g), (s, next_g), (before, next_g), (before, g))):
        pltpu.make_async_remote_copy(
            src_ref=lat_own,
            dst_ref=lat_near.at[slot],
            send_sem=near_send,
            recv_sem=near_recv,
            device_id=device,
            device_id_type=MESH,
        ).start()

    pltpu.make_async_copy(lat_near, lat_near, near_recv).wait()

    has_before = (s > 0).astype(F32)
    has_after = (s < SEQ - 1).astype(F32)
    has_frames = (g > 0).astype(F32)
    tiles = [
        [lat_near[0].astype(F32) * (has_before * has_frames), lat_near[1].astype(F32) * has_before],
        [lat_near[2].astype(F32) * has_frames, lat_own[...].astype(F32)],
        [lat_near[3].astype(F32) * (has_after * has_frames), lat_near[4].astype(F32) * has_after],
    ]
    lane = lax.broadcasted_iota(jnp.int32, (8, 128), 1)
    line = lax.broadcasted_iota(jnp.int32, (8, 128), 0)
    sides = ([], [])
    for f in range(4):
        for r in range(3):
            here = tiles[r][f // 2][(f % 2) * 8 : (f % 2) * 8 + 8]
            left = jnp.where(line == 0, 0.0, pltpu.roll(here, 1, 0))
            right = jnp.where(line == 7, 0.0, pltpu.roll(here, 7, 0))
            sides[0].append(jnp.where(lane < 64, left, here))
            sides[1].append(jnp.where(lane < 64, here, right))
    windows = [
        dot(jnp.concatenate(side, axis=0).astype(BF16), chosen, ((1,), (0,))) for side, chosen in zip(sides, (pick[0], pick[1]))
    ]

    def window(f, r, b):
        at = (f * 3 + r) * 8
        return windows[b][at : at + 8]

    lines = []
    for f in range(2):
        for pair in range(2):
            for b in range(2):
                pieces = [window(f + t, pair + r, b) for t in range(3) for r in range(2)]
                lines.append(jnp.concatenate(pieces, axis=1))
    conv = dot(jnp.concatenate(lines, axis=0).astype(BF16), w_two[...], ((1,), (0,)))
    for half in range(2):
        out = conv[:, half * CH : half * CH + CH] + b_in_ref[...].reshape(1, CH)
        mean_sq = jnp.mean(out * out, axis=1, keepdims=True)
        normed = out * lax.rsqrt(mean_sq + 1e-6) * gain_ref[...].reshape(1, CH)
        active = normed / (1.0 + jnp.exp(-normed))
        for f in range(2):
            for pair in range(2):
                y = 2 * pair + half
                for b in range(2):
                    at = ((f * 2 + pair) * 2 + b) * 8
                    part = active[at : at + 8]
                    if y == 0:
                        part = part * has_before
                    if y == 3:
                        part = part * has_after
                    for twice in range(2):
                        for tile in range(3):
                            enlarged[tile, f * 4 + y, pl.ds(EDGE + 2 * b + twice, 8, stride=4), :] = part[
                                :, tile * 128 : tile * 128 + 128
                            ]

    for v in range(3):
        for f in range(2):
            for y in range(4):
                piece = [enlarged[tile, f * 4 + y, EDGE - 1 + v : EDGE + 31 + v, :] for tile in range(3)]
                piece = jnp.concatenate(piece, axis=1).astype(BF16)
                for line_out in range(4):
                    for u in range(3):
                        if (line_out + u + 1) // 2 == y:
                            at = (f * 4 + line_out) * 32
                            to = (u * 3 + v) * CH
                            columns[at : at + 32, to : to + CH] = piece
    planes = b_up_ref[...]
    for tap in range(9):
        planes = planes + dot(
            columns[:, tap * CH : tap * CH + CH], w_up[tap * OUTCH : tap * OUTCH + OUTCH, :], ((1,), (1,))
        )
    out_ref[...] = planes.astype(BF16)

    for kind in range(3):
        sent = v_row.at[: ROW - OWN]
        pltpu.make_async_copy(sent, sent, plane_send.at[kind]).wait()
    sent = queries.at[: PLANE - ROW]
    pltpu.make_async_copy(sent, sent, plane_send.at[3]).wait()
    for way, kind, ring, count in ((0, 0, keys, 8), (0, 1, values, 7), (1, 0, keys, 7), (1, 1, values, 8)):
        sent = ring.at[:count]
        pltpu.make_async_copy(sent, sent, ring_send.at[way, kind]).wait()
    sent = parts.at[: PLANE - OWN]
    pltpu.make_async_copy(sent, sent, part_send).wait()
    pltpu.make_async_copy(lat_near, lat_near, near_send).wait()


def on_device(
    query_states,
    key_states,
    value_states,
    base_patch,
    head_proj,
    latent_std,
    latent_mean,
    w_in,
    b_in,
    gain_mid,
    w_up,
    b_up,
):
    here = pl.BlockSpec(memory_space=pltpu.VMEM)
    far = pl.BlockSpec(memory_space=pltpu.HBM)
    DMA = pltpu.SemaphoreType.DMA
    planes = pl.pallas_call(
        kernel,
        out_shape=pltpu.VMEM((256, OUTCH), BF16),
        in_specs=[far] * 12,
        out_specs=here,
        scratch_shapes=[
            pltpu.VMEM((16, ROW, WIDE), BF16),
            pltpu.VMEM((16, NUM, ROW), BF16),
            pltpu.VMEM((ROW, WIDE), BF16),
            pltpu.VMEM((PLANE, WIDE), BF16),
            pltpu.VMEM((WIDE, PLANE), BF16),
            pltpu.VMEM((8, PLANE), F32),
            pltpu.VMEM((8, PLANE), F32),
            pltpu.VMEM((LOCAL, 2 * ROW, PLANE), BF16),
            pltpu.VMEM((LOCAL * TALL, PLANE), F32),
            pltpu.VMEM((MSG, PLANE), F32),
            pltpu.VMEM((PLANE, MSG), BF16),
            pltpu.VMEM((PLANE, MSG), BF16),
            pltpu.VMEM((OWN, 128), BF16),
            pltpu.VMEM((5, OWN, 128), BF16),
            pltpu.VMEM((OWN, PATCH), BF16),
            pltpu.VMEM((PATCH, WIDE), BF16),
            pltpu.VMEM((1, 16), F32),
            pltpu.VMEM((1, 16), F32),
            pltpu.VMEM((27 * 16, CH), BF16),
            pltpu.VMEM((CH,), F32),
            pltpu.VMEM((CH,), F32),
            pltpu.VMEM((9 * OUTCH, CH), BF16),
            pltpu.VMEM((1, OUTCH), F32),
            pltpu.VMEM((768, 2 * CH), BF16),
            pltpu.VMEM((3, 8, LINE, 128), F32),
            pltpu.VMEM((256, 9 * CH), BF16),
            pltpu.VMEM((MSG, NUM), BF16),
            pltpu.VMEM((2, 128, 128), BF16),
            pltpu.VMEM((8, 128), F32),
            DMA((4,)),
            DMA((4,)),
            DMA((2, 2)),
            DMA((2, 16, 2)),
            DMA,
            DMA,
            DMA,
            DMA,
            DMA((9,)),
        ],
        compiler_params=pltpu.CompilerParams(
            collective_id=0, has_side_effects=True, vmem_limit_bytes=60 * 1024 * 1024
        ),
        name="attend_and_decode",
    )(
        query_states,
        key_states,
        value_states,
        base_patch,
        head_proj.T,
        latent_std.reshape(1, 16),
        latent_mean.reshape(1, 16),
        w_in.reshape(27 * 16, CH),
        b_in,
        gain_mid,
        w_up.transpose(0, 1, 3, 2).reshape(9 * OUTCH, CH),
        b_up.reshape(1, OUTCH),
    )
    return planes.reshape(2, 4, 32, OUTCH)


def solution(mesh):
    in_specs = (
        P(("seq", "head"), None),
        P(("seq", "head"), None),
        P(("seq", "head"), None),
        P(("seq", "head"), None),
        P("head", None),
        P(),
        P(),
        P(),
        P(),
        P(),
        P(),
        P(),
    )
    out_specs = P("head", "seq", None, None)
    return jax.shard_map(
        on_device, mesh=mesh, in_specs=in_specs, out_specs=out_specs, check_vma=False
    )
```

```python
import math

import jax
import jax.numpy as jnp
from jax import lax
from jax.experimental import pallas as pl
from jax.experimental.pallas import tpu as pltpu
from jax.sharding import PartitionSpec as P

MESH = pl.DeviceIdType.MESH
F32, BF16 = jnp.float32, jnp.bfloat16

SEQ, GROUPS = 64, 8
ROWS = 4
PLACES = ROWS * GROUPS
OWN = 16
ROW = OWN * GROUPS
PLANE = ROW * ROWS
HD, LOCAL = 128, 3
WIDE = HD * LOCAL
PATCH = 64
NUM = PATCH * LOCAL
MSG = 256
TALL = PATCH + 8
CH, OUTCH = 384, 192
EDGE = 8
LINE = 48
TO_LOG2 = math.log2(math.e) / math.sqrt(HD)


def dot(a, b, dims):
    return lax.dot_general(a, b, (dims, ((), ())), preferred_element_type=F32)


def kernel(
    q_in, k_in, v_in, base_far, proj_far, std_far, mean_far, w_in_far, b_in_far, gain_far, w_up_far, b_up_far,
    out_ref,
    keys, values, v_row, queries, turned_queries, top, fade, weighted, summed, turned, sending, parts, lat_own, lat_near,
    base_ref, proj_ref, std_ref, mean_ref, w_in, b_in_ref, gain_ref, w_up, b_up_ref, w_two, enlarged, shifted, spread, pick, affine,
    plane_send, plane_recv, ring_send, ring_recv, part_send, part_recv, near_send, near_recv, weight_sem,
):
    s, g = lax.axis_index("seq"), lax.axis_index("head")
    z, row = s // ROWS, s % ROWS
    place = row * GROUPS + g
    up, down = ((s + ROWS) % SEQ, g), ((s + SEQ - ROWS) % SEQ, g)
    after, before = (s + 1) % SEQ, (s + SEQ - 1) % SEQ
    next_g, last_g = (g + 1) % GROUPS, (g + GROUPS - 1) % GROUPS

    def peer(i):
        other = (place + i) % PLACES
        return other, (z * ROWS + other // GROUPS, other % GROUPS)

    def columns_of(group):
        return pl.ds(pl.multiple_of(group * WIDE, WIDE), WIDE)

    def tokens_of(index):
        return pl.ds(pl.multiple_of(index * OWN, OWN), OWN)

    barrier = pltpu.get_barrier_semaphore()

    for i in range(1, PLACES):
        pl.semaphore_signal(barrier, inc=1, device_id=peer(i)[1], device_id_type=MESH)
    for other in (up, down, (after, g), (before, g), (after, last_g), (before, last_g)):
        pl.semaphore_signal(barrier, inc=1, device_id=other, device_id_type=MESH)

    q_row = queries.at[pl.ds(pl.multiple_of(row * ROW, ROW), ROW)]
    rows_of = ((k_in, keys.at[0]), (v_in, v_row), (q_in, q_row))
    proj_in = pltpu.make_async_copy(proj_far, proj_ref, weight_sem.at[8])
    proj_in.start()
    pl.semaphore_wait(barrier, PLACES - 1 + 6)

    for kind, (source, target) in enumerate(rows_of):
        for i in range(1, GROUPS):
            other = (g + i) % GROUPS
            pltpu.make_async_remote_copy(
                src_ref=source.at[:, columns_of(other)],
                dst_ref=target.at[tokens_of(g)],
                send_sem=plane_send.at[kind],
                recv_sem=plane_recv.at[kind],
                device_id=(s, other),
                device_id_type=MESH,
            ).start()
        pltpu.make_async_copy(source.at[:, columns_of(g)], target.at[tokens_of(g)], plane_recv.at[kind]).start()

    def portion(kind, slot, part):
        return values.at[slot] if kind else keys.at[slot, pl.ds(part * ROW // 2, ROW // 2)]

    def hop(kind, source, target, way, part):
        pltpu.make_async_remote_copy(
            src_ref=portion(kind, source, part),
            dst_ref=portion(kind, target, part),
            send_sem=ring_send.at[way, kind],
            recv_sem=ring_recv.at[kind, target, part],
            device_id=(up, down)[way],
            device_id_type=MESH,
        ).start()

    def arrived(kind, slot, part):
        pltpu.make_async_copy(
            portion(kind, slot, part), portion(kind, slot, part), ring_recv.at[kind, slot, part]
        ).wait()

    for kind, (source, target) in enumerate(rows_of[:2]):
        pltpu.make_async_copy(target, target, plane_recv.at[kind]).wait()
        if kind == 1:
            proj_in.wait()
            for h in range(LOCAL):
                lanes = slice(h * HD, h * HD + HD)
                values[0, h * PATCH : h * PATCH + PATCH, :] = dot(
                    proj_ref[:, lanes], v_row[:, lanes], ((1,), (1,))
                ).astype(BF16)
        for part in range(2 - kind):
            hop(kind, 0, 1, 0, part)
            hop(kind, 0, 9, 1, part)

    pltpu.make_async_copy(q_row, q_row, plane_recv.at[2]).wait()
    for i in range(1, ROWS):
        pltpu.make_async_remote_copy(
            src_ref=q_row,
            dst_ref=q_row,
            send_sem=plane_send.at[3],
            recv_sem=plane_recv.at[3],
            device_id=(z * ROWS + (row + i) % ROWS, g),
            device_id_type=MESH,
        ).start()

    parameters = [
        pltpu.make_async_copy(source, target, weight_sem.at[i])
        for i, (source, target) in enumerate(
            (
                (w_in_far, w_in),
                (w_up_far, w_up),
                (base_far, base_ref),
                (std_far, std_ref),
                (mean_far, mean_ref),
                (b_in_far, b_in_ref),
                (gain_far, gain_ref),
                (b_up_far, b_up_ref),
            )
        )
    ]
    for copy in parameters:
        copy.start()

    def joined(pieces, axis):
        return pieces[0] if len(pieces) == 1 else jnp.concatenate(pieces, axis=axis)

    units = [
        (h, slice(h * HD, h * HD + HD), slice(c * 256, c * 256 + 256)) for h in range(LOCAL) for c in range(2)
    ]

    def add_up(slots, chosen, first=False):
        for h, lanes, some in chosen:
            some_values = joined([values[slot, h * PATCH : h * PATCH + PATCH, :] for slot in slots], 1)
            some_values = jnp.concatenate([some_values, jnp.ones((16, len(slots) * ROW), BF16)], axis=0)
            product = dot(some_values, weighted[h, : len(slots) * ROW, some], ((1,), (0,)))[:TALL]
            rows = slice(h * TALL, h * TALL + TALL)
            summed[rows, some] = product if first else summed[rows, some] * fade[h : h + 1, some] + product

    def attend(earlier, slots, chosen):
        scores = [
            dot(joined([keys[slot, :, lanes] for slot in slots], 0), turned_queries[lanes, some], ((1,), (0,)))
            for h, lanes, some in chosen
        ]
        first = earlier == []
        if earlier:
            add_up(earlier, chosen, first=earlier == [0])
        for (h, lanes, some), score in zip(chosen, scores):
            new = jnp.max(score, axis=0, keepdims=True)
            if not first:
                old = top[h : h + 1, some]
                new = jnp.maximum(old, new)
                fading = jnp.exp2((old - new) * TO_LOG2)
                fade[h : h + 1, some] = fading
            weights = jnp.exp2((score - new) * TO_LOG2)
            top[h : h + 1, some] = new
            weighted[h, : len(slots) * ROW, some] = weights.astype(BF16)

    some, rest = units[:3], units[3:]

    def pass_on(kind, t, part):
        arrived(kind, t, part)
        hop(kind, t, t + 1, 0, part)
        arrived(kind, t + 8, part)
        hop(kind, t + 8, t + 9, 1, part)

    pass_on(0, 1, 0)
    pass_on(0, 1, 1)
    pass_on(1, 1, 0)

    for copy in parameters:
        copy.wait()
    w_two[...] = jnp.zeros_like(w_two)
    for t in range(3):
        for u in range(3):
            piece = w_in[(t * 3 + u) * 48 : (t * 3 + u) * 48 + 48, :]
            for half in range(2):
                at = t * 256 + (u + half) * 64
                w_two[at : at + 48, half * CH : half * CH + CH] = piece

    enlarged[...] = jnp.zeros_like(enlarged)
    turned[...] = jnp.zeros_like(turned)

    def ones_where(shape, made):
        r = lax.broadcasted_iota(jnp.int32, shape, 0)
        c = lax.broadcasted_iota(jnp.int32, shape, 1)
        return made(r, c).astype(F32).astype(BF16)

    spread[...] = ones_where(
        (MSG, NUM),
        lambda r, c: (r >= NUM) & (r < NUM + 3 * LOCAL) & ((r - NUM) % LOCAL == c // PATCH),
    )
    def picks(b):
        def made(r, c):
            a, v, low = c // 64, (c // 16) % 4, c % 16
            spot = v + 1 - b
            wanted = (spot // 2) * 64 + a * 32 + (spot % 2) * 16 + low
            return (v < 3) & (r == wanted)

        return ones_where((128, 128), made)

    pick[0] = picks(0)
    pick[1] = picks(1)
    for i, ref in enumerate((std_ref, mean_ref)):
        affine[i : i + 1, :PATCH] = jnp.concatenate([ref[...]] * 4, axis=1)

    others = queries.at[: PLANE - ROW]
    pltpu.make_async_copy(others, others, plane_recv.at[3]).wait()
    turned_queries[...] = queries[...].T
    attend([], [0], units)
    pass_on(0, 2, 0)
    pass_on(0, 2, 1)
    attend([0], [1, 9], some)
    pass_on(1, 2, 0)
    attend([0], [1, 9], rest)

    def step(t, carry):
        for event, (kind, part) in enumerate(((0, 0), (0, 1), (1, 0))):
            pass_on(kind, t, part)
            attend([t - 2, t + 6], [t - 1, t + 7], units[event * 2 : event * 2 + 2])
        return carry

    lax.fori_loop(3, 7, step, 0)
    for part in range(2):
        arrived(0, 7, part)
        hop(0, 7, 8, 0, part)
        arrived(0, 15, part)
        attend([5, 13], [6, 14], units[part * 2 : part * 2 + 2])
    arrived(1, 15, 0)
    hop(1, 15, 8, 1, 0)
    arrived(1, 7, 0)
    attend([5, 13], [6, 14], units[4:])
    attend([6, 14], [7, 15], units)
    add_up([7, 15], units)
    for part in range(2):
        arrived(0, 8, part)
    attend(None, [8], units)
    arrived(1, 8, 0)
    add_up([8], units)

    for h in range(LOCAL):
        sums = summed[h * TALL + PATCH : h * TALL + PATCH + 1, :]
        turned[h * PATCH : h * PATCH + PATCH, :] = summed[h * TALL : h * TALL + PATCH, :] * (1.0 / sums)
        level = top[h : h + 1, :] * TO_LOG2 + jnp.log(sums) * math.log2(math.e)
        for term in range(3):
            rounded = level.astype(BF16).astype(F32)
            turned[NUM + term * LOCAL + h : NUM + term * LOCAL + h + 1, :] = rounded
            level = level - rounded
    for away in (1, 2, 3, 0):
        to_row = (row + away) % ROWS
        lanes = pl.ds(pl.multiple_of(to_row * ROW, ROW), ROW)
        sending[lanes, :] = turned[:, lanes].astype(BF16).T
        if away == 0:
            pltpu.make_async_copy(sending.at[tokens_of(place)], parts.at[tokens_of(place)], part_recv).start()
        for i in range(0 if away else 1, GROUPS):
            to_group = (g + i) % GROUPS
            pltpu.make_async_remote_copy(
                src_ref=sending.at[tokens_of(to_row * GROUPS + to_group)],
                dst_ref=parts.at[tokens_of(place)],
                send_sem=part_send,
                recv_sem=part_recv,
                device_id=(z * ROWS + to_row, to_group),
                device_id_type=MESH,
            ).start()

    pltpu.make_async_copy(parts, parts, part_recv).wait()

    levels = dot(parts[...], spread[...], ((1,), (0,)))
    numbers = parts[:, :NUM].astype(F32)
    by_row = [slice(r * ROW, r * ROW + ROW) for r in range(ROWS)]
    highest = levels[by_row[0]]
    for r in range(1, ROWS):
        highest = jnp.maximum(highest, levels[by_row[r]])
    above, below = 0.0, 0.0
    for r in range(ROWS):
        share = jnp.exp2(levels[by_row[r]] - highest)
        above = above + share * numbers[by_row[r]]
        below = below + share
    merged = above / below
    tokens = merged[:OWN]
    for other in range(1, GROUPS):
        tokens = tokens + merged[other * OWN : other * OWN + OWN]
    patch = base_ref[...].astype(F32)
    for h in range(LOCAL):
        patch = patch + tokens[:, h * PATCH : h * PATCH + PATCH]
    latent = patch * affine[0:1, :PATCH] + affine[1:2, :PATCH]
    lat_own[...] = jnp.concatenate([latent, latent], axis=1).astype(BF16)

    for slot, device in enumerate(((after, next_g), (after, g), (s, next_g), (before, next_g), (before, g))):
        pltpu.make_async_remote_copy(
            src_ref=lat_own,
            dst_ref=lat_near.at[slot],
            send_sem=near_send,
            recv_sem=near_recv,
            device_id=device,
            device_id_type=MESH,
        ).start()

    pltpu.make_async_copy(lat_near, lat_near, near_recv).wait()

    has_before = (s > 0).astype(F32)
    has_after = (s < SEQ - 1).astype(F32)
    has_frames = (g > 0).astype(F32)
    tiles = [
        [lat_near[0].astype(F32) * (has_before * has_frames), lat_near[1].astype(F32) * has_before],
        [lat_near[2].astype(F32) * has_frames, lat_own[...].astype(F32)],
        [lat_near[3].astype(F32) * (has_after * has_frames), lat_near[4].astype(F32) * has_after],
    ]
    lane = lax.broadcasted_iota(jnp.int32, (8, 128), 1)
    line = lax.broadcasted_iota(jnp.int32, (8, 128), 0)
    sides = ([], [])
    for f in range(4):
        for r in range(3):
            here = tiles[r][f // 2][(f % 2) * 8 : (f % 2) * 8 + 8]
            left = jnp.where(line == 0, 0.0, pltpu.roll(here, 1, 0))
            right = jnp.where(line == 7, 0.0, pltpu.roll(here, 7, 0))
            sides[0].append(jnp.where(lane < 64, left, here))
            sides[1].append(jnp.where(lane < 64, here, right))
    windows = [
        dot(jnp.concatenate(side, axis=0).astype(BF16), chosen, ((1,), (0,))) for side, chosen in zip(sides, (pick[0], pick[1]))
    ]

    def window(f, r, b):
        at = (f * 3 + r) * 8
        return windows[b][at : at + 8]

    lines = []
    for f in range(2):
        for pair in range(2):
            for b in range(2):
                pieces = [window(f + t, pair + r, b) for t in range(3) for r in range(2)]
                lines.append(jnp.concatenate(pieces, axis=1))
    conv = dot(jnp.concatenate(lines, axis=0).astype(BF16), w_two[...], ((1,), (0,)))
    for half in range(2):
        out = conv[:, half * CH : half * CH + CH] + b_in_ref[...].reshape(1, CH)
        mean_sq = jnp.mean(out * out, axis=1, keepdims=True)
        normed = out * lax.rsqrt(mean_sq + 1e-6) * gain_ref[...].reshape(1, CH)
        active = normed / (1.0 + jnp.exp(-normed))
        for f in range(2):
            for pair in range(2):
                y = 2 * pair + half
                for b in range(2):
                    at = ((f * 2 + pair) * 2 + b) * 8
                    part = active[at : at + 8]
                    if y == 0:
                        part = part * has_before
                    if y == 3:
                        part = part * has_after
                    for twice in range(2):
                        for tile in range(3):
                            enlarged[tile, f * 4 + y, pl.ds(EDGE + 2 * b + twice, 8, stride=4), :] = part[
                                :, tile * 128 : tile * 128 + 128
                            ]

    for v in range(3):
        for line in range(8):
            piece = [enlarged[tile, line, EDGE - 1 + v : EDGE + 31 + v, :] for tile in range(3)]
            shifted[v, line] = jnp.concatenate(piece, axis=1).astype(BF16)
    planes = b_up_ref[...]
    for u in range(3):
        for v in range(3):
            tap = u * 3 + v
            lines = [shifted[v, f * 4 + (line_out + u + 1) // 2] for f in range(2) for line_out in range(4)]
            planes = planes + dot(
                jnp.concatenate(lines, axis=0), w_up[tap * OUTCH : tap * OUTCH + OUTCH, :], ((1,), (1,))
            )
    out_ref[...] = planes.astype(BF16)

    for kind in range(3):
        sent = v_row.at[: ROW - OWN]
        pltpu.make_async_copy(sent, sent, plane_send.at[kind]).wait()
    sent = queries.at[: PLANE - ROW]
    pltpu.make_async_copy(sent, sent, plane_send.at[3]).wait()
    for way, kind, ring, count in ((0, 0, keys, 8), (0, 1, values, 7), (1, 0, keys, 7), (1, 1, values, 8)):
        sent = ring.at[:count]
        pltpu.make_async_copy(sent, sent, ring_send.at[way, kind]).wait()
    sent = parts.at[: PLANE - OWN]
    pltpu.make_async_copy(sent, sent, part_send).wait()
    pltpu.make_async_copy(lat_near, lat_near, near_send).wait()


def on_device(
    query_states,
    key_states,
    value_states,
    base_patch,
    head_proj,
    latent_std,
    latent_mean,
    w_in,
    b_in,
    gain_mid,
    w_up,
    b_up,
):
    here = pl.BlockSpec(memory_space=pltpu.VMEM)
    far = pl.BlockSpec(memory_space=pltpu.HBM)
    DMA = pltpu.SemaphoreType.DMA
    planes = pl.pallas_call(
        kernel,
        out_shape=pltpu.VMEM((256, OUTCH), BF16),
        in_specs=[far] * 12,
        out_specs=here,
        scratch_shapes=[
            pltpu.VMEM((16, ROW, WIDE), BF16),
            pltpu.VMEM((16, NUM, ROW), BF16),
            pltpu.VMEM((ROW, WIDE), BF16),
            pltpu.VMEM((PLANE, WIDE), BF16),
            pltpu.VMEM((WIDE, PLANE), BF16),
            pltpu.VMEM((8, PLANE), F32),
            pltpu.VMEM((8, PLANE), F32),
            pltpu.VMEM((LOCAL, 2 * ROW, PLANE), BF16),
            pltpu.VMEM((LOCAL * TALL, PLANE), F32),
            pltpu.VMEM((MSG, PLANE), F32),
            pltpu.VMEM((PLANE, MSG), BF16),
            pltpu.VMEM((PLANE, MSG), BF16),
            pltpu.VMEM((OWN, 128), BF16),
            pltpu.VMEM((5, OWN, 128), BF16),
            pltpu.VMEM((OWN, PATCH), BF16),
            pltpu.VMEM((PATCH, WIDE), BF16),
            pltpu.VMEM((1, 16), F32),
            pltpu.VMEM((1, 16), F32),
            pltpu.VMEM((27 * 16, CH), BF16),
            pltpu.VMEM((CH,), F32),
            pltpu.VMEM((CH,), F32),
            pltpu.VMEM((9 * OUTCH, CH), BF16),
            pltpu.VMEM((1, OUTCH), F32),
            pltpu.VMEM((768, 2 * CH), BF16),
            pltpu.VMEM((3, 8, LINE, 128), F32),
            pltpu.VMEM((3, 8, 32, CH), BF16),
            pltpu.VMEM((MSG, NUM), BF16),
            pltpu.VMEM((2, 128, 128), BF16),
            pltpu.VMEM((8, 128), F32),
            DMA((4,)),
            DMA((4,)),
            DMA((2, 2)),
            DMA((2, 16, 2)),
            DMA,
            DMA,
            DMA,
            DMA,
            DMA((9,)),
        ],
        compiler_params=pltpu.CompilerParams(
            collective_id=0, has_side_effects=True, vmem_limit_bytes=60 * 1024 * 1024
        ),
        name="attend_and_decode",
    )(
        query_states,
        key_states,
        value_states,
        base_patch,
        head_proj.T,
        latent_std.reshape(1, 16),
        latent_mean.reshape(1, 16),
        w_in.reshape(27 * 16, CH),
        b_in,
        gain_mid,
        w_up.transpose(0, 1, 3, 2).reshape(9 * OUTCH, CH),
        b_up.reshape(1, OUTCH),
    )
    return planes.reshape(2, 4, 32, OUTCH)


def solution(mesh):
    in_specs = (
        P(("seq", "head"), None),
        P(("seq", "head"), None),
        P(("seq", "head"), None),
        P(("seq", "head"), None),
        P("head", None),
        P(),
        P(),
        P(),
        P(),
        P(),
        P(),
        P(),
    )
    out_specs = P("head", "seq", None, None)
    return jax.shard_map(
        on_device, mesh=mesh, in_specs=in_specs, out_specs=out_specs, check_vma=False
    )
```

```python
import math

import jax
import jax.numpy as jnp
from jax import lax
from jax.experimental import pallas as pl
from jax.experimental.pallas import tpu as pltpu
from jax.sharding import PartitionSpec as P

MESH = pl.DeviceIdType.MESH
F32, BF16 = jnp.float32, jnp.bfloat16

SEQ, GROUPS = 64, 8
ROWS = 4
PLACES = ROWS * GROUPS
OWN = 16
ROW = OWN * GROUPS
PLANE = ROW * ROWS
HD, LOCAL = 128, 3
WIDE = HD * LOCAL
PATCH = 64
NUM = PATCH * LOCAL
MSG = 256
TALL = PATCH + 8
CH, OUTCH = 384, 192
EDGE = 8
LINE = 48
TO_LOG2 = math.log2(math.e) / math.sqrt(HD)


def dot(a, b, dims):
    return lax.dot_general(a, b, (dims, ((), ())), preferred_element_type=F32)


def kernel(
    q_in, k_in, v_in, base_far, proj_far, std_far, mean_far, w_in_far, b_in_far, gain_far, w_up_far, b_up_far,
    out_ref,
    keys, values, v_row, queries, turned_queries, top, fade, weighted, summed, turned, sending, parts, lat_own, lat_near,
    base_ref, proj_ref, std_ref, mean_ref, w_in, b_in_ref, gain_ref, w_up, b_up_ref, w_two, enlarged, shifted, spread, pick, affine,
    plane_send, plane_recv, ring_send, ring_recv, part_send, part_recv, near_send, near_recv, weight_sem,
):
    s, g = lax.axis_index("seq"), lax.axis_index("head")
    z, row = s // ROWS, s % ROWS
    place = row * GROUPS + g
    up, down = ((s + ROWS) % SEQ, g), ((s + SEQ - ROWS) % SEQ, g)
    after, before = (s + 1) % SEQ, (s + SEQ - 1) % SEQ
    next_g, last_g = (g + 1) % GROUPS, (g + GROUPS - 1) % GROUPS

    def peer(i):
        other = (place + i) % PLACES
        return other, (z * ROWS + other // GROUPS, other % GROUPS)

    def columns_of(group):
        return pl.ds(pl.multiple_of(group * WIDE, WIDE), WIDE)

    def tokens_of(index):
        return pl.ds(pl.multiple_of(index * OWN, OWN), OWN)

    barrier = pltpu.get_barrier_semaphore()

    for other in (up, down, (after, g), (before, g), (after, last_g), (before, last_g)):
        pl.semaphore_signal(barrier, inc=1, device_id=other, device_id_type=MESH)
    for i in range(1, PLACES):
        pl.semaphore_signal(barrier, inc=1, device_id=peer(i)[1], device_id_type=MESH)

    q_row = queries.at[pl.ds(pl.multiple_of(row * ROW, ROW), ROW)]
    rows_of = ((k_in, keys.at[0]), (v_in, v_row), (q_in, q_row))
    proj_in = pltpu.make_async_copy(proj_far, proj_ref, weight_sem.at[8])
    proj_in.start()
    pl.semaphore_wait(barrier, PLACES - 1 + 6)

    for kind, (source, target) in enumerate(rows_of):
        for i in range(1, GROUPS):
            other = (g + i) % GROUPS
            pltpu.make_async_remote_copy(
                src_ref=source.at[:, columns_of(other)],
                dst_ref=target.at[tokens_of(g)],
                send_sem=plane_send.at[kind],
                recv_sem=plane_recv.at[kind],
                device_id=(s, other),
                device_id_type=MESH,
            ).start()
        pltpu.make_async_copy(source.at[:, columns_of(g)], target.at[tokens_of(g)], plane_recv.at[kind]).start()

    def portion(kind, slot, part):
        return values.at[slot] if kind else keys.at[slot, pl.ds(part * ROW // 2, ROW // 2)]

    def hop(kind, source, target, way, part):
        pltpu.make_async_remote_copy(
            src_ref=portion(kind, source, part),
            dst_ref=portion(kind, target, part),
            send_sem=ring_send.at[way, kind],
            recv_sem=ring_recv.at[kind, target, part],
            device_id=(up, down)[way],
            device_id_type=MESH,
        ).start()

    def arrived(kind, slot, part):
        pltpu.make_async_copy(
            portion(kind, slot, part), portion(kind, slot, part), ring_recv.at[kind, slot, part]
        ).wait()

    for kind, (source, target) in enumerate(rows_of[:2]):
        pltpu.make_async_copy(target, target, plane_recv.at[kind]).wait()
        if kind == 1:
            proj_in.wait()
            for h in range(LOCAL):
                lanes = slice(h * HD, h * HD + HD)
                values[0, h * PATCH : h * PATCH + PATCH, :] = dot(
                    proj_ref[:, lanes], v_row[:, lanes], ((1,), (1,))
                ).astype(BF16)
        for part in range(2 - kind):
            hop(kind, 0, 1, 0, part)
            hop(kind, 0, 9, 1, part)

    pltpu.make_async_copy(q_row, q_row, plane_recv.at[2]).wait()
    for i in range(1, ROWS):
        pltpu.make_async_remote_copy(
            src_ref=q_row,
            dst_ref=q_row,
            send_sem=plane_send.at[3],
            recv_sem=plane_recv.at[3],
            device_id=(z * ROWS + (row + i) % ROWS, g),
            device_id_type=MESH,
        ).start()

    parameters = [
        pltpu.make_async_copy(source, target, weight_sem.at[i])
        for i, (source, target) in enumerate(
            (
                (w_in_far, w_in),
                (w_up_far, w_up),
                (base_far, base_ref),
                (std_far, std_ref),
                (mean_far, mean_ref),
                (b_in_far, b_in_ref),
                (gain_far, gain_ref),
                (b_up_far, b_up_ref),
            )
        )
    ]
    for copy in parameters:
        copy.start()

    def joined(pieces, axis):
        return pieces[0] if len(pieces) == 1 else jnp.concatenate(pieces, axis=axis)

    units = [
        (h, slice(h * HD, h * HD + HD), slice(c * 256, c * 256 + 256)) for h in range(LOCAL) for c in range(2)
    ]

    def add_up(slots, chosen, first=False):
        for h, lanes, some in chosen:
            some_values = joined([values[slot, h * PATCH : h * PATCH + PATCH, :] for slot in slots], 1)
            some_values = jnp.concatenate([some_values, jnp.ones((16, len(slots) * ROW), BF16)], axis=0)
            product = dot(some_values, weighted[h, : len(slots) * ROW, some], ((1,), (0,)))[:TALL]
            rows = slice(h * TALL, h * TALL + TALL)
            summed[rows, some] = product if first else summed[rows, some] * fade[h : h + 1, some] + product

    def attend(earlier, slots, chosen):
        scores = [
            dot(joined([keys[slot, :, lanes] for slot in slots], 0), turned_queries[lanes, some], ((1,), (0,)))
            for h, lanes, some in chosen
        ]
        first = earlier == []
        if earlier:
            add_up(earlier, chosen, first=earlier == [0])
        for (h, lanes, some), score in zip(chosen, scores):
            new = jnp.max(score, axis=0, keepdims=True)
            if not first:
                old = top[h : h + 1, some]
                new = jnp.maximum(old, new)
                fading = jnp.exp2((old - new) * TO_LOG2)
                fade[h : h + 1, some] = fading
            weights = jnp.exp2((score - new) * TO_LOG2)
            top[h : h + 1, some] = new
            weighted[h, : len(slots) * ROW, some] = weights.astype(BF16)

    some, rest = units[:3], units[3:]

    def pass_on(kind, t, part):
        arrived(kind, t, part)
        hop(kind, t, t + 1, 0, part)
        arrived(kind, t + 8, part)
        hop(kind, t + 8, t + 9, 1, part)

    pass_on(0, 1, 0)
    pass_on(0, 1, 1)
    pass_on(1, 1, 0)

    for copy in parameters:
        copy.wait()
    w_two[...] = jnp.zeros_like(w_two)
    for t in range(3):
        for u in range(3):
            piece = w_in[(t * 3 + u) * 48 : (t * 3 + u) * 48 + 48, :]
            for half in range(2):
                at = t * 256 + (u + half) * 64
                w_two[at : at + 48, half * CH : half * CH + CH] = piece

    enlarged[...] = jnp.zeros_like(enlarged)
    turned[...] = jnp.zeros_like(turned)

    def ones_where(shape, made):
        r = lax.broadcasted_iota(jnp.int32, shape, 0)
        c = lax.broadcasted_iota(jnp.int32, shape, 1)
        return made(r, c).astype(F32).astype(BF16)

    spread[...] = ones_where(
        (MSG, NUM),
        lambda r, c: (r >= NUM) & (r < NUM + 3 * LOCAL) & ((r - NUM) % LOCAL == c // PATCH),
    )
    def picks(b):
        def made(r, c):
            a, v, low = c // 64, (c // 16) % 4, c % 16
            spot = v + 1 - b
            wanted = (spot // 2) * 64 + a * 32 + (spot % 2) * 16 + low
            return (v < 3) & (r == wanted)

        return ones_where((128, 128), made)

    pick[0] = picks(0)
    pick[1] = picks(1)
    for i, ref in enumerate((std_ref, mean_ref)):
        affine[i : i + 1, :PATCH] = jnp.concatenate([ref[...]] * 4, axis=1)

    others = queries.at[: PLANE - ROW]
    pltpu.make_async_copy(others, others, plane_recv.at[3]).wait()
    turned_queries[...] = queries[...].T
    attend([], [0], units)
    pass_on(0, 2, 0)
    pass_on(0, 2, 1)
    attend([0], [1, 9], some)
    pass_on(1, 2, 0)
    attend([0], [1, 9], rest)

    def step(t, carry):
        for event, (kind, part) in enumerate(((0, 0), (0, 1), (1, 0))):
            pass_on(kind, t, part)
            attend([t - 2, t + 6], [t - 1, t + 7], units[event * 2 : event * 2 + 2])
        return carry

    lax.fori_loop(3, 7, step, 0)
    for part in range(2):
        arrived(0, 7, part)
        hop(0, 7, 8, 0, part)
        arrived(0, 15, part)
        attend([5, 13], [6, 14], units[part * 2 : part * 2 + 2])
    arrived(1, 15, 0)
    hop(1, 15, 8, 1, 0)
    arrived(1, 7, 0)
    attend([5, 13], [6, 14], units[4:])
    attend([6, 14], [7, 15], units)
    add_up([7, 15], units)
    for part in range(2):
        arrived(0, 8, part)
    attend(None, [8], units)
    arrived(1, 8, 0)
    add_up([8], units)

    for h in range(LOCAL):
        sums = summed[h * TALL + PATCH : h * TALL + PATCH + 1, :]
        turned[h * PATCH : h * PATCH + PATCH, :] = summed[h * TALL : h * TALL + PATCH, :] * (1.0 / sums)
        level = top[h : h + 1, :] * TO_LOG2 + jnp.log(sums) * math.log2(math.e)
        for term in range(3):
            rounded = level.astype(BF16).astype(F32)
            turned[NUM + term * LOCAL + h : NUM + term * LOCAL + h + 1, :] = rounded
            level = level - rounded
    for away in (1, 2, 3, 0):
        to_row = (row + away) % ROWS
        lanes = pl.ds(pl.multiple_of(to_row * ROW, ROW), ROW)
        sending[lanes, :] = turned[:, lanes].astype(BF16).T
        if away == 0:
            pltpu.make_async_copy(sending.at[tokens_of(place)], parts.at[tokens_of(place)], part_recv).start()
        for i in range(0 if away else 1, GROUPS):
            to_group = (g + i) % GROUPS
            pltpu.make_async_remote_copy(
                src_ref=sending.at[tokens_of(to_row * GROUPS + to_group)],
                dst_ref=parts.at[tokens_of(place)],
                send_sem=part_send,
                recv_sem=part_recv,
                device_id=(z * ROWS + to_row, to_group),
                device_id_type=MESH,
            ).start()

    pltpu.make_async_copy(parts, parts, part_recv).wait()

    levels = dot(parts[...], spread[...], ((1,), (0,)))
    numbers = parts[:, :NUM].astype(F32)
    by_row = [slice(r * ROW, r * ROW + ROW) for r in range(ROWS)]
    highest = levels[by_row[0]]
    for r in range(1, ROWS):
        highest = jnp.maximum(highest, levels[by_row[r]])
    above, below = 0.0, 0.0
    for r in range(ROWS):
        share = jnp.exp2(levels[by_row[r]] - highest)
        above = above + share * numbers[by_row[r]]
        below = below + share
    merged = above / below
    tokens = merged[:OWN]
    for other in range(1, GROUPS):
        tokens = tokens + merged[other * OWN : other * OWN + OWN]
    patch = base_ref[...].astype(F32)
    for h in range(LOCAL):
        patch = patch + tokens[:, h * PATCH : h * PATCH + PATCH]
    latent = patch * affine[0:1, :PATCH] + affine[1:2, :PATCH]
    lat_own[...] = jnp.concatenate([latent, latent], axis=1).astype(BF16)

    for slot, device in enumerate(((after, next_g), (after, g), (s, next_g), (before, next_g), (before, g))):
        pltpu.make_async_remote_copy(
            src_ref=lat_own,
            dst_ref=lat_near.at[slot],
            send_sem=near_send,
            recv_sem=near_recv,
            device_id=device,
            device_id_type=MESH,
        ).start()

    pltpu.make_async_copy(lat_near, lat_near, near_recv).wait()

    has_before = (s > 0).astype(F32)
    has_after = (s < SEQ - 1).astype(F32)
    has_frames = (g > 0).astype(F32)
    tiles = [
        [lat_near[0].astype(F32) * (has_before * has_frames), lat_near[1].astype(F32) * has_before],
        [lat_near[2].astype(F32) * has_frames, lat_own[...].astype(F32)],
        [lat_near[3].astype(F32) * (has_after * has_frames), lat_near[4].astype(F32) * has_after],
    ]
    lane = lax.broadcasted_iota(jnp.int32, (8, 128), 1)
    line = lax.broadcasted_iota(jnp.int32, (8, 128), 0)
    sides = ([], [])
    for f in range(4):
        for r in range(3):
            here = tiles[r][f // 2][(f % 2) * 8 : (f % 2) * 8 + 8]
            left = jnp.where(line == 0, 0.0, pltpu.roll(here, 1, 0))
            right = jnp.where(line == 7, 0.0, pltpu.roll(here, 7, 0))
            sides[0].append(jnp.where(lane < 64, left, here))
            sides[1].append(jnp.where(lane < 64, here, right))
    windows = [
        dot(jnp.concatenate(side, axis=0).astype(BF16), chosen, ((1,), (0,))) for side, chosen in zip(sides, (pick[0], pick[1]))
    ]

    def window(f, r, b):
        at = (f * 3 + r) * 8
        return windows[b][at : at + 8]

    lines = []
    for f in range(2):
        for pair in range(2):
            for b in range(2):
                pieces = [window(f + t, pair + r, b) for t in range(3) for r in range(2)]
                lines.append(jnp.concatenate(pieces, axis=1))
    conv = dot(jnp.concatenate(lines, axis=0).astype(BF16), w_two[...], ((1,), (0,)))
    for half in range(2):
        out = conv[:, half * CH : half * CH + CH] + b_in_ref[...].reshape(1, CH)
        mean_sq = jnp.mean(out * out, axis=1, keepdims=True)
        normed = out * lax.rsqrt(mean_sq + 1e-6) * gain_ref[...].reshape(1, CH)
        active = normed / (1.0 + jnp.exp(-normed))
        for f in range(2):
            for pair in range(2):
                y = 2 * pair + half
                for b in range(2):
                    at = ((f * 2 + pair) * 2 + b) * 8
                    part = active[at : at + 8]
                    if y == 0:
                        part = part * has_before
                    if y == 3:
                        part = part * has_after
                    for twice in range(2):
                        for tile in range(3):
                            enlarged[tile, f * 4 + y, pl.ds(EDGE + 2 * b + twice, 8, stride=4), :] = part[
                                :, tile * 128 : tile * 128 + 128
                            ]

    for v in range(3):
        for line in range(8):
            piece = [enlarged[tile, line, EDGE - 1 + v : EDGE + 31 + v, :] for tile in range(3)]
            shifted[v, line] = jnp.concatenate(piece, axis=1).astype(BF16)
    planes = b_up_ref[...]
    for u in range(3):
        for v in range(3):
            tap = u * 3 + v
            lines = [shifted[v, f * 4 + (line_out + u + 1) // 2] for f in range(2) for line_out in range(4)]
            planes = planes + dot(
                jnp.concatenate(lines, axis=0), w_up[tap * OUTCH : tap * OUTCH + OUTCH, :], ((1,), (1,))
            )
    out_ref[...] = planes.astype(BF16)

    for kind in range(3):
        sent = v_row.at[: ROW - OWN]
        pltpu.make_async_copy(sent, sent, plane_send.at[kind]).wait()
    sent = queries.at[: PLANE - ROW]
    pltpu.make_async_copy(sent, sent, plane_send.at[3]).wait()
    for way, kind, ring, count in ((0, 0, keys, 8), (0, 1, values, 7), (1, 0, keys, 7), (1, 1, values, 8)):
        sent = ring.at[:count]
        pltpu.make_async_copy(sent, sent, ring_send.at[way, kind]).wait()
    sent = parts.at[: PLANE - OWN]
    pltpu.make_async_copy(sent, sent, part_send).wait()
    pltpu.make_async_copy(lat_near, lat_near, near_send).wait()


def on_device(
    query_states,
    key_states,
    value_states,
    base_patch,
    head_proj,
    latent_std,
    latent_mean,
    w_in,
    b_in,
    gain_mid,
    w_up,
    b_up,
):
    here = pl.BlockSpec(memory_space=pltpu.VMEM)
    far = pl.BlockSpec(memory_space=pltpu.HBM)
    DMA = pltpu.SemaphoreType.DMA
    planes = pl.pallas_call(
        kernel,
        out_shape=pltpu.VMEM((256, OUTCH), BF16),
        in_specs=[far] * 12,
        out_specs=here,
        scratch_shapes=[
            pltpu.VMEM((16, ROW, WIDE), BF16),
            pltpu.VMEM((16, NUM, ROW), BF16),
            pltpu.VMEM((ROW, WIDE), BF16),
            pltpu.VMEM((PLANE, WIDE), BF16),
            pltpu.VMEM((WIDE, PLANE), BF16),
            pltpu.VMEM((8, PLANE), F32),
            pltpu.VMEM((8, PLANE), F32),
            pltpu.VMEM((LOCAL, 2 * ROW, PLANE), BF16),
            pltpu.VMEM((LOCAL * TALL, PLANE), F32),
            pltpu.VMEM((MSG, PLANE), F32),
            pltpu.VMEM((PLANE, MSG), BF16),
            pltpu.VMEM((PLANE, MSG), BF16),
            pltpu.VMEM((OWN, 128), BF16),
            pltpu.VMEM((5, OWN, 128), BF16),
            pltpu.VMEM((OWN, PATCH), BF16),
            pltpu.VMEM((PATCH, WIDE), BF16),
            pltpu.VMEM((1, 16), F32),
            pltpu.VMEM((1, 16), F32),
            pltpu.VMEM((27 * 16, CH), BF16),
            pltpu.VMEM((CH,), F32),
            pltpu.VMEM((CH,), F32),
            pltpu.VMEM((9 * OUTCH, CH), BF16),
            pltpu.VMEM((1, OUTCH), F32),
            pltpu.VMEM((768, 2 * CH), BF16),
            pltpu.VMEM((3, 8, LINE, 128), F32),
            pltpu.VMEM((3, 8, 32, CH), BF16),
            pltpu.VMEM((MSG, NUM), BF16),
            pltpu.VMEM((2, 128, 128), BF16),
            pltpu.VMEM((8, 128), F32),
            DMA((4,)),
            DMA((4,)),
            DMA((2, 2)),
            DMA((2, 16, 2)),
            DMA,
            DMA,
            DMA,
            DMA,
            DMA((9,)),
        ],
        compiler_params=pltpu.CompilerParams(
            collective_id=0, has_side_effects=True, vmem_limit_bytes=60 * 1024 * 1024
        ),
        name="attend_and_decode",
    )(
        query_states,
        key_states,
        value_states,
        base_patch,
        head_proj.T,
        latent_std.reshape(1, 16),
        latent_mean.reshape(1, 16),
        w_in.reshape(27 * 16, CH),
        b_in,
        gain_mid,
        w_up.transpose(0, 1, 3, 2).reshape(9 * OUTCH, CH),
        b_up.reshape(1, OUTCH),
    )
    return planes.reshape(2, 4, 32, OUTCH)


def solution(mesh):
    in_specs = (
        P(("seq", "head"), None),
        P(("seq", "head"), None),
        P(("seq", "head"), None),
        P(("seq", "head"), None),
        P("head", None),
        P(),
        P(),
        P(),
        P(),
        P(),
        P(),
        P(),
    )
    out_specs = P("head", "seq", None, None)
    return jax.shard_map(
        on_device, mesh=mesh, in_specs=in_specs, out_specs=out_specs, check_vma=False
    )
```
